32 devices in a mesh: ctx: 16 (over z, y, x), fsdp: 2 (over core).
Axes of the slice: x: 2, y: 2, z: 4, core: 2. Of those that a mesh axis runs over, the one named last changes fastest.
Arguments:
- hidden_in: bfloat16 [2, 2048, 2048], P('fsdp', 'ctx'), may hold values from -6 to 6
- teacher: bfloat16 [2, 2048, 2048], P('fsdp', 'ctx'), may hold values from -8 to 8
- doc_starts: int32 [2, 4], P('fsdp'), may hold values from 0 to 2047, as said below
- routes: int32 [2, 2048, 6], P('fsdp', 'ctx'), may hold values from 0 to 15, all different within a row; in each aligned block of 128 rows (0 to 127, 128 to 255, ..., all dimensions but the last counted through in order) at most 72 rows name the same one
- gate_logits: float32 [2, 2048, 6], P('fsdp', 'ctx'), may hold values from -3 to 3
- input_gain: bfloat16 [2048], P(('ctx', 'fsdp')), may hold values from 0.5 to 1.5
- query_weight: bfloat16 [2048, 3072], P(('ctx', 'fsdp')), may hold values from -0.125 to 0.125
- latent_weight: bfloat16 [2048, 576], P(('ctx', 'fsdp')), may hold values from -0.125 to 0.125
- latent_gain: bfloat16 [512], P(('ctx', 'fsdp')), may hold values from 0.5 to 1.5
- expand_weight: bfloat16 [512, 4096], P(('ctx', 'fsdp')), may hold values from -0.25 to 0.25
- output_weight: bfloat16 [2048, 2048], P(('ctx', 'fsdp')), may hold values from -1 to 1
- mixer_gain: bfloat16 [2048], P(('ctx', 'fsdp')), may hold values from 0.5 to 1.5
- shared_gate: bfloat16 [2048, 2816], P(('ctx', 'fsdp')), may hold values from -0.125 to 0.125
- shared_up: bfloat16 [2048, 2816], P(('ctx', 'fsdp')), may hold values from -0.125 to 0.125
- shared_down: bfloat16 [2816, 2048], P(('ctx', 'fsdp')), may hold values from -0.15625 to 0.15625
- expert_gate: bfloat16 [16, 2048, 1408], P('ctx', None, 'fsdp'), may hold values from -0.25 to 0.25
- expert_up: bfloat16 [16, 2048, 1408], P('ctx', None, 'fsdp'), may hold values from -0.25 to 0.25
- expert_down: bfloat16 [16, 1408, 2048], P('ctx', 'fsdp'), may hold values from -0.21875 to 0.21875
Outputs:
- layer_out: bfloat16 [2, 2048, 2048], P('fsdp', 'ctx')
- loss_value: float32 [], replicated
- grad_input: float32 [2, 2048, 2048], P('fsdp', 'ctx')
- grad_input_gain: float32 [2048], P(('ctx', 'fsdp'))
- grad_query_weight: float32 [2048, 3072], P(('ctx', 'fsdp'))
- grad_latent_weight: float32 [2048, 576], P(('ctx', 'fsdp'))
- grad_latent_gain: float32 [512], P(('ctx', 'fsdp'))
- grad_expand_weight: float32 [512, 4096], P(('ctx', 'fsdp'))
- grad_output_weight: float32 [2048, 2048], P(('ctx', 'fsdp'))
- grad_mixer_gain: float32 [2048], P(('ctx', 'fsdp'))
- grad_shared_gate: float32 [2048, 2816], P(('ctx', 'fsdp'))
- grad_shared_up: float32 [2048, 2816], P(('ctx', 'fsdp'))
- grad_shared_down: float32 [2816, 2048], P(('ctx', 'fsdp'))
- grad_expert_gate: float32 [16, 2048, 1408], P('ctx', None, 'fsdp')
- grad_expert_up: float32 [16, 2048, 1408], P('ctx', None, 'fsdp')
- grad_expert_down: float32 [16, 1408, 2048], P('ctx', 'fsdp')
The draws below stay inside these ranges and needn't reach their ends.
Inputs may be any that keep to these rules, and one draw needn't show every extreme that they name: `doc_starts`: in each stream the 4 starts rise strictly and the first is 0; one document begins within the first 128 positions and ends within the last 128. `routes`: each row names 6 different experts; within the rows of one device no expert is named more than 72 times.
All inputs are finite; a program needn't handle non-finite values.
Results may differ from the reference program's by a relative error of at most 0.019.
Values may be sent and summed in bfloat16 or wider, within the bound.
A program may use at most 384 MiB of HBM per device.

```python
import math
import jax
import jax.numpy as jnp
import numpy as np
from jax import lax

D = 2048
H = 16
DN = 128
DR = 64
DV = 128
KVR = 512
FF = 1408
TOPK = 6
TOK_DEV = 128
SFF = 2816
EXPERTS = 16
SEQS = 2
LEN = 2048
CAP = 72


def draw_teacher(key, part):
    key = jax.random.fold_in(key, 11)
    shape = (SEQS, LEN, D)
    where = jnp.arange(LEN, dtype=jnp.float32)[None, :, None] / LEN
    noise = jnp.clip(jax.random.normal(key, shape, jnp.float32), -4.0, 4.0)
    scale = 0.5 * jnp.exp(where * 1.386)
    return (noise * scale).astype(jnp.bfloat16)


def draw_doc_starts(key, part):
    key = jax.random.fold_in(key, 7)
    keys = jax.random.split(key, 3)
    half = TOK_DEV // 2
    first = jax.random.randint(keys[0], (SEQS, 1), 1, half + 1)
    last = LEN - jax.random.randint(keys[1], (SEQS, 1), 1, half + 1)
    middle = jax.random.randint(keys[2], (SEQS, 1), LEN - TOK_DEV + 1, last)
    zeros = jnp.zeros((SEQS, 1), jnp.int32)
    return jnp.concatenate([zeros, first, middle, last], axis=1).astype(jnp.int32)


def block_levels(rng, shape, shards, low, largest):
    factor_of = 1.0
    for dim, shards_of in shards:
        draws = jax.random.uniform(jax.random.fold_in(jax.random.fold_in(rng, 6), dim), (shards_of,), jnp.float32, low / len(shards), largest / len(shards))
        factor_of = factor_of * jnp.repeat(jnp.exp(draws), shape[dim] // shards_of).reshape((-1,) + (1,) * (len(shape) - 1 - dim))
    return factor_of


def shared_out(own_key, own, number, rows, number_of, top, most, skew):
    sequence = jax.random.permutation(own_key, number_of)
    crowded, common = shares(number_of, rows * top, most, skew, True), shares(number_of, rows * top, most, skew, False)
    places = jnp.arange(number_of)

    def named(lengths, turn):
        used = int((lengths > 0).sum())
        fixed = max(1, used // 4)
        moved = fixed + (places - fixed + turn * (used - fixed)) % max(1, number_of - fixed)
        return jnp.zeros((number_of,), jnp.int32).at[sequence[jnp.where(places < fixed, places, moved)]].set(jnp.asarray(lengths, jnp.int32))

    lengths = jnp.where(number % 4 == 0, named(crowded, number // 4), named(common, number - number // 4 - 1))
    mixed = jax.random.permutation(jax.random.fold_in(own, 3), number_of)
    donor, taker = mixed[0:number_of // 2 * 2:2], mixed[1:number_of // 2 * 2:2]
    room = jnp.minimum(lengths[donor] - 1, most - lengths[taker]) // 2
    room = jnp.where((donor == sequence[0]) | (taker == sequence[0]) | (lengths[taker] == 0), 0, jnp.maximum(room, 0))
    moved = jax.random.randint(jax.random.fold_in(own, 4), (number_of // 2,), 0, 1 << 20) % (room + 1)
    lengths = lengths.at[donor].add(-moved).at[taker].add(moved)
    labels = jnp.searchsorted(jnp.cumsum(lengths), jnp.arange(rows * top), side="right").astype(jnp.int32)
    table = labels.reshape(top, rows).T
    table = table[jax.random.permutation(jax.random.fold_in(own, 1), rows)]
    turn = jax.random.randint(jax.random.fold_in(own, 2), (rows, 1), 0, top)
    return jnp.take_along_axis(table, (jnp.arange(top)[None, :] + turn) % top, axis=1)


def shares(count, total, limit, skew, full):
    portions = [(1 << 20) // math.isqrt(rank ** skew) + 1 for rank in range(1, count + 1)]
    largest = limit if full else min(limit, max(-(-total // count), total * portions[0] // sum(portions)))
    least = 1 if total - largest >= count - 1 else 0
    holding, surplus = [largest] + [least] * (count - 1), total - largest - least * (count - 1)
    while surplus > 0:
        free = [i for i in range(1, count) if holding[i] < largest] or [i for i in range(1, count) if holding[i] < limit]
        pool, remaining = sum([portions[i] for i in free]), surplus
        for i in free:
            extra = min(limit - holding[i], max(1, remaining * portions[i] // pool), surplus)
            holding[i] = holding[i] + extra
            surplus = surplus - extra
    return np.array(holding)


def gaussian(own_key, shape, deviation, bound, shards=(), held_as=jnp.bfloat16):
    entries = deviation * jax.random.normal(own_key, shape, jnp.float32)
    if shards:
        entries = entries * block_levels(own_key, shape, shards, -0.22, 0.18)
    return jnp.clip(entries, -bound, bound).astype(held_as)


def setup_inputs(seed: int = 0) -> dict:
    splits = jax.random.split(jax.random.key(seed), 19)
    hidden_in = gaussian(splits[0], (SEQS, LEN, D), 1.0, 6.0, ((0, 2), (1, 16)))
    teacher = draw_teacher(jax.random.fold_in(splits[18], 71), 0)
    doc_starts = draw_doc_starts(jax.random.fold_in(splits[18], 71), 0)
    routes_keys = jax.random.split(jax.random.fold_in(splits[3], 1), SEQS * LEN // TOK_DEV)
    routes_turns = jax.random.permutation(jax.random.fold_in(splits[3], 3), SEQS * LEN // TOK_DEV)
    routes = jax.vmap(lambda own, number: shared_out(jax.random.fold_in(splits[3], 2), own, number, TOK_DEV, EXPERTS, TOPK, CAP, 1))(routes_keys, routes_turns).reshape((SEQS, LEN, TOPK))
    gate_logits = gaussian(splits[4], (SEQS, LEN, TOPK), 0.5, 3.0, ((0, 2), (1, 16)), jnp.float32)
    input_gain = jnp.clip(1.0 + 0.1 * jax.random.normal(splits[5], (D,), jnp.float32), 0.5, 1.5).astype(jnp.bfloat16)
    query_weight = gaussian(splits[6], (D, H * (DN + DR)), D ** -0.5, 0.125, ((0, 32),))
    latent_weight = gaussian(splits[7], (D, KVR + DR), D ** -0.5, 0.125, ((0, 32),))
    latent_gain = jnp.clip(1.0 + 0.1 * jax.random.normal(splits[8], (KVR,), jnp.float32), 0.5, 1.5).astype(jnp.bfloat16)
    expand_weight = gaussian(splits[9], (KVR, H * (DN + DV)), KVR ** -0.5, 0.25, ((0, 32),))
    output_weight = gaussian(splits[10], (H * DV, D), (H * DV // 64) ** -0.5, 1.0, ((0, 32),))
    mixer_gain = jnp.clip(1.0 + 0.1 * jax.random.normal(splits[11], (D,), jnp.float32), 0.5, 1.5).astype(jnp.bfloat16)
    shared_gate = gaussian(splits[12], (D, SFF), D ** -0.5, 0.125, ((0, 32),))
    shared_up = gaussian(splits[13], (D, SFF), D ** -0.5, 0.125, ((0, 32),))
    shared_down = gaussian(splits[14], (SFF, D), (SFF // 2) ** -0.5, 0.15625, ((0, 32),))
    expert_gate = gaussian(splits[15], (EXPERTS, D, FF), (D // 4) ** -0.5, 0.25, ((0, 16), (2, 2)))
    expert_up = gaussian(splits[16], (EXPERTS, D, FF), (D // 4) ** -0.5, 0.25, ((0, 16), (2, 2)))
    expert_down = gaussian(splits[17], (EXPERTS, FF, D), (FF // 2) ** -0.5, 0.21875, ((0, 16), (1, 2)))
    return dict(hidden_in=hidden_in, teacher=teacher, doc_starts=doc_starts, routes=routes, gate_logits=gate_logits, input_gain=input_gain, query_weight=query_weight, latent_weight=latent_weight, latent_gain=latent_gain, expand_weight=expand_weight, output_weight=output_weight, mixer_gain=mixer_gain, shared_gate=shared_gate, shared_up=shared_up, shared_down=shared_down, expert_gate=expert_gate, expert_up=expert_up, expert_down=expert_down)


@jax.custom_vjp
def low(v):
    return lax.optimization_barrier(v.astype(jnp.bfloat16)).astype(jnp.float32)

@jax.custom_vjp
def low_back(v):
    return v

def low_keep(v):
    return (low(v), None)

def low_pass(kept, grad):
    return (grad,)

def back_keep(v):
    return (v, None)

def back_low(kept, grad):
    return (low(grad),)
low.defvjp(low_keep, low_pass)
low_back.defvjp(back_keep, back_low)
EPS = 1e-06
NEG = -1e+30
HIGH = lax.Precision.HIGHEST

def rms_norm(rows, gain):
    factor = lax.rsqrt(lax.optimization_barrier(jnp.mean(rows * rows, axis=-1, keepdims=True)) + EPS)
    return rows * factor * gain

def rotate(values, cosine, sine):
    half = values.shape[-1] // 2
    first = values[..., :half]
    second = values[..., half:]
    return jnp.concatenate([first * cosine - second * sine, second * cosine + first * sine], axis=-1)

def doc_tables(starts, positions):
    inside = starts[None, :] <= positions[:, None]
    doc_ids = lax.optimization_barrier(jnp.sum(inside.astype(jnp.int32), axis=1))
    first = lax.optimization_barrier(jnp.max(jnp.where(inside, starts[None, :], 0), axis=1))
    return (doc_ids, positions - first)

def rope_tables(offsets):
    freqs = 10000.0 ** (-(jnp.arange(DR // 2, dtype=jnp.float32) * 2.0) / DR)
    angle = offsets.astype(jnp.float32)[:, None] * freqs[None, :]
    return (jnp.cos(angle), jnp.sin(angle))

def attend_block(queries, query_doc, query_pos, keys, values, key_doc, key_pos):
    scores = low_back(jnp.einsum('qhd,khd->hqk', queries, keys, precision=HIGH))
    allowed = (key_doc[None, :] == query_doc[:, None]) & (key_pos[None, :] <= query_pos[:, None])
    scores = jnp.where(allowed[None], scores, NEG)
    top = lax.optimization_barrier(jnp.max(scores, axis=-1, keepdims=True))
    weights = jnp.exp(scores - top)
    probs = low(weights / lax.optimization_barrier(jnp.sum(weights, axis=-1, keepdims=True)))
    return jnp.einsum('hqk,khv->qhv', probs, values, precision=HIGH)

def stream_attention(residual_stream, starts, first_norm_scale, query_project_weight, latent_project_weight, latent_norm_scale, latent_expand_weight, output_project_weight):
    positions = jnp.arange(LEN, dtype=jnp.int32)
    doc_ids, offsets = doc_tables(starts, positions)
    cosine, sine = rope_tables(offsets)
    scale = (DN + DR) ** (-0.5)
    act_one = low(rms_norm(residual_stream, first_norm_scale))
    query_raw = low_back(jnp.dot(act_one, query_project_weight, precision=HIGH)).reshape(LEN, H, DN + DR)
    query_rope = rotate(query_raw[..., DN:], cosine[:, None, :], sine[:, None, :])
    queries = low(jnp.concatenate([query_raw[..., :DN], query_rope], axis=-1) * scale)
    latent_raw = low_back(jnp.dot(act_one, latent_project_weight, precision=HIGH))
    latent = low(rms_norm(latent_raw[:, :KVR], latent_norm_scale))
    key_rope = low(rotate(latent_raw[:, KVR:], cosine, sine))
    expanded = low(jnp.dot(latent, latent_expand_weight, precision=HIGH)).reshape(LEN, H, DN + DV)
    keys = jnp.concatenate([expanded[..., :DN], jnp.broadcast_to(key_rope[:, None, :], (LEN, H, DR))], axis=-1)
    values = expanded[..., DN:]
    block = math.gcd(LEN, 512)

    def one_block(pieces):
        block_queries, block_doc, block_pos = pieces
        return attend_block(block_queries, block_doc, block_pos, keys, values, doc_ids, positions)
    attended = lax.map(jax.checkpoint(one_block), (queries.reshape(LEN // block, block, H, DN + DR), doc_ids.reshape(LEN // block, block), positions.reshape(LEN // block, block)))
    attended = low_back(low(attended.reshape(LEN, H * DV)))
    return residual_stream + low_back(jnp.dot(attended, output_project_weight, precision=HIGH))

def slot_tables(routes, probs):
    per_block = TOK_DEV * TOPK
    chosen = routes.reshape(-1, per_block)
    weight_flat = probs.reshape(-1, per_block)
    blocks = chosen.shape[0]
    onehot = (chosen[:, :, None] == jnp.arange(EXPERTS, dtype=jnp.int32)[None, None, :]).astype(jnp.int32)
    order = lax.optimization_barrier(jnp.sum(jnp.cumsum(onehot, axis=1) * onehot, axis=2)) - 1
    slot = chosen * CAP + order
    marks = jnp.broadcast_to(jnp.arange(per_block, dtype=jnp.int32) + 1, slot.shape)
    table = jax.vmap(lambda where, what: jnp.zeros((EXPERTS * CAP,), jnp.int32).at[where].set(what))(slot, marks)
    live = table > 0
    entry = jnp.maximum(table - 1, 0)
    rows = jnp.arange(blocks, dtype=jnp.int32)[:, None] * TOK_DEV + entry // TOPK
    weight = jnp.take_along_axis(weight_flat, entry, axis=1)

    def by_expert(values):
        return jnp.transpose(values.reshape(blocks, EXPERTS, CAP), (1, 0, 2)).reshape(EXPERTS, blocks * CAP)
    return (by_expert(rows), by_expert(jnp.where(live, 1.0, 0.0)), by_expert(weight))

def attention_mixer(flattened_rows, second_norm_scale, shared_gate_weight, shared_up_weight, shared_down_weight, expert_gate_weight, expert_up_weight, expert_down_weight, slot_token_rows, slot_valid_mask, slot_gate_weight):
    act_two = low(rms_norm(flattened_rows, second_norm_scale))
    gate_val = low_back(jnp.dot(act_two, shared_gate_weight, precision=HIGH))
    up_val = low_back(jnp.dot(act_two, shared_up_weight, precision=HIGH))
    hidden_val = low(jax.nn.silu(gate_val) * up_val)
    grand_total = flattened_rows + low_back(jnp.dot(hidden_val, shared_down_weight, precision=HIGH))

    def single_expert(carry, pieces):
        w_gate, w_up, w_down, rows, live, weight = pieces
        chosen = act_two[rows] * live[:, None]
        gate_e = low_back(jnp.dot(chosen, w_gate, precision=HIGH))
        up_e = low_back(jnp.dot(chosen, w_up, precision=HIGH))
        hidden_e = low(jax.nn.silu(gate_e) * up_e)
        outcome = low(low_back(jnp.dot(hidden_e, w_down, precision=HIGH)))
        return (carry.at[rows].add(outcome * (weight * live)[:, None]), None)
    grand_total, ignored_value = lax.scan(jax.checkpoint(single_expert), grand_total, (expert_gate_weight, expert_up_weight, expert_down_weight, slot_token_rows, slot_valid_mask, slot_gate_weight))
    return grand_total

def reference(hidden_in, teacher, doc_starts, routes, gate_logits, input_gain, query_weight, latent_weight, latent_gain, expand_weight, output_weight, mixer_gain, shared_gate, shared_up, shared_down, expert_gate, expert_up, expert_down):
    probs = jax.nn.softmax(gate_logits.astype(jnp.float32), axis=-1)
    slot_token_rows, slot_valid_mask, slot_gate_weight = slot_tables(routes, probs)

    def forward_pass(residual_stream, first_norm_scale, query_project_weight, latent_project_weight, latent_norm_scale, latent_expand_weight, output_project_weight, second_norm_scale, shared_gate_weight, shared_up_weight, shared_down_weight, expert_gate_weight, expert_up_weight, expert_down_weight):

        def one_stream(pieces):
            return stream_attention(pieces[0], pieces[1], first_norm_scale, query_project_weight, latent_project_weight, latent_norm_scale, latent_expand_weight, output_project_weight)
        mixed = lax.map(one_stream, (residual_stream, doc_starts))
        flattened_rows = mixed.reshape(SEQS * LEN, D)
        grand_total = attention_mixer(flattened_rows, second_norm_scale, shared_gate_weight, shared_up_weight, shared_down_weight, expert_gate_weight, expert_up_weight, expert_down_weight, slot_token_rows, slot_valid_mask, slot_gate_weight)
        return grand_total.reshape(SEQS, LEN, D)
    inputs = tuple((item.astype(jnp.float32) for item in (hidden_in, input_gain, query_weight, latent_weight, latent_gain, expand_weight, output_weight, mixer_gain, shared_gate, shared_up, shared_down, expert_gate, expert_up, expert_down)))
    result, pull = jax.vjp(forward_pass, *inputs)
    diff = result - teacher.astype(jnp.float32)
    loss_value = 0.5 * jnp.mean(diff * diff)
    grads = pull(diff)
    return (result.astype(jnp.bfloat16), loss_value, grads[0], grads[1], grads[2], grads[3], grads[4], grads[5], grads[6], grads[7], grads[8], grads[9], grads[10], grads[11], grads[12], grads[13])
```

```python
import functools
import math

import jax
import jax.numpy as jnp
from jax import lax
from jax.experimental import pallas as pl
from jax.experimental.pallas import tpu as pltpu
from jax.sharding import PartitionSpec as P

D = 2048
H = 16
DN = 128
DR = 64
DV = 128
KVR = 512
TOPK = 6

EPS = 1e-06
NEG = -1e30
MESH = pl.DeviceIdType.MESH
f32 = jnp.float32
bf16 = jnp.bfloat16


def norm_forward(rows, gain):
    factor = lax.rsqrt(jnp.mean(rows * rows, axis=-1, keepdims=True) + EPS)
    return (rows * factor * gain, factor)


def norm_back_rows(rows, factor, gain, grad_out):
    scaled = grad_out * gain
    normed = rows * factor
    return factor * (scaled - normed * jnp.mean(scaled * normed, axis=-1, keepdims=True))


def rotate(values, cosine, sine):
    half = values.shape[-1] // 2
    first = values[..., :half]
    second = values[..., half:]
    return jnp.concatenate(
        [first * cosine - second * sine, second * cosine + first * sine], axis=-1
    )


def rope_tables(offsets):
    freqs = 10000.0 ** (-(jnp.arange(DR // 2, dtype=f32) * 2.0) / DR)
    angle = offsets.astype(f32)[:, None] * freqs[None, :]
    return (jnp.cos(angle), jnp.sin(angle))


def silu_grads(gate_val, up_val, grad_hidden):
    sigma = jax.nn.sigmoid(gate_val)
    grad_gate = grad_hidden * up_val * sigma * (1.0 + gate_val * (1.0 - sigma))
    grad_up = grad_hidden * gate_val * sigma
    return (grad_gate.astype(bf16), grad_up.astype(bf16))


def dot(left, right):
    return jnp.dot(left, right, preferred_element_type=f32)


def dot_first(left, right):
    return lax.dot_general(left, right, (((0,), (0,)), ((), ())), preferred_element_type=f32)


def dot_last(left, right):
    return lax.dot_general(left, right, (((1,), (1,)), ((), ())), preferred_element_type=f32)


def flip(me, mask):
    out = me
    bit = 1
    while bit <= mask:
        if mask & bit:
            out = out + bit * (1 - 2 * ((me // bit) % 2))
        bit *= 2
    return out


def row_parts(rows, bits):
    low, high = [1, 2], [1 << k for k in range(bits - 1, 1, -1)]
    orders = (high + low, high + low[::-1], low + high)
    unit = rows // 8
    if unit % 16 and rows % 16 == 0:
        units = rows // 16
        first = -(-3 * units // 8)
        counts = [first * 16, min(first, units - first) * 16]
        counts.append(rows - sum(counts))
    else:
        counts = [3 * unit, 3 * unit, 2 * unit]
    parts, start = [], 0
    for count, order in zip(counts, orders):
        if count:
            parts.append((start, count, tuple(order)))
            start += count
    return tuple(parts)


def greet(bits):
    me = lax.axis_index("ctx")
    barrier = pltpu.get_barrier_semaphore()
    for k in range(bits):
        pl.semaphore_signal(
            barrier, inc=1, device_id={"ctx": flip(me, 1 << k)}, device_id_type=MESH
        )
    pl.semaphore_wait(barrier, bits)


def gather_events(parts, bits):
    events = []
    for p, (_, _, order) in enumerate(parts):
        for slot in range(1 << bits):
            hops = [k for k, b in enumerate(order) if slot & b]
            for k in range(hops[-1] + 1 if hops else 0, bits):
                events.append((len(hops), k, p, slot, order[k]))
    return tuple(sorted(events))


def gather_kernel(parts, bits, events, x_ref, o_ref, send_sem, recv_sem, own_sem):
    me = lax.axis_index("ctx")
    own = pltpu.make_async_copy(x_ref, o_ref.at[me], own_sem)
    own.start()
    greet(bits)

    def copy(p, slot, bit, index):
        start, count, _ = parts[p]
        rows = pl.ds(start, count)
        block = flip(me, slot)
        return pltpu.make_async_remote_copy(
            src_ref=x_ref.at[rows] if slot == 0 else o_ref.at[block, rows],
            dst_ref=o_ref.at[block, rows],
            send_sem=send_sem.at[index],
            recv_sem=recv_sem.at[p, slot ^ bit],
            device_id={"ctx": flip(me, bit)},
            device_id_type=MESH,
        )

    def arrived(p, slot):
        start, count, order = parts[p]
        rows = pl.ds(start, count)
        bit = [b for b in order if slot & b][-1]
        pltpu.make_async_remote_copy(
            src_ref=x_ref.at[rows],
            dst_ref=o_ref.at[flip(me, slot), rows],
            send_sem=send_sem.at[0],
            recv_sem=recv_sem.at[p, slot],
            device_id={"ctx": flip(me, bit)},
            device_id_type=MESH,
        ).wait_recv()

    seen = set()
    started = []
    for index, (_, _, p, slot, bit) in enumerate(events):
        if slot and (p, slot) not in seen:
            arrived(p, slot)
            seen.add((p, slot))
        sent = copy(p, slot, bit, index)
        sent.start()
        started.append(sent)
    for p in range(len(parts)):
        for slot in range(1, 1 << bits):
            if (p, slot) not in seen:
                arrived(p, slot)
    for sent in started:
        sent.wait_send()
    own.wait()


def gather_ctx(x, bits):
    rows, cols = x.shape
    parts = row_parts(rows, bits)
    events = gather_events(parts, bits)
    return pl.pallas_call(
        functools.partial(gather_kernel, parts, bits, events),
        name="gather_ctx",
        out_shape=jax.ShapeDtypeStruct((1 << bits, rows, cols), x.dtype),
        in_specs=[pl.BlockSpec(memory_space=pl.ANY)],
        out_specs=pl.BlockSpec(memory_space=pl.ANY),
        scratch_shapes=[
            pltpu.SemaphoreType.DMA((len(events),)),
            pltpu.SemaphoreType.DMA((len(parts), 1 << bits)),
            pltpu.SemaphoreType.DMA,
        ],
        compiler_params=pltpu.CompilerParams(collective_id=1, has_side_effects=True),
    )(x)


def scatter_kernel(parts, bits, x_ref, o_ref, recv, send, send_sem, recv_sem):
    me = lax.axis_index("ctx")
    greet(bits)

    def copy(p, slot, k, src):
        start, count, order = parts[p]
        return pltpu.make_async_remote_copy(
            src_ref=src,
            dst_ref=recv.at[slot - 1, pl.ds(start, count)],
            send_sem=send_sem.at[p, slot - 1],
            recv_sem=recv_sem.at[p, slot - 1],
            device_id={"ctx": flip(me, order[k])},
            device_id_type=MESH,
        )

    started = []
    for k in range(bits + 1):
        for j in range(1 << max(bits - 1 - k, 0)):
            for p, (start, count, order) in enumerate(parts):
                rows = pl.ds(start, count)
                slot = order[k] if k < bits else 0
                for q, b in enumerate(order[k + 1 :]):
                    if (j >> q) & 1:
                        slot |= b
                block = flip(me, slot)
                if k == 0:
                    sent = copy(p, slot, 0, x_ref.at[block, rows])
                    sent.start()
                    started.append(sent)
                    continue
                for e in range(k):
                    other = slot | order[e]
                    copy(p, other, e, recv.at[other - 1, rows]).wait_recv()
                target = send.at[slot - 1] if k < bits else o_ref

                @pl.loop(0, count // 16)
                def _(t, k=k, slot=slot, block=block, start=start, order=order, target=target):
                    part = pl.ds(pl.multiple_of(start + t * 16, 16), 16)
                    total = x_ref[block, part].astype(f32)
                    for e in range(k):
                        total = total + recv[(slot | order[e]) - 1, part].astype(f32)
                    target[part] = total.astype(target.dtype)

                if k < bits:
                    sent = copy(p, slot, k, send.at[slot - 1, rows])
                    sent.start()
                    started.append(sent)
    for sent in started:
        sent.wait_send()


def scatter_ctx(x, bits):
    _, rows, cols = x.shape
    parts = tuple((start, count, order[::-1]) for start, count, order in row_parts(rows, bits))
    others = (1 << bits) - 1
    return pl.pallas_call(
        functools.partial(scatter_kernel, parts, bits),
        name="scatter_ctx",
        out_shape=jax.ShapeDtypeStruct((rows, cols), f32),
        in_specs=[pl.BlockSpec(memory_space=pltpu.VMEM)],
        out_specs=pl.BlockSpec(memory_space=pltpu.VMEM),
        scratch_shapes=[
            pltpu.VMEM((others, rows, cols), bf16),
            pltpu.VMEM((others, rows, cols), bf16),
            pltpu.SemaphoreType.DMA((len(parts), others)),
            pltpu.SemaphoreType.DMA((len(parts), others)),
        ],
        compiler_params=pltpu.CompilerParams(
            collective_id=2, has_side_effects=True, vmem_limit_bytes=56 << 20
        ),
    )(x)


def attend_kernel(block, count, q_ref, k_ref, v_ref, first_ref, o_ref, log_ref):
    step = pl.program_id(0)
    for i in range(count):

        @pl.when(step == i)
        def _(i=i):
            extent = (i + 1) * block
            scores = dot_last(q_ref[...], k_ref[:extent, :])
            key_pos = lax.broadcasted_iota(jnp.int32, (block, extent), 1)
            query_pos = i * block + lax.broadcasted_iota(jnp.int32, (block, extent), 0)
            allowed = (key_pos >= first_ref[...]) & (key_pos <= query_pos)
            scores = jnp.where(allowed, scores, NEG)
            top = jnp.max(scores, axis=-1, keepdims=True)
            weights = jnp.exp(scores - top)
            total = jnp.sum(weights, axis=-1, keepdims=True)
            summed = dot(weights.astype(bf16), v_ref[:extent, :])
            o_ref[...] = summed / total
            log_ref[...] = top + jnp.log(total)


def attend(queries, keys, values, first):
    length = queries.shape[0]
    block = min(256, length)
    count = length // block
    return pl.pallas_call(
        functools.partial(attend_kernel, block, count),
        name="attend",
        grid=(count,),
        out_shape=(
            jax.ShapeDtypeStruct((length, DV), f32),
            jax.ShapeDtypeStruct((length, 1), f32),
        ),
        in_specs=[
            pl.BlockSpec((block, DN + DR), lambda i: (i, 0)),
            pl.BlockSpec((length, DN + DR), lambda i: (0, 0)),
            pl.BlockSpec((length, DV), lambda i: (0, 0)),
            pl.BlockSpec((block, 1), lambda i: (i, 0)),
        ],
        out_specs=(
            pl.BlockSpec((block, DV), lambda i: (i, 0)),
            pl.BlockSpec((block, 1), lambda i: (i, 0)),
        ),
        compiler_params=pltpu.CompilerParams(vmem_limit_bytes=56 << 20),
        cost_estimate=pl.CostEstimate(
            flops=length * length * (DN + DR + DV),
            bytes_accessed=length * 2000,
            transcendentals=length * length // 2,
        ),
    )(queries, keys, values, first)


def attend_back_kernel(
    block, count, q_ref, k_ref, v_ref, g_ref, first_ref, log_ref, delta_ref, dq_ref, dk_ref, dv_ref
):
    step = pl.program_id(0)

    @pl.when(step == 0)
    def _():
        dk_ref[...] = jnp.zeros_like(dk_ref)
        dv_ref[...] = jnp.zeros_like(dv_ref)

    for i in range(count):

        @pl.when(step == i)
        def _(i=i):
            extent = (i + 1) * block
            keys = k_ref[:extent, :]
            scores = dot_last(keys, q_ref[...])
            key_pos = lax.broadcasted_iota(jnp.int32, (extent, block), 0)
            query_pos = i * block + lax.broadcasted_iota(jnp.int32, (extent, block), 1)
            allowed = (key_pos >= first_ref[...]) & (key_pos <= query_pos)
            weights = jnp.where(allowed, jnp.exp(scores - log_ref[...]), 0.0)
            grad_weights = dot_last(v_ref[:extent, :], g_ref[...])
            grad_scores = (weights * (grad_weights - delta_ref[...])).astype(bf16)
            dv_ref[:extent, :] += dot(weights.astype(bf16), g_ref[...])
            dk_ref[:extent, :] += dot(grad_scores, q_ref[...])
            dq_ref[...] = dot_first(grad_scores, keys)


def attend_back(queries, keys, values, grad, first, log_total, delta):
    length = queries.shape[0]
    block = min(256, length)
    count = length // block
    row = lambda: pl.BlockSpec((1, block), lambda i: (0, i))
    whole = lambda width: pl.BlockSpec((length, width), lambda i: (0, 0))
    part = lambda width: pl.BlockSpec((block, width), lambda i: (i, 0))
    return pl.pallas_call(
        functools.partial(attend_back_kernel, block, count),
        name="attend_back",
        grid=(count,),
        out_shape=(
            jax.ShapeDtypeStruct((length, DN + DR), f32),
            jax.ShapeDtypeStruct((length, DN + DR), f32),
            jax.ShapeDtypeStruct((length, DV), f32),
        ),
        in_specs=[
            part(DN + DR),
            whole(DN + DR),
            whole(DV),
            part(DV),
            row(),
            row(),
            row(),
        ],
        out_specs=(part(DN + DR), whole(DN + DR), whole(DV)),
        compiler_params=pltpu.CompilerParams(vmem_limit_bytes=56 << 20),
        cost_estimate=pl.CostEstimate(
            flops=length * length * (3 * (DN + DR) + 2 * DV),
            bytes_accessed=length * 4000,
            transcendentals=length * length // 2,
        ),
    )(queries, keys, values, grad, first, log_total, delta)


def shift_fsdp(x, groups, by):
    return lax.ppermute(x, "fsdp", [(i, (i + by) % groups) for i in range(groups)])


def gather_fsdp(x, groups):
    if groups != 2:
        return lax.all_gather(x, "fsdp", axis=0)
    other = shift_fsdp(x, groups, 1)
    mine_first = lax.axis_index("fsdp") == 0
    return jnp.stack([jnp.where(mine_first, x, other), jnp.where(mine_first, other, x)])


def scatter_fsdp(x, groups):
    if groups != 2:
        return lax.psum_scatter(x.astype(bf16), "fsdp", scatter_dimension=0).astype(f32)
    me = lax.axis_index("fsdp")
    away = lax.dynamic_index_in_dim(x, 1 - me, 0, keepdims=False).astype(bf16)
    mine = lax.dynamic_index_in_dim(x, me, 0, keepdims=False).astype(f32)
    return mine + shift_fsdp(away, groups, 1).astype(f32)


def shards(
    hidden_in,
    teacher,
    doc_starts,
    routes,
    gate_logits,
    input_gain,
    query_weight,
    latent_weight,
    latent_gain,
    expand_weight,
    output_weight,
    mixer_gain,
    shared_gate,
    shared_up,
    shared_down,
    expert_gate,
    expert_up,
    expert_down,
):
    cycle = lax.axis_size("ctx")
    groups = lax.axis_size("fsdp")
    bits = cycle.bit_length() - 1
    tokens = hidden_in.shape[1]
    length = tokens * cycle
    everyone = ("ctx", "fsdp")
    capacity = min(tokens, 3 * tokens * TOPK // (2 * cycle))
    scale = (DN + DR) ** (-0.5)
    copies = max(1, cycle // H)
    ctx_index = lax.axis_index("ctx")
    copy_index = ctx_index % copies
    slab = query_weight.shape[0]
    slab_latent = expand_weight.shape[0]

    def columns(weight):
        rows, width = weight.shape
        pieces = jnp.transpose(weight.reshape(rows, cycle, width // cycle), (1, 0, 2))
        pieces = lax.all_to_all(pieces, "ctx", split_axis=0, concat_axis=0, tiled=True)
        pieces = jnp.transpose(gather_fsdp(pieces, groups), (1, 0, 2, 3))
        return pieces.reshape(cycle * groups * rows, width // cycle)

    def rows_back(grads):
        rows, width = grads.shape
        slab_rows = rows // (cycle * groups)
        pieces = jnp.transpose(grads.reshape(cycle, groups, slab_rows, width), (1, 0, 2, 3))
        pieces = scatter_fsdp(pieces, groups).astype(bf16)
        pieces = lax.all_to_all(pieces, "ctx", split_axis=0, concat_axis=0, tiled=True)
        return jnp.transpose(pieces, (1, 0, 2)).reshape(slab_rows, cycle * width).astype(f32)

    def same_head(part):
        if copies == 1:
            return part
        teams = [[i * copies + j for j in range(copies)] for i in range(H)]
        return lax.all_gather(part, "ctx", axis=1, tiled=True, axis_index_groups=teams)

    def own_part(full):
        if copies == 1:
            return full
        width = full.shape[1] // copies
        return lax.dynamic_slice_in_dim(full, copy_index * width, width, 1)

    spare = jnp.zeros((slab - slab_latent,), bf16)
    narrow = jnp.concatenate(
        [
            latent_weight,
            input_gain[:, None],
            mixer_gain[:, None],
            jnp.concatenate([latent_gain, spare])[:, None],
        ],
        axis=1,
    )
    narrow = lax.all_gather(narrow, everyone, axis=0, tiled=True)
    w_latent = narrow[:, : KVR + DR]
    gain_one = narrow[:, KVR + DR].astype(f32)
    gain_two = narrow[:, KVR + DR + 1].astype(f32)
    gain_latent = narrow[:, KVR + DR + 2].reshape(-1, slab)[:, :slab_latent].reshape(-1).astype(f32)
    w_query = same_head(columns(query_weight))
    w_expand = same_head(columns(expand_weight))
    probs = jax.nn.softmax(gate_logits[0], axis=-1)
    chosen = routes[0][:, :, None] == jnp.arange(cycle, dtype=jnp.int32)[None, None, :]
    dense_probs = jnp.sum(jnp.where(chosen, probs[:, :, None], 0.0), axis=1)
    all_probs = lax.all_gather(dense_probs, "ctx", axis=0, tiled=True)
    w_output = lax.all_gather(output_weight, everyone, axis=0, tiled=True)

    starts = doc_starts[0]
    positions = jnp.arange(length, dtype=jnp.int32)
    inside = starts[None, :] <= positions[:, None]
    first_pos = jnp.max(jnp.where(inside, starts[None, :], 0), axis=1)
    cosine, sine = rope_tables(positions - first_pos)
    residual = hidden_in[0].astype(f32)
    all_hidden = gather_ctx(hidden_in[0], bits).reshape(length, D).astype(f32)
    act_one, factor_all = norm_forward(all_hidden, gain_one)
    act_one = act_one.astype(bf16)
    query_raw = dot(act_one, w_query)
    queries = jnp.concatenate(
        [query_raw[:, :DN], rotate(query_raw[:, DN:], cosine, sine)], axis=-1
    )
    queries = (queries * scale).astype(bf16)
    latent_raw = dot(act_one, w_latent)
    latent, factor_latent = norm_forward(latent_raw[:, :KVR], gain_latent)
    latent = latent.astype(bf16)
    key_rope = rotate(latent_raw[:, KVR:], cosine, sine).astype(bf16)
    expanded = dot(latent, w_expand).astype(bf16)
    keys = jnp.concatenate([expanded[:, :DN], key_rope], axis=-1)
    values = expanded[:, DN:]
    attended, log_total = attend(queries, keys, values, first_pos[:, None])
    attended_low = attended.astype(bf16)
    attended_mine = lax.all_to_all(
        own_part(attended_low).reshape(cycle, tokens, DV // copies),
        "ctx",
        split_axis=0,
        concat_axis=0,
        tiled=True,
    )
    attended_mine = jnp.transpose(attended_mine, (1, 0, 2)).reshape(tokens, H * DV)
    mixed = residual + dot(attended_mine, w_output)

    normed_two, factor_two = norm_forward(mixed, gain_two)
    act_two = normed_two.astype(bf16)
    all_act = gather_ctx(act_two, bits)
    my_probs = lax.dynamic_index_in_dim(all_probs, ctx_index, 1, keepdims=False)
    my_probs = my_probs.reshape(cycle, tokens)
    used = my_probs > 0.0
    place = jnp.cumsum(used.astype(jnp.int32), axis=1) - 1
    slots = jnp.arange(capacity, dtype=jnp.int32)
    select = (place[:, None, :] == slots[None, :, None]) & used[:, None, :]
    slot_probs = jnp.sum(jnp.where(select, my_probs[:, None, :], 0.0), axis=-1).reshape(-1, 1)
    select = select.astype(bf16)

    def pick(blocks):
        return jnp.einsum("bst,btd->bsd", select, blocks, preferred_element_type=f32).reshape(
            cycle * capacity, D
        )

    def place_back(rows):
        return jnp.einsum(
            "bst,bsd->btd", select, rows.reshape(cycle, capacity, D), preferred_element_type=f32
        )

    w_gate = columns(shared_gate)
    w_up = columns(shared_up)
    w_down = gather_fsdp(shared_down, groups).reshape(-1, D)
    shares = [(expert_gate[0], expert_up[0], expert_down[0])]
    for r in range(1, groups):
        shares.append(tuple(shift_fsdp(item, groups, r) for item in shares[0]))
    flat_act = all_act.reshape(length, D)
    gate_s = dot(flat_act, w_gate)
    up_s = dot(flat_act, w_up)
    hidden_s = (jax.nn.silu(gate_s) * up_s).astype(bf16)
    rows = pick(all_act).astype(bf16)
    kept = []
    total = 0.0
    for part_gate, part_up, part_down in shares:
        gate_e = dot(rows, part_gate)
        up_e = dot(rows, part_up)
        hidden_e = (jax.nn.silu(gate_e) * up_e).astype(bf16)
        kept.append((gate_e, up_e, hidden_e))
        total = total + dot(hidden_e, part_down)
    outputs = (slot_probs * total).astype(bf16)
    partial = place_back(outputs) + dot(hidden_s, w_down).reshape(cycle, tokens, D)
    result = mixed + scatter_ctx(partial.astype(bf16), bits)
    diff = result - teacher[0].astype(f32)
    share = 0.5 * jnp.sum(diff * diff)
    loss_value = jnp.sum(lax.all_gather(share, everyone)) / (length * groups * D)

    all_diff = gather_ctx(diff.astype(bf16), bits)
    flat_diff = all_diff.reshape(length, D)
    grad_w_down = dot_first(hidden_s, flat_diff)
    grad_gate_s, grad_up_s = silu_grads(gate_s, up_s, dot_last(flat_diff, w_down))
    grad_rows = (slot_probs * pick(all_diff)).astype(bf16)
    row_grad = 0.0
    grad_shares = []
    for (part_gate, part_up, part_down), (gate_e, up_e, hidden_e) in zip(shares, kept):
        grad_gate_e, grad_up_e = silu_grads(gate_e, up_e, dot_last(grad_rows, part_down))
        row_grad = row_grad + dot_last(grad_gate_e, part_gate) + dot_last(grad_up_e, part_up)
        grad_shares.append((hidden_e, grad_gate_e, grad_up_e))
    partial = (
        place_back(row_grad.astype(bf16))
        + (dot_last(grad_gate_s, w_gate) + dot_last(grad_up_s, w_up)).reshape(cycle, tokens, D)
    )
    grad_act_two = scatter_ctx(partial.astype(bf16), bits)
    expert_grads = None
    for r, (hidden_e, grad_gate_e, grad_up_e) in enumerate(grad_shares):
        grads = (
            dot_first(rows, grad_gate_e),
            dot_first(rows, grad_up_e),
            dot_first(hidden_e, grad_rows),
        )
        if r:
            grads = tuple(
                total + shift_fsdp(item.astype(bf16), groups, -r).astype(f32)
                for total, item in zip(expert_grads, grads)
            )
        expert_grads = grads
    grad_w_gate = rows_back(dot_first(flat_act, grad_gate_s))
    grad_w_up = rows_back(dot_first(flat_act, grad_up_s))
    grad_w_down = scatter_fsdp(grad_w_down.reshape(groups, -1, D), groups)

    grad_gain_two = jnp.sum(grad_act_two * mixed * factor_two, axis=0)
    grad_mixed = diff + norm_back_rows(mixed, factor_two, gain_two, grad_act_two)
    grad_mixed_low = grad_mixed.astype(bf16)
    grad_w_output = lax.psum_scatter(
        dot_first(attended_mine, grad_mixed_low).astype(bf16),
        everyone,
        scatter_dimension=0,
        tiled=True,
    ).astype(f32)
    grad_attended = dot_last(grad_mixed_low, w_output).astype(bf16)
    grad_attended = lax.all_to_all(
        jnp.transpose(grad_attended.reshape(tokens, cycle, DV // copies), (1, 0, 2)),
        "ctx",
        split_axis=0,
        concat_axis=0,
        tiled=True,
    ).reshape(length, DV // copies)
    grad_attended = same_head(grad_attended)
    delta = jnp.sum(grad_attended.astype(f32) * attended, axis=-1)
    grad_query, grad_keys, grad_values = attend_back(
        queries,
        keys,
        values,
        grad_attended,
        first_pos[None, :],
        log_total.reshape(1, length),
        delta[None, :],
    )
    grad_expanded = jnp.concatenate([grad_keys[:, :DN], grad_values], axis=-1).astype(bf16)
    grad_w_expand = rows_back(own_part(dot_first(latent, grad_expanded)))
    grad_latent = dot_last(own_part(grad_expanded), own_part(w_expand))
    normed_latent = latent_raw[:, :KVR] * factor_latent
    grad_gain_latent = jnp.sum(grad_latent * normed_latent, axis=0)
    grad_latent = norm_back_rows(latent_raw[:, :KVR], factor_latent, gain_latent, grad_latent)
    grad_rope = rotate(grad_keys[:, DN:], cosine, -sine) / copies
    grad_latent_raw = jnp.concatenate([grad_latent, grad_rope], axis=-1).astype(bf16)
    grad_query = grad_query * scale
    grad_query = jnp.concatenate(
        [grad_query[:, :DN], rotate(grad_query[:, DN:], cosine, -sine)], axis=-1
    ).astype(bf16)
    partial = dot_last(own_part(grad_query), own_part(w_query)) + dot_last(
        grad_latent_raw, w_latent
    )
    grad_act_one = scatter_ctx(partial.astype(bf16).reshape(cycle, tokens, D), bits)
    grad_gain_one = jnp.sum(partial * (all_hidden * factor_all), axis=0)
    grad_w_query = rows_back(own_part(dot_first(act_one, grad_query)))
    spare = jnp.zeros((cycle * groups, slab - slab_latent), f32)
    grad_gain_latent = jnp.concatenate(
        [grad_gain_latent.reshape(cycle * groups, slab_latent), spare], axis=1
    ).reshape(-1)
    grad_narrow = jnp.concatenate(
        [
            dot_first(act_one, grad_latent_raw),
            grad_gain_one[:, None],
            grad_gain_two[:, None],
            grad_gain_latent[:, None],
        ],
        axis=1,
    )
    grad_narrow = lax.psum_scatter(
        grad_narrow.astype(bf16), everyone, scatter_dimension=0, tiled=True
    ).astype(f32)
    _, factor_one = norm_forward(residual, gain_one)
    grad_input = grad_mixed + norm_back_rows(residual, factor_one, gain_one, grad_act_one)
    return (
        result.astype(bf16)[None],
        loss_value,
        grad_input[None],
        grad_narrow[:, KVR + DR],
        grad_w_query,
        grad_narrow[:, : KVR + DR],
        grad_narrow[:slab_latent, KVR + DR + 2],
        grad_w_expand,
        grad_w_output,
        grad_narrow[:, KVR + DR + 1],
        grad_w_gate,
        grad_w_up,
        grad_w_down,
        expert_grads[0][None],
        expert_grads[1][None],
        expert_grads[2][None],
    )


def solution(mesh):
    tokens = P("fsdp", "ctx", None)
    rows = P(("ctx", "fsdp"), None)
    gain = P(("ctx", "fsdp"))
    wide = P("ctx", None, "fsdp")
    deep = P("ctx", "fsdp", None)
    in_specs = (
        tokens,
        tokens,
        P("fsdp", None),
        tokens,
        tokens,
        gain,
        rows,
        rows,
        gain,
        rows,
        rows,
        gain,
        rows,
        rows,
        rows,
        wide,
        wide,
        deep,
    )
    out_specs = (
        tokens,
        P(),
        tokens,
        gain,
        rows,
        rows,
        gain,
        rows,
        rows,
        gain,
        rows,
        rows,
        rows,
        wide,
        wide,
        deep,
    )
    return jax.shard_map(shards, mesh=mesh, in_specs=in_specs, out_specs=out_specs, check_vma=False)
```

```python
import functools
import math

import jax
import jax.numpy as jnp
from jax import lax
from jax.experimental import pallas as pl
from jax.experimental.pallas import tpu as pltpu
from jax.sharding import PartitionSpec as P

D = 2048
H = 16
DN = 128
DR = 64
DV = 128
KVR = 512
TOPK = 6
WIDE = 256

EPS = 1e-06
NEG = -1e30
MESH = pl.DeviceIdType.MESH
f32 = jnp.float32
bf16 = jnp.bfloat16


def norm_forward(rows, gain):
    factor = lax.rsqrt(jnp.mean(rows * rows, axis=-1, keepdims=True) + EPS)
    return (rows * factor * gain, factor)


def norm_back_rows(rows, factor, gain, grad_out):
    scaled = grad_out * gain
    normed = rows * factor
    return factor * (scaled - normed * jnp.mean(scaled * normed, axis=-1, keepdims=True))


def rotate(values, cosine, sine):
    half = values.shape[-1] // 2
    first = values[..., :half]
    second = values[..., half:]
    return jnp.concatenate(
        [first * cosine - second * sine, second * cosine + first * sine], axis=-1
    )


def rope_tables(offsets):
    freqs = 10000.0 ** (-(jnp.arange(DR // 2, dtype=f32) * 2.0) / DR)
    angle = offsets.astype(f32)[:, None] * freqs[None, :]
    return (jnp.cos(angle), jnp.sin(angle))


def silu_grads(gate_val, up_val, grad_hidden):
    sigma = jax.nn.sigmoid(gate_val)
    grad_gate = grad_hidden * up_val * sigma * (1.0 + gate_val * (1.0 - sigma))
    grad_up = grad_hidden * gate_val * sigma
    return (grad_gate.astype(bf16), grad_up.astype(bf16))


def dot(left, right):
    return jnp.dot(left, right, preferred_element_type=f32)


def dot_first(left, right):
    return lax.dot_general(left, right, (((0,), (0,)), ((), ())), preferred_element_type=f32)


def dot_last(left, right):
    return lax.dot_general(left, right, (((1,), (1,)), ((), ())), preferred_element_type=f32)


def flip(me, mask):
    out = me
    bit = 1
    while bit <= mask:
        if mask & bit:
            out = out + bit * (1 - 2 * ((me // bit) % 2))
        bit *= 2
    return out


def row_parts(rows, bits):
    low, high = [1, 2], [1 << k for k in range(bits - 1, 1, -1)]
    orders = (high + low, high + low[::-1], low + high)
    units = rows // 16
    if units < 3:
        return ((0, rows, tuple(orders[0])),)
    third = max(1, units // 4)
    first = (units - third) // 2
    counts = (first * 16, (units - third - first) * 16, third * 16)
    parts, start = [], 0
    for count, order in zip(counts, orders):
        parts.append((start, count, tuple(order)))
        start += count
    return tuple(parts)


def all_parts(shapes, bits):
    return tuple(
        (a,) + part for a, shape in enumerate(shapes) for part in row_parts(shape[-2], bits)
    )


def greet(bits):
    me = lax.axis_index("ctx")
    barrier = pltpu.get_barrier_semaphore()
    for k in range(bits):
        pl.semaphore_signal(
            barrier, inc=1, device_id={"ctx": flip(me, 1 << k)}, device_id_type=MESH
        )
    pl.semaphore_wait(barrier, bits)


def gather_events(parts, bits):
    events = []
    for p, (_, _, _, order) in enumerate(parts):
        for slot in range(1 << bits):
            hops = [k for k, b in enumerate(order) if slot & b]
            for k in range(hops[-1] + 1 if hops else 0, bits):
                events.append((len(hops), k, p, slot, order[k]))
    return tuple(sorted(events))


def gather_kernel(parts, bits, events, count, *refs):
    x_refs, o_refs = refs[:count], refs[count : 2 * count]
    send_sem, recv_sem, own_sem = refs[2 * count :]
    me = lax.axis_index("ctx")
    own = [
        pltpu.make_async_copy(x_refs[a], o_refs[a].at[me], own_sem.at[a]) for a in range(count)
    ]
    for item in own:
        item.start()
    greet(bits)

    def copy(p, slot, bit, index):
        a, start, size, _ = parts[p]
        rows = pl.ds(start, size)
        block = flip(me, slot)
        return pltpu.make_async_remote_copy(
            src_ref=x_refs[a].at[rows] if slot == 0 else o_refs[a].at[block, rows],
            dst_ref=o_refs[a].at[block, rows],
            send_sem=send_sem.at[index],
            recv_sem=recv_sem.at[p, slot ^ bit],
            device_id={"ctx": flip(me, bit)},
            device_id_type=MESH,
        )

    def arrived(p, slot):
        a, start, size, order = parts[p]
        rows = pl.ds(start, size)
        bit = [b for b in order if slot & b][-1]
        pltpu.make_async_remote_copy(
            src_ref=x_refs[a].at[rows],
            dst_ref=o_refs[a].at[flip(me, slot), rows],
            send_sem=send_sem.at[0],
            recv_sem=recv_sem.at[p, slot],
            device_id={"ctx": flip(me, bit)},
            device_id_type=MESH,
        ).wait_recv()

    seen = set()
    started = []
    for index, (_, _, p, slot, bit) in enumerate(events):
        if slot and (p, slot) not in seen:
            arrived(p, slot)
            seen.add((p, slot))
        sent = copy(p, slot, bit, index)
        sent.start()
        started.append(sent)
    for p in range(len(parts)):
        for slot in range(1, 1 << bits):
            if (p, slot) not in seen:
                arrived(p, slot)
    for sent in started:
        sent.wait_send()
    for item in own:
        item.wait()


def gather_ctx(arrays, bits, collective):
    parts = all_parts([item.shape for item in arrays], bits)
    events = gather_events(parts, bits)
    count = len(arrays)
    return pl.pallas_call(
        functools.partial(gather_kernel, parts, bits, events, count),
        name="gather_ctx",
        out_shape=[jax.ShapeDtypeStruct((1 << bits,) + item.shape, item.dtype) for item in arrays],
        in_specs=[pl.BlockSpec(memory_space=pl.ANY)] * count,
        out_specs=[pl.BlockSpec(memory_space=pl.ANY)] * count,
        scratch_shapes=[
            pltpu.SemaphoreType.DMA((len(events),)),
            pltpu.SemaphoreType.DMA((len(parts), 1 << bits)),
            pltpu.SemaphoreType.DMA((count,)),
        ],
        compiler_params=pltpu.CompilerParams(collective_id=collective, has_side_effects=True),
    )(*arrays)


def gather_multiply_kernel(
    parts, bits, events, shares, tile, x_ref, rows_ref, dy_ref, *refs
):
    lefts, refs = refs[: 3 * shares], refs[3 * shares :]
    o_ref, outs, refs = refs[0], refs[1:4], refs[4:]
    rows, dy, left, sent, got, stage = refs[:6]
    send_sem, recv_sem, own_sem, load_sem, out_sem, far_sem, near_sem = refs[6:]
    me, place = lax.axis_index("ctx"), lax.axis_index("fsdp")
    half, width = left.shape[2], rows.shape[1]
    tiles = width // tile
    loads = [pltpu.make_async_copy(rows_ref, rows, load_sem.at[3 * shares])]
    loads.append(pltpu.make_async_copy(dy_ref, dy, load_sem.at[3 * shares + 1]))
    order = list(range(3, 3 * shares)) + [0, 1, 2]
    for i in range(3 * shares):
        loads.append(pltpu.make_async_copy(lefts[i], left.at[i], load_sem.at[i]))
    own = pltpu.make_async_copy(x_ref, o_ref.at[me], own_sem)
    own.start()
    barrier = pltpu.get_barrier_semaphore()
    for k in range(bits):
        pl.semaphore_signal(
            barrier, inc=1, device_id={"ctx": flip(me, 1 << k)}, device_id_type=MESH
        )
    for r in range(1, shares):
        pl.semaphore_signal(
            barrier, inc=1, device_id={"fsdp": (place + r) % shares}, device_id_type=MESH
        )
    pl.semaphore_wait(barrier, bits + shares - 1)
    for i in [0, 2 + 3 % (3 * shares), 1] if shares > 1 else [0, 2, 1]:
        loads[i].start()
    for i in range(2, len(loads)):
        if i != 2 + 3 % (3 * shares):
            loads[i].start()
    ready = set()

    def need(i):
        if i not in ready:
            loads[i].wait()
            ready.add(i)

    def copy(p, slot, bit, index):
        _, start, size, _ = parts[p]
        part = pl.ds(start, size)
        block = flip(me, slot)
        return pltpu.make_async_remote_copy(
            src_ref=x_ref.at[part] if slot == 0 else o_ref.at[block, part],
            dst_ref=o_ref.at[block, part],
            send_sem=send_sem.at[index],
            recv_sem=recv_sem.at[p, slot ^ bit],
            device_id={"ctx": flip(me, bit)},
            device_id_type=MESH,
        )

    def arrived(p, slot):
        _, start, size, path = parts[p]
        part = pl.ds(start, size)
        bit = [b for b in path if slot & b][-1]
        pltpu.make_async_remote_copy(
            src_ref=x_ref.at[part],
            dst_ref=o_ref.at[flip(me, slot), part],
            send_sem=send_sem.at[0],
            recv_sem=recv_sem.at[p, slot],
            device_id={"ctx": flip(me, bit)},
            device_id_type=MESH,
        ).wait_recv()

    def far(i, t):
        spot = (i - 3, slice(None), pl.ds(t * tile, tile))
        return pltpu.make_async_remote_copy(
            src_ref=sent.at[spot],
            dst_ref=got.at[spot],
            send_sem=far_sem.at[i - 3, t],
            recv_sem=near_sem.at[i - 3, t],
            device_id={"fsdp": (place + shares - i // 3) % shares},
            device_id_type=MESH,
        )

    def store(i, t):
        buffer = (i * tiles + t) % 2
        return pltpu.make_async_copy(
            stage.at[buffer], outs[i].at[:, pl.ds(t * tile, tile)], out_sem.at[i, t]
        )

    def multiply(i, t):
        need(2 + i)
        need(1 if i % 3 == 2 else 0)
        right = dy if i % 3 == 2 else rows
        total = dot_first(left[i], right[:, t * tile : (t + 1) * tile])
        if i >= 3:
            sent[i - 3, :, t * tile : (t + 1) * tile] = total.astype(bf16)
            far(i, t).start()
            return
        for r in range(1, shares):
            far(i + 3 * r, t).wait_recv()
            total = total + got[i + 3 * r - 3, :, t * tile : (t + 1) * tile].astype(f32)
        last = i * tiles + t - 2
        if last >= 0:
            store(last // tiles, last % tiles).wait()
        stage[(i * tiles + t) % 2] = total.astype(bf16)
        store(i, t).start()

    work = [(i, t) for i in order for t in range(tiles)]
    done = 0
    seen = set()
    started = []
    for index, (_, _, p, slot, bit) in enumerate(events):
        if slot and (p, slot) not in seen:
            arrived(p, slot)
            seen.add((p, slot))
        item = copy(p, slot, bit, index)
        item.start()
        started.append(item)
        first = bits * len(parts)
        if index >= first:
            while done < len(work) * (index - first + 1) // (len(events) - first):
                multiply(*work[done])
                done += 1
    for p in range(len(parts)):
        for slot in range(1, 1 << bits):
            if (p, slot) not in seen:
                arrived(p, slot)
    for item in started:
        item.wait_send()
    own.wait()
    for i in range(3, 3 * shares):
        for t in range(tiles):
            far(i, t).wait_send()
    for last in range(max(0, 3 * tiles - 2), 3 * tiles):
        store(last // tiles, last % tiles).wait()


def gather_multiply(x, rows, dy, lefts, bits, collective):
    parts = all_parts([x.shape], bits)
    events = gather_events(parts, bits)
    shares = len(lefts) // 3
    count, half = lefts[0].shape
    width = rows.shape[1]
    tile = width // 2
    anywhere = pl.BlockSpec(memory_space=pl.ANY)
    others = max(1, 3 * shares - 3)
    return pl.pallas_call(
        functools.partial(gather_multiply_kernel, parts, bits, events, shares, tile),
        name="gather_multiply",
        out_shape=[jax.ShapeDtypeStruct((1 << bits,) + x.shape, x.dtype)]
        + [jax.ShapeDtypeStruct((half, width), bf16)] * 3,
        in_specs=[anywhere] * (3 + 3 * shares),
        out_specs=[anywhere] * 4,
        scratch_shapes=[
            pltpu.VMEM((count, width), bf16),
            pltpu.VMEM((count, width), bf16),
            pltpu.VMEM((3 * shares, count, half), bf16),
            pltpu.VMEM((others, half, width), bf16),
            pltpu.VMEM((others, half, width), bf16),
            pltpu.VMEM((2, half, tile), bf16),
            pltpu.SemaphoreType.DMA((len(events),)),
            pltpu.SemaphoreType.DMA((len(parts), 1 << bits)),
            pltpu.SemaphoreType.DMA,
            pltpu.SemaphoreType.DMA((3 * shares + 2,)),
            pltpu.SemaphoreType.DMA((3, width // tile)),
            pltpu.SemaphoreType.DMA((others, width // tile)),
            pltpu.SemaphoreType.DMA((others, width // tile)),
        ],
        compiler_params=pltpu.CompilerParams(
            collective_id=collective, has_side_effects=True, vmem_limit_bytes=60 << 20
        ),
    )(x, rows, dy, *lefts)


def scatter_events(parts, bits):
    events = []
    for p, (_, _, _, order) in enumerate(parts):
        for slot in range(1, 1 << bits):
            k = [i for i, b in enumerate(order) if slot & b][0]
            later = tuple(-int(bool(slot & b)) for b in order[k + 1 :])
            events.append((k, later, p, slot))
    return tuple((k, p, slot) for k, _, p, slot in sorted(events))


def scatter_kernel(parts, bits, events, count, *refs):
    x_refs, o_refs = refs[:count], refs[count : 2 * count]
    recvs, sends, owns = (refs[(2 + i) * count : (3 + i) * count] for i in range(3))
    send_sem, recv_sem, own_sem = refs[5 * count :]
    me = lax.axis_index("ctx")
    later = [sorted({s for k, p, s in events if k and parts[p][0] == a}) for a in range(count)]

    def load(a, slot):
        place = later[a].index(slot) + 1 if slot else 0
        return pltpu.make_async_copy(
            x_refs[a].at[flip(me, slot)], owns[a].at[place], own_sem.at[a, place]
        )

    greet(bits)

    def copy(p, slot, k, src):
        a, start, size, order = parts[p]
        return pltpu.make_async_remote_copy(
            src_ref=src,
            dst_ref=recvs[a].at[slot - 1, pl.ds(start, size)],
            send_sem=send_sem.at[p, slot - 1],
            recv_sem=recv_sem.at[p, slot - 1],
            device_id={"ctx": flip(me, order[k])},
            device_id_type=MESH,
        )

    loaded = set()

    def add_up(p, slot, k):
        a, start, size, order = parts[p]
        place = later[a].index(slot) + 1 if slot else 0
        if (a, slot) not in loaded:
            load(a, slot).wait()
            loaded.add((a, slot))
        for e in range(k):
            other = slot | order[e]
            copy(p, other, e, recvs[a].at[other - 1, pl.ds(start, size)]).wait_recv()
        target = sends[a].at[place - 1] if slot else o_refs[a]

        @pl.loop(0, size // 16)
        def _(t):
            part = pl.ds(pl.multiple_of(start + t * 16, 16), 16)
            total = owns[a][place, part].astype(f32)
            for e in range(k):
                total = total + recvs[a][(slot | order[e]) - 1, part].astype(f32)
            target[part] = total.astype(target.dtype)

    started = []
    first = [event for event in events if event[0] == 0]
    for index, (k, p, slot) in enumerate(events):
        a, start, size, order = parts[p]
        rows = pl.ds(start, size)
        if k == 0:
            src = x_refs[a].at[flip(me, slot), rows]
        else:
            add_up(p, slot, k)
            src = sends[a].at[later[a].index(slot), rows]
        sent = copy(p, slot, k, src)
        sent.start()
        started.append(sent)
        if index == len(first) // 2:
            for a in range(count):
                for own in [0] + later[a]:
                    load(a, own).start()
    for p in range(len(parts)):
        add_up(p, 0, bits)
    for sent in started:
        sent.wait_send()


def scatter_ctx(arrays, bits, collective):
    shapes = [item.shape[1:] for item in arrays]
    parts = all_parts(shapes, bits)
    parts = tuple((a, start, size, order[::-1]) for a, start, size, order in parts)
    events = scatter_events(parts, bits)
    count = len(arrays)
    others = (1 << bits) - 1
    held = [
        1 + len({s for k, p, s in events if k and parts[p][0] == a}) for a in range(count)
    ]
    return pl.pallas_call(
        functools.partial(scatter_kernel, parts, bits, events, count),
        name="scatter_ctx",
        out_shape=[jax.ShapeDtypeStruct(shape, f32) for shape in shapes],
        in_specs=[pl.BlockSpec(memory_space=pl.ANY)] * count,
        out_specs=[pl.BlockSpec(memory_space=pltpu.VMEM)] * count,
        scratch_shapes=[pltpu.VMEM((others,) + shape, bf16) for shape in shapes]
        + [pltpu.VMEM((n - 1,) + shape, bf16) for n, shape in zip(held, shapes)]
        + [pltpu.VMEM((n,) + shape, bf16) for n, shape in zip(held, shapes)]
        + [
            pltpu.SemaphoreType.DMA((len(parts), others)),
            pltpu.SemaphoreType.DMA((len(parts), others)),
            pltpu.SemaphoreType.DMA((count, max(held))),
        ],
        compiler_params=pltpu.CompilerParams(
            collective_id=collective, has_side_effects=True, vmem_limit_bytes=58 << 20
        ),
    )(*arrays)


def attend_kernel(block, count, q_ref, k_ref, v_ref, first_ref, wo_ref, o_ref, log_ref, part_ref):
    step = pl.program_id(0)
    for i in range(count):

        @pl.when(step == i)
        def _(i=i):
            extent = (i + 1) * block
            scores = dot_last(q_ref[...], k_ref[:extent, :])
            key_pos = lax.broadcasted_iota(jnp.int32, (block, extent), 1)
            query_pos = i * block + lax.broadcasted_iota(jnp.int32, (block, extent), 0)
            allowed = (key_pos >= first_ref[...]) & (key_pos <= query_pos)
            scores = jnp.where(allowed, scores, NEG)
            top = jnp.max(scores, axis=-1, keepdims=True)
            weights = jnp.exp(scores - top)
            total = jnp.sum(weights, axis=-1, keepdims=True)
            summed = dot(weights.astype(bf16), v_ref[:extent, :])
            o_ref[...] = summed / total
            log_ref[...] = top + jnp.log(total)
            part_ref[...] = dot((summed / total).astype(bf16), wo_ref[...]).astype(bf16)


def attend(queries, keys, values, first, w_output):
    length = queries.shape[0]
    block = min(256, length)
    count = length // block
    return pl.pallas_call(
        functools.partial(attend_kernel, block, count),
        name="attend",
        grid=(count,),
        out_shape=(
            jax.ShapeDtypeStruct((length, DV), f32),
            jax.ShapeDtypeStruct((length, 1), f32),
            jax.ShapeDtypeStruct((length, D), bf16),
        ),
        in_specs=[
            pl.BlockSpec((block, WIDE), lambda i: (i, 0)),
            pl.BlockSpec((length, WIDE), lambda i: (0, 0)),
            pl.BlockSpec((length, DV), lambda i: (0, 0)),
            pl.BlockSpec((block, 1), lambda i: (i, 0)),
            pl.BlockSpec((DV, D), lambda i: (0, 0)),
        ],
        out_specs=(
            pl.BlockSpec((block, DV), lambda i: (i, 0)),
            pl.BlockSpec((block, 1), lambda i: (i, 0)),
            pl.BlockSpec((block, D), lambda i: (i, 0)),
        ),
        compiler_params=pltpu.CompilerParams(vmem_limit_bytes=56 << 20),
        cost_estimate=pl.CostEstimate(
            flops=length * length * (DN + DR + DV),
            bytes_accessed=length * 2000,
            transcendentals=length * length // 2,
        ),
    )(queries, keys, values, first, w_output)


def attend_back_kernel(
    block, count, q_ref, k_ref, v_ref, m_ref, att_ref, wo_ref, first_ref, log_ref,
    dq_ref, dk_ref, dv_ref, gwo_ref,
):
    step = pl.program_id(0)

    @pl.when(step == 0)
    def _():
        dk_ref[...] = jnp.zeros_like(dk_ref)
        dv_ref[...] = jnp.zeros_like(dv_ref)
        gwo_ref[...] = jnp.zeros_like(gwo_ref)

    grad = dot_last(m_ref[...], wo_ref[...]).astype(bf16)
    gwo_ref[...] += dot_first(att_ref[...].astype(bf16), m_ref[...])
    delta = jnp.sum((grad.astype(f32) * att_ref[...]).T, axis=0, keepdims=True)
    for i in range(count):

        @pl.when(step == i)
        def _(i=i):
            extent = (i + 1) * block
            keys = k_ref[:extent, :]
            scores = dot_last(keys, q_ref[...])
            key_pos = lax.broadcasted_iota(jnp.int32, (extent, block), 0)
            query_pos = i * block + lax.broadcasted_iota(jnp.int32, (extent, block), 1)
            allowed = (key_pos >= first_ref[...]) & (key_pos <= query_pos)
            weights = jnp.where(allowed, jnp.exp(scores - log_ref[...]), 0.0)
            grad_weights = dot_last(v_ref[:extent, :], grad)
            grad_scores = (weights * (grad_weights - delta)).astype(bf16)
            dv_ref[:extent, :] += dot(weights.astype(bf16), grad)
            dk_ref[:extent, :] += dot(grad_scores, q_ref[...])
            dq_ref[...] = dot_first(grad_scores, keys)


def attend_back(queries, keys, values, grad_mixed, attended, w_output, first, log_total):
    length = queries.shape[0]
    block = min(256, length)
    count = length // block
    row = lambda: pl.BlockSpec((1, block), lambda i: (0, i))
    whole = lambda height, width: pl.BlockSpec((height, width), lambda i: (0, 0))
    part = lambda width: pl.BlockSpec((block, width), lambda i: (i, 0))
    return pl.pallas_call(
        functools.partial(attend_back_kernel, block, count),
        name="attend_back",
        grid=(count,),
        out_shape=(
            jax.ShapeDtypeStruct((length, WIDE), f32),
            jax.ShapeDtypeStruct((length, WIDE), f32),
            jax.ShapeDtypeStruct((length, DV), f32),
            jax.ShapeDtypeStruct((DV, D), f32),
        ),
        in_specs=[
            part(WIDE),
            whole(length, WIDE),
            whole(length, DV),
            part(D),
            part(DV),
            whole(DV, D),
            row(),
            row(),
        ],
        out_specs=(part(WIDE), whole(length, WIDE), whole(length, DV), whole(DV, D)),
        compiler_params=pltpu.CompilerParams(vmem_limit_bytes=56 << 20),
        cost_estimate=pl.CostEstimate(
            flops=length * length * (3 * (DN + DR) + 2 * DV),
            bytes_accessed=length * 4000,
            transcendentals=length * length // 2,
        ),
    )(queries, keys, values, grad_mixed, attended, w_output, first, log_total)


def lanes_of(value):
    return lax.broadcasted_iota(jnp.int32, value.shape, len(value.shape) - 1)


def swap_lanes(ropes):
    return jnp.where(
        lanes_of(ropes) % DR < DR // 2, -pltpu.roll(ropes, 96, 1), pltpu.roll(ropes, 32, 1)
    )


def assemble_kernel(
    cycle, slab, mine_ref, other_ref, mine_n_ref, other_n_ref,
    w_ref, we_ref, gains_ref, narrow_ref, expand_ref,
):
    me = lax.axis_index("fsdp")
    for f, (pack_ref, slim_ref) in enumerate(((mine_ref, mine_n_ref), (other_ref, other_n_ref))):
        owner = me if f == 0 else 1 - me

        @pl.loop(0, cycle)
        def _(c):
            rows = pl.ds(pl.multiple_of((c * 2 + owner) * slab, slab), slab)
            w_ref[rows, :DN] = pack_ref[c, :, :DN]
            w_ref[rows, 3 * DN :] = slim_ref[c, :, :KVR]
            tail = pack_ref[c, :, DN:256].astype(f32)
            slim = slim_ref[c, :, KVR:].astype(f32)
            ropes = jnp.where(lanes_of(tail) < DR, tail, pltpu.roll(slim, DR, 1))
            w_ref[rows, DN : 2 * DN] = ropes.astype(bf16)
            w_ref[rows, 2 * DN : 3 * DN] = swap_lanes(ropes).astype(bf16)
            narrow_ref[rows, :] = slim
            quarter = slab // 4
            for q in range(2):
                left = tail[2 * q * quarter : (2 * q + 1) * quarter]
                right = tail[(2 * q + 1) * quarter : (2 * q + 2) * quarter]
                both = jnp.where(lanes_of(left) < DR, pltpu.roll(left, DR, 1), right)
                spot = pl.ds(pl.multiple_of((c * 2 + owner) * quarter, quarter), quarter)
                expand_ref[spot, q * DN : (q + 1) * DN] = both

    we_ref[...] = expand_ref[...].astype(bf16)
    gains_ref[...] = narrow_ref[...].T[DR : DR + 8, :]


def assemble(mine, other, mine_n, other_n):
    cycle, slab, _ = mine.shape
    return pl.pallas_call(
        functools.partial(assemble_kernel, cycle, slab),
        name="assemble",
        out_shape=(
            jax.ShapeDtypeStruct((D, 3 * DN + KVR), bf16),
            jax.ShapeDtypeStruct((KVR, DN + DV), bf16),
            jax.ShapeDtypeStruct((8, D), f32),
        ),
        scratch_shapes=[pltpu.VMEM((D, DN), f32), pltpu.VMEM((KVR, DN + DV), f32)],
        compiler_params=pltpu.CompilerParams(vmem_limit_bytes=40 << 20),
    )(mine, other, mine_n, other_n)


def finish_kernel(cycle, slab, gw_ref, gwe_ref, w_ref, we_ref, extra_ref, first_ref, slim_ref):
    quarter = slab // 4
    turned = gw_ref[:, 2 * DN : 3 * DN]
    ropes = gw_ref[:, DN : 2 * DN] - swap_lanes(turned)
    gain_one = jnp.sum(gw_ref[...] * w_ref[...].astype(f32), axis=1, keepdims=True)
    gain_latent = jnp.sum(gwe_ref[...] * we_ref[...].astype(f32), axis=1, keepdims=True)
    lanes = lanes_of(ropes)
    first_ref[:, :DN] = gw_ref[:, :DN].astype(bf16)
    slim_ref[:, :KVR] = gw_ref[:, 3 * DN :].astype(bf16)
    tail = jnp.where(lanes < DR, pltpu.roll(ropes, DR, 1), 0.0)
    tail = jnp.where(lanes == DR, gain_one, tail)
    tail = jnp.where(lanes == DR + 1, extra_ref[...], tail)
    for part in range(cycle * 2):
        rows = slice(part * slab, (part + 1) * slab)
        some = slice(part * quarter, (part + 1) * quarter)
        expand = gwe_ref[some, :]
        pieces = [
            pltpu.roll(expand[:, :DN], DR, 1),
            expand[:, :DN],
            pltpu.roll(expand[:, DN:], DR, 1),
            expand[:, DN:],
        ]
        pieces = jnp.concatenate(pieces, axis=0)
        first_ref[rows, DN:] = jnp.where(lanes[rows] < DR, ropes[rows], pieces).astype(bf16)
        column = jnp.concatenate(
            [gain_latent[some], jnp.zeros((slab - quarter, 1), f32)], axis=0
        )
        slim_ref[rows, KVR:] = jnp.where(lanes[rows] == DR + 2, column, tail[rows]).astype(bf16)


def finish(grad_w, grad_we, w_cat, w_expand, extra, cycle, slab):
    return pl.pallas_call(
        functools.partial(finish_kernel, cycle, slab),
        name="finish",
        out_shape=(
            jax.ShapeDtypeStruct((D, 256), bf16),
            jax.ShapeDtypeStruct((D, KVR + DN), bf16),
        ),
        compiler_params=pltpu.CompilerParams(vmem_limit_bytes=56 << 20),
    )(grad_w, grad_we, w_cat, w_expand, extra)


def place_lanes(out_ref, pieces, width):
    total = width * len(pieces)
    for start in range(0, total, DN):
        tile = None
        for c in range(start // width, min(len(pieces), -(-(start + DN) // width))):
            moved = pieces[c]
            shift = (c * width - start) % 256
            if shift:
                moved = pltpu.roll(moved, shift, 1)
            moved = moved[:, :DN]
            lanes = lanes_of(moved) + start
            inside = (lanes >= c * width) & (lanes < (c + 1) * width)
            tile = jnp.where(inside, moved, 0.0 if tile is None else tile)
        out_ref[:, start : start + DN] = tile


def spread_kernel(cycle, slab, pack_ref, pack_s_ref, gq_ref, gwe_ref, gg_ref, gu_ref):
    quarter = slab // 4
    for ref, out_ref, start in (
        (pack_ref, gq_ref, 0),
        (pack_s_ref, gg_ref, 0),
        (pack_s_ref, gu_ref, 256),
    ):
        pieces = [ref[c, :, start : start + 256].astype(f32) for c in range(cycle)]
        place_lanes(out_ref, pieces, out_ref.shape[1] // cycle)
    for c in range(cycle):
        tail = pack_ref[c, :, DN:256].astype(f32)
        for q in range(2):
            left = tail[2 * q * quarter : (2 * q + 1) * quarter]
            right = tail[(2 * q + 1) * quarter : (2 * q + 2) * quarter]
            both = jnp.where(lanes_of(left) < DR, pltpu.roll(left, DR, 1), right)
            at = c * 2 * DN + q * DN
            gwe_ref[:, at : at + DN] = both


def spread(packed, packed_s, widths):
    cycle, slab, _ = packed.shape
    return pl.pallas_call(
        functools.partial(spread_kernel, cycle, slab),
        name="spread",
        out_shape=(
            jax.ShapeDtypeStruct((slab, widths[0]), f32),
            jax.ShapeDtypeStruct((slab // 4, widths[1]), f32),
            jax.ShapeDtypeStruct((slab, widths[2]), f32),
            jax.ShapeDtypeStruct((slab, widths[3]), f32),
        ),
        compiler_params=pltpu.CompilerParams(vmem_limit_bytes=40 << 20),
    )(packed, packed_s)


def fixed(shape):
    return pl.BlockSpec(shape, lambda i: (0,) * len(shape), pipeline_mode=pl.Buffered(1))


def second(shape):
    return pl.BlockSpec(shape, lambda i: (0, 1), pipeline_mode=pl.Buffered(1))


def by_rows(rows, cols):
    return pl.BlockSpec((rows, cols), lambda i: (i, 0))


def project_kernel(
    scale, x_ref, gain_ref, w_ref, gain_l_ref, we_ref, cos_ref, sin_ref,
    act_ref, q_ref, k_ref, v_ref, latent_ref, raw_ref,
):
    act = norm_forward(x_ref[...].astype(f32), gain_ref[...])[0].astype(bf16)
    act_ref[...] = act
    raw = dot(act, w_ref[...])
    turned = raw[:, DN : 2 * DN] * cos_ref[...] + raw[:, 2 * DN : 3 * DN] * sin_ref[...]
    low = lax.broadcasted_iota(jnp.int32, turned.shape, 1) < DR
    q_ref[:, :DN] = (raw[:, :DN] * scale).astype(bf16)
    q_ref[:, DN:] = jnp.where(low, turned * scale, 0.0).astype(bf16)
    raw_latent = raw[:, 3 * DN :]
    raw_ref[...] = raw_latent
    latent = norm_forward(raw_latent, gain_l_ref[...])[0].astype(bf16)
    latent_ref[...] = latent
    expanded = dot(latent, we_ref[...]).astype(bf16)
    k_ref[:, :DN] = expanded[:, :DN]
    k_ref[:, DN:] = jnp.where(low, pltpu.roll(turned, DR, 1), 0.0).astype(bf16)
    v_ref[...] = expanded[:, DN:]


def project(x, gain, w_cat, gain_latent, w_expand, cosine, sine, scale):
    length = x.shape[0]
    block = min(256, length)
    width = w_cat.shape[1]
    return pl.pallas_call(
        functools.partial(project_kernel, scale),
        name="project",
        grid=(length // block,),
        out_shape=(
            jax.ShapeDtypeStruct((length, D), bf16),
            jax.ShapeDtypeStruct((length, WIDE), bf16),
            jax.ShapeDtypeStruct((length, WIDE), bf16),
            jax.ShapeDtypeStruct((length, DV), bf16),
            jax.ShapeDtypeStruct((length, KVR), bf16),
            jax.ShapeDtypeStruct((length, KVR), f32),
        ),
        in_specs=[
            by_rows(block, D),
            fixed((1, D)),
            fixed((D, width)),
            fixed((1, KVR)),
            fixed((KVR, DN + DV)),
            by_rows(block, DN),
            by_rows(block, DN),
        ],
        out_specs=(
            by_rows(block, D),
            by_rows(block, WIDE),
            by_rows(block, WIDE),
            by_rows(block, DV),
            by_rows(block, KVR),
            by_rows(block, KVR),
        ),
        compiler_params=pltpu.CompilerParams(vmem_limit_bytes=40 << 20),
        cost_estimate=pl.CostEstimate(
            flops=2 * length * D * width, bytes_accessed=length * D * 6, transcendentals=0
        ),
    )(x, gain[None, :], w_cat, gain_latent[None, :], w_expand, cosine, sine)


def project_back_kernel(
    scale, copies, dq_ref, dk_ref, dv_ref, raw_ref, latent_ref, act_ref, cos_ref, sin_ref,
    w_ref, we_ref, gain_l_ref, keep_q_ref, keep_e_ref, part_ref, gw_ref, gwe_ref,
):
    @pl.when(pl.program_id(0) == 0)
    def _():
        gw_ref[...] = jnp.zeros_like(gw_ref)
        gwe_ref[...] = jnp.zeros_like(gwe_ref)

    grad_q = dq_ref[...] * scale
    grad_k = dk_ref[:, :DN]
    grad_v = dv_ref[...]
    if copies > 1:
        grad_q = grad_q * keep_q_ref[...]
        grad_k = grad_k * keep_e_ref[:, :DN]
        grad_v = grad_v * keep_e_ref[:, DN:]
    rope_q = grad_q[:, DN:]
    low = lax.broadcasted_iota(jnp.int32, rope_q.shape, 1) < DR
    rope_k = jnp.where(low, dk_ref[:, DN:] * (1.0 / copies), 0.0)
    ropes = jnp.where(low, rope_q, pltpu.roll(rope_k, DR, 1))
    expanded = jnp.concatenate([grad_k, grad_v], axis=-1).astype(bf16)
    grad_latent = dot_last(expanded, we_ref[...])
    raw = raw_ref[...]
    factor = lax.rsqrt(jnp.mean(raw * raw, axis=-1, keepdims=True) + EPS)
    grad_latent = norm_back_rows(raw, factor, gain_l_ref[...], grad_latent)
    grads = jnp.concatenate(
        [
            grad_q[:, :DN].astype(bf16),
            (ropes * cos_ref[...]).astype(bf16),
            (ropes * sin_ref[...]).astype(bf16),
            grad_latent.astype(bf16),
        ],
        axis=-1,
    )
    part_ref[...] = dot_last(grads, w_ref[...]).astype(bf16)
    gw_ref[...] += dot_first(act_ref[...], grads)
    gwe_ref[...] += dot_first(latent_ref[...], expanded)


def project_back(
    grad_q, grad_k, grad_v, raw, latent, act, cosine, sine, w_cat, w_expand, gain_latent, keep_q,
    keep_e, scale, copies,
):
    length = act.shape[0]
    block = min(256, length)
    width = w_cat.shape[1]
    return pl.pallas_call(
        functools.partial(project_back_kernel, scale, copies),
        name="project_back",
        grid=(length // block,),
        out_shape=(
            jax.ShapeDtypeStruct((length, D), bf16),
            jax.ShapeDtypeStruct((D, width), f32),
            jax.ShapeDtypeStruct((KVR, DN + DV), f32),
        ),
        in_specs=[
            by_rows(block, WIDE),
            by_rows(block, WIDE),
            by_rows(block, DV),
            by_rows(block, KVR),
            by_rows(block, KVR),
            by_rows(block, D),
            by_rows(block, DN),
            by_rows(block, DN),
            fixed((D, width)),
            fixed((KVR, DN + DV)),
            fixed((1, KVR)),
            fixed((1, WIDE)),
            fixed((1, DN + DV)),
        ],
        out_specs=(
            by_rows(block, D),
            pl.BlockSpec((D, width), lambda i: (0, 0)),
            pl.BlockSpec((KVR, DN + DV), lambda i: (0, 0)),
        ),
        compiler_params=pltpu.CompilerParams(vmem_limit_bytes=56 << 20),
        cost_estimate=pl.CostEstimate(
            flops=4 * length * D * width, bytes_accessed=length * D * 6, transcendentals=0
        ),
    )(
        grad_q, grad_k, grad_v, raw, latent, act, cosine, sine, w_cat, w_expand,
        gain_latent[None, :], keep_q, keep_e,
    )


def choose(shape, dim, place):
    return (lax.broadcasted_iota(jnp.int32, shape, dim) == place).astype(f32).astype(bf16)


def experts_kernel(shares, unit, capacity, tokens, *refs):
    x_ref, row_ref, col_ref, prob_ref = refs[:4]
    weights = refs[4 : 4 + 3 * shares]
    wgs_ref, wus_ref, wds_ref = refs[4 + 3 * shares : 7 + 3 * shares]
    outs = refs[7 + 3 * shares :]
    part_ref, rows_ref, gs_ref, us_ref, hs_ref = outs[:5]
    kept = outs[5:]
    tall, short = unit * tokens, unit * capacity
    count = x_ref.shape[0] // tall
    for j in range(count):
        inside = slice(j * tall, (j + 1) * tall)
        pick = choose((short, tall), 0, row_ref[:, inside])
        rows_ref[j * short : (j + 1) * short, :] = dot(pick, x_ref[inside, :]).astype(bf16)
    rows = rows_ref[...]
    total = 0.0
    for s in range(shares):
        wg_ref, wu_ref, wd_ref = weights[3 * s : 3 * s + 3]
        gate = dot_last(rows, wg_ref[...])
        up = dot_last(rows, wu_ref[...])
        hidden = (gate * jax.nn.sigmoid(gate) * up).astype(bf16)
        for ref, value in zip(kept[3 * s : 3 * s + 3], (gate, up, hidden)):
            ref[...] = value.astype(bf16)
        total = total + dot(hidden, wd_ref[...])
    total = (total * prob_ref[...]).astype(bf16)
    gate = dot(x_ref[...], wgs_ref[...])
    up = dot(x_ref[...], wus_ref[...])
    hidden = (gate * jax.nn.sigmoid(gate) * up).astype(bf16)
    gs_ref[...] = gate.astype(bf16)
    us_ref[...] = up.astype(bf16)
    hs_ref[...] = hidden
    for j in range(count):
        inside = slice(j * tall, (j + 1) * tall)
        put = choose((tall, short), 1, col_ref[inside, :])
        part_ref[inside, :] = (
            dot(put, total[j * short : (j + 1) * short, :])
            + dot(hidden[inside, :], wds_ref[...])
        ).astype(bf16)


def expert_sizes(capacity, tokens, length):
    unit = 1
    while unit * capacity % 16:
        unit *= 2
    blocks = max(4, unit)
    return unit, blocks * tokens, blocks * capacity, length // (blocks * tokens)


def experts(x, place_row, place_col, prob, weights, shared, capacity, tokens):
    length = x.shape[0]
    unit, tall, short, steps = expert_sizes(capacity, tokens, length)
    shares = len(weights) // 3
    half = weights[0].shape[0]
    width = shared[2].shape[0]
    wide = [fixed((half, D))] * (3 * shares)
    return pl.pallas_call(
        functools.partial(experts_kernel, shares, unit, capacity, tokens),
        name="experts",
        grid=(steps,),
        out_shape=[
            jax.ShapeDtypeStruct((length, D), bf16),
            jax.ShapeDtypeStruct((steps * short, D), bf16),
        ]
        + [jax.ShapeDtypeStruct((length, width), bf16)] * 3
        + [jax.ShapeDtypeStruct((steps * short, half), bf16)] * (3 * shares),
        in_specs=[
            by_rows(tall, D),
            pl.BlockSpec((1, tall), lambda i: (0, i)),
            by_rows(tall, 1),
            by_rows(short, 1),
        ]
        + wide
        + [fixed((D, width)), second((D, width)), fixed((width, D))],
        out_specs=[by_rows(tall, D), by_rows(short, D)]
        + [by_rows(tall, width)] * 3
        + [by_rows(short, half)] * (3 * shares),
        compiler_params=pltpu.CompilerParams(vmem_limit_bytes=58 << 20),
        cost_estimate=pl.CostEstimate(
            flops=6 * D * (steps * short * half * shares + length * width),
            bytes_accessed=30 << 20,
            transcendentals=0,
        ),
    )(x, place_row, place_col, prob, *weights, *shared)


def experts_back_kernel(shares, unit, capacity, tokens, *refs):
    d_ref, x_ref, row_ref, col_ref, prob_ref, gs_ref, us_ref, hs_ref = refs[:8]
    refs = refs[8:]
    kept, refs = refs[: 2 * shares], refs[2 * shares :]
    weights, refs = refs[: 3 * shares], refs[3 * shares :]
    wgs_ref, wus_ref, wds_ref = refs[:3]
    part_ref, dy_ref, gws_ref, gwd_ref = refs[3:7]
    grads, (gwg_ref, gwu_ref) = refs[7:-2], refs[-2:]

    @pl.when(pl.program_id(0) == 0)
    def _():
        for ref in (gwg_ref, gwu_ref, gwd_ref):
            ref[...] = jnp.zeros_like(ref)

    tall, short = unit * tokens, unit * capacity
    count = x_ref.shape[0] // tall
    for j in range(count):
        inside = slice(j * tall, (j + 1) * tall)
        taken = slice(j * short, (j + 1) * short)
        pick = choose((short, tall), 0, row_ref[:, inside])
        dy_ref[taken, :] = (dot(pick, d_ref[inside, :]) * prob_ref[taken, :]).astype(bf16)
    total = 0.0
    for s in range(shares):
        wg_ref, wu_ref, wd_ref = weights[3 * s : 3 * s + 3]
        grad_hidden = dot_last(dy_ref[...], wd_ref[...])
        gate, up = (ref[...].astype(f32) for ref in kept[2 * s : 2 * s + 2])
        grad_gate, grad_up = silu_grads(gate, up, grad_hidden)
        grads[2 * s][...] = grad_gate
        grads[2 * s + 1][...] = grad_up
        total = total + dot(grad_gate, wg_ref[...]) + dot(grad_up, wu_ref[...])
    total = total.astype(bf16)
    grad_hidden = dot_last(d_ref[...], wds_ref[...])
    grad_gate, grad_up = silu_grads(
        gs_ref[...].astype(f32), us_ref[...].astype(f32), grad_hidden
    )
    gwg_ref[...] += dot_first(grad_gate, x_ref[...])
    gwu_ref[...] += dot_first(grad_up, x_ref[...])
    gwd_ref[...] += dot_first(hs_ref[...], d_ref[...])
    for j in range(count):
        inside = slice(j * tall, (j + 1) * tall)
        put = choose((tall, short), 1, col_ref[inside, :])
        part_ref[inside, :] = (
            dot(put, total[j * short : (j + 1) * short, :])
            + dot_last(grad_gate[inside, :], wgs_ref[...])
            + dot_last(grad_up[inside, :], wus_ref[...])
        ).astype(bf16)

    @pl.when(pl.program_id(0) == pl.num_programs(0) - 1)
    def _():
        width = gwg_ref.shape[0]
        gws_ref[:, :width] = gwg_ref[...].T.astype(bf16)
        gws_ref[:, width:] = gwu_ref[...].T.astype(bf16)


def experts_back(d, x, place_row, place_col, prob, saved, kept, weights, shared, capacity, tokens):
    length = x.shape[0]
    unit, tall, short, steps = expert_sizes(capacity, tokens, length)
    shares = len(weights) // 3
    half = weights[0].shape[0]
    width = shared[2].shape[0]
    wide = [fixed((half, D))] * (3 * shares)
    return pl.pallas_call(
        functools.partial(experts_back_kernel, shares, unit, capacity, tokens),
        name="experts_back",
        grid=(steps,),
        out_shape=[
            jax.ShapeDtypeStruct((length, D), bf16),
            jax.ShapeDtypeStruct((steps * short, D), bf16),
        ]
        + [jax.ShapeDtypeStruct((D, 2 * width), bf16), jax.ShapeDtypeStruct((width, D), f32)]
        + [jax.ShapeDtypeStruct((steps * short, half), bf16)] * (2 * shares),
        in_specs=[
            by_rows(tall, D),
            by_rows(tall, D),
            pl.BlockSpec((1, tall), lambda i: (0, i)),
            by_rows(tall, 1),
            by_rows(short, 1),
        ]
        + [by_rows(tall, width)] * 3
        + [by_rows(short, half)] * (2 * shares)
        + wide
        + [fixed((D, width)), second((D, width)), fixed((width, D))],
        out_specs=[by_rows(tall, D), by_rows(short, D)]
        + [fixed((D, 2 * width)), fixed((width, D))]
        + [by_rows(short, half)] * (2 * shares),
        scratch_shapes=[pltpu.VMEM((width, D), f32)] * 2,
        compiler_params=pltpu.CompilerParams(vmem_limit_bytes=60 << 20),
        cost_estimate=pl.CostEstimate(
            flops=6 * D * (steps * short * half * shares + 2 * length * width),
            bytes_accessed=50 << 20,
            transcendentals=0,
        ),
    )(d, x, place_row, place_col, prob, *saved, *kept, *weights, *shared)


def shift_fsdp(x, groups, by):
    return lax.ppermute(x, "fsdp", [(i, (i + by) % groups) for i in range(groups)])


def gather_fsdp(x, groups):
    if groups != 2:
        return lax.all_gather(x, "fsdp", axis=0)
    other = shift_fsdp(x, groups, 1)
    mine_first = lax.axis_index("fsdp") == 0
    return jnp.stack([jnp.where(mine_first, x, other), jnp.where(mine_first, other, x)])


def scatter_fsdp(x, groups):
    if groups != 2:
        return lax.psum_scatter(x.astype(bf16), "fsdp", scatter_dimension=0).astype(f32)
    me = lax.axis_index("fsdp")
    away = lax.dynamic_index_in_dim(x, 1 - me, 0, keepdims=False).astype(bf16)
    mine = lax.dynamic_index_in_dim(x, me, 0, keepdims=False).astype(f32)
    return mine + shift_fsdp(away, groups, 1).astype(f32)


def shards(
    hidden_in,
    teacher,
    doc_starts,
    routes,
    gate_logits,
    input_gain,
    query_weight,
    latent_weight,
    latent_gain,
    expand_weight,
    output_weight,
    mixer_gain,
    shared_gate,
    shared_up,
    shared_down,
    expert_gate,
    expert_up,
    expert_down,
):
    cycle = lax.axis_size("ctx")
    groups = lax.axis_size("fsdp")
    bits = cycle.bit_length() - 1
    tokens = hidden_in.shape[1]
    length = tokens * cycle
    capacity = min(tokens, 3 * tokens * TOPK // (2 * cycle))
    scale = (DN + DR) ** (-0.5)
    copies = max(1, cycle // H)
    ctx_index = lax.axis_index("ctx")
    copy_index = ctx_index % copies
    slab = query_weight.shape[0]
    slab_latent = expand_weight.shape[0]

    def pieces(weight):
        rows, width = weight.shape
        return jnp.transpose(weight.reshape(rows, cycle, width // cycle), (1, 0, 2))

    def padded(item, width):
        return jnp.pad(item, ((0, 0), (0, 0), (0, width - item.shape[2])))

    def exchange(packed):
        return lax.all_to_all(packed, "ctx", split_axis=0, concat_axis=0, tiled=True)

    def same_head(part, axis):
        if copies == 1:
            return part
        teams = [[i * copies + j for j in range(copies)] for i in range(H)]
        return lax.all_gather(part, "ctx", axis=axis, tiled=True, axis_index_groups=teams)

    def own_part(full, axis=1):
        if copies == 1:
            return full
        width = full.shape[axis] // copies
        return lax.dynamic_slice_in_dim(full, copy_index * width, width, axis)

    def swap(pair):
        half = pair.shape[1] // 2
        return jnp.concatenate([-pair[:, half:], pair[:, :half]], axis=1)

    def all_rows(item):
        both = jnp.transpose(gather_fsdp(item, groups), (1, 0, 2, 3))
        return both.reshape(-1, item.shape[2])

    fast = copies == 1 and groups == 2 and cycle * groups * slab == D and slab == 64
    part_q, part_e = H * (DN + DR) // cycle, H * (DN + DV) // cycle
    part_s = shared_gate.shape[1] // cycle
    shared_width = -(-part_s // 128) * 128

    probs = jax.nn.softmax(gate_logits[0], axis=-1)
    chosen = routes[0][:, :, None] == jnp.arange(cycle, dtype=jnp.int32)[None, None, :]
    dense_probs = jnp.sum(jnp.where(chosen, probs[:, :, None], 0.0), axis=1).T
    high = lax.reduce_precision(dense_probs, 8, 7)
    dense_probs = jnp.concatenate([high, dense_probs - high], axis=1).astype(bf16)
    prob_width = 2 * tokens // slab
    dense_probs = dense_probs.reshape(cycle, slab, prob_width)
    expand_pieces = pieces(expand_weight)
    if fast:
        quarter = part_e // 4
        expand_pieces = jnp.concatenate(
            [expand_pieces[:, :, q * quarter : (q + 1) * quarter] for q in range(4)], axis=1
        )
    else:
        expand_pieces = expand_pieces.reshape(cycle, slab, -1)
    block_q = -(-(part_q + expand_pieces.shape[2]) // 128) * 128
    block_s = -(-(part_s + prob_width) // 128) * 128
    packed = padded(jnp.concatenate([pieces(query_weight), expand_pieces], axis=2), block_q)
    packed = exchange(packed)
    packed_s = jnp.concatenate(
        [
            padded(jnp.concatenate([pieces(shared_gate), dense_probs], axis=2), block_s),
            padded(pieces(shared_up), block_s),
        ],
        axis=2,
    )
    narrow = jnp.concatenate(
        [
            latent_weight,
            input_gain[:, None],
            mixer_gain[:, None],
            jnp.concatenate([latent_gain, jnp.zeros((slab - slab_latent,), bf16)])[:, None],
            jnp.zeros((slab, -(KVR + DR + 3) % 128), bf16),
        ],
        axis=1,
    )
    w_down_s = gather_fsdp(shared_down, groups).reshape(-1, D)
    w_down_s = jnp.pad(w_down_s, ((0, shared_width - w_down_s.shape[0]), (0, 0)))
    w_output = gather_fsdp(output_weight, groups).reshape(-1, D)
    if copies > 1:
        rows_o = w_output.shape[0]
        own_output = lax.dynamic_update_slice_in_dim(
            jnp.zeros((DV, D), bf16), w_output, copy_index * rows_o, 0
        )
        w_output = same_head(w_output, 0)
    else:
        own_output = w_output
    weights = [expert_gate[0].T, expert_up[0].T, expert_down[0]]
    for r in range(1, groups):
        weights += [shift_fsdp(item, groups, r) for item in weights[:3]]
    starts = doc_starts[0]
    positions = jnp.arange(length, dtype=jnp.int32)
    inside = starts[None, :] <= positions[:, None]
    first_pos = jnp.max(jnp.where(inside, starts[None, :], 0), axis=1)
    cosine, sine = rope_tables(positions - first_pos)
    cosine = jnp.tile(cosine, (1, 4))
    sine = jnp.tile(sine, (1, 4))

    all_hidden, narrow = gather_ctx([hidden_in[0], narrow], bits, 1)
    packed_s, _ = lax.optimization_barrier((packed_s, all_hidden))
    packed_s = exchange(packed_s)
    my_probs = packed_s[:, :, part_s : part_s + prob_width]
    my_probs = my_probs.reshape(cycle, 2, tokens).astype(f32)
    my_probs = my_probs[:, 0] + my_probs[:, 1]
    if fast:
        w_cat, w_expand, gains = assemble(
            packed, shift_fsdp(packed, groups, 1), narrow, shift_fsdp(narrow, groups, 1)
        )
        gain_one, gain_two = gains[0], gains[1]
        gain_latent = gains[2].reshape(-1, slab)[:, :slab_latent].reshape(-1)
    else:
        narrow, packed = all_rows(narrow), all_rows(packed)
        gain_one = narrow[:, KVR + DR].astype(f32)
        gain_two = narrow[:, KVR + DR + 1].astype(f32)
        gain_latent = narrow[:, KVR + DR + 2].reshape(-1, slab)[:, :slab_latent]
        gain_latent = gain_latent.reshape(-1).astype(f32)
        w_query = same_head(packed[:, :part_q], 1)
        w_expand = packed[:, part_q : part_q + expand_pieces.shape[2]].reshape(KVR, part_e)
        w_expand = same_head(w_expand, 1)
        rope_k = narrow[:, KVR : KVR + DR]
        w_cat = jnp.concatenate(
            [w_query, rope_k, swap(w_query[:, DN:]), swap(rope_k), narrow[:, :KVR]], axis=1
        )

    w_both_s = all_rows(packed_s)

    residual = hidden_in[0].astype(f32)
    act_one, queries, keys, values, latent, latent_raw = project(
        all_hidden.reshape(length, D), gain_one, w_cat, gain_latent, w_expand, cosine, sine, scale
    )
    attended, log_total, partial = attend(
        queries, keys, values, first_pos[:, None], own_output
    )
    (mixing,) = scatter_ctx([partial.reshape(cycle, tokens, D)], bits, 3)
    mixed = residual + mixing

    normed_two, factor_two = norm_forward(mixed, gain_two)
    (all_act,) = gather_ctx([normed_two.astype(bf16)], bits, 2)
    all_act = all_act.reshape(length, D)
    used = my_probs > 0.0
    place = jnp.cumsum(used.astype(jnp.int32), axis=1) - 1
    slots = jnp.arange(capacity, dtype=jnp.int32)
    select = (place[:, None, :] == slots[None, :, None]) & used[:, None, :]
    slot_probs = jnp.sum(jnp.where(select, my_probs[:, None, :], 0.0), axis=-1).reshape(-1, 1)
    unit = expert_sizes(capacity, tokens, length)[0]
    turn = jnp.arange(cycle, dtype=jnp.int32)[:, None] % unit
    place = jnp.where(used, place + capacity * turn, -1).reshape(-1)
    routing = (place[None, :], place[:, None], slot_probs)
    shared = [w_both_s, w_both_s, w_down_s]
    partial, rows, gate_s, up_s, hidden_s, *kept = experts(
        all_act, *routing, weights, shared, capacity, tokens
    )
    (routed,) = scatter_ctx([partial.reshape(cycle, tokens, D)], bits, 3)
    result = mixed + routed
    diff = result - teacher[0].astype(f32)
    share = jnp.sum(gather_fsdp(0.5 * jnp.sum(diff * diff, keepdims=True), groups))

    (all_diff,) = gather_ctx([diff.astype(bf16)], bits, 2)
    gates = [item for s in range(groups) for item in kept[3 * s : 3 * s + 2]]
    partial, grad_rows, grad_shared, grad_w_down, *grads = experts_back(
        all_diff.reshape(length, D),
        all_act,
        *routing,
        [gate_s, up_s, hidden_s],
        gates,
        weights,
        shared,
        capacity,
        tokens,
    )
    (grad_act_two,) = scatter_ctx([partial.reshape(cycle, tokens, D)], bits, 3)
    grad_w_down = scatter_fsdp(grad_w_down[:part_s].reshape(groups, -1, D), groups)

    grad_gain_two = jnp.sum(grad_act_two * mixed * factor_two, axis=0)
    grad_mixed = diff + norm_back_rows(mixed, factor_two, gain_two, grad_act_two)
    lefts = []
    for r in range(groups):
        lefts += [grads[2 * r], grads[2 * r + 1], kept[3 * r + 2]]
    all_mixed, *expert_grads = gather_multiply(
        grad_mixed.astype(bf16), rows, grad_rows, lefts, bits, 5
    )
    def by_owner(grad):
        cut = jnp.transpose(grad.reshape(cycle, groups, slab, -1), (1, 0, 2, 3))
        return scatter_fsdp(cut, groups).astype(bf16)

    grad_shared, _ = lax.optimization_barrier((grad_shared, all_mixed))
    grad_shared = by_owner(grad_shared)
    high = lax.reduce_precision(share, 8, 7)
    mid = lax.reduce_precision(share - high, 8, 7)
    loss_parts = jnp.stack([high, mid, share - high - mid]).astype(bf16)
    spot = jnp.arange(grad_shared.shape[2], dtype=jnp.int32) - part_s
    loss_row = sum(jnp.where(spot == i, loss_parts[i], bf16(0)) for i in range(3))
    grad_shared = jnp.where(((spot >= 0) & (spot < 3))[None, None, :], loss_row, grad_shared)
    packed_s = exchange(grad_shared)
    loss_parts = packed_s[:, 0, part_s : part_s + 3].astype(f32)
    loss_value = jnp.sum(loss_parts) / (length * groups * D)
    grad_query, grad_keys, grad_values, grad_w_output = attend_back(
        queries,
        keys,
        values,
        all_mixed.reshape(length, D),
        attended,
        w_output,
        first_pos[None, :],
        log_total.reshape(1, length),
    )
    grad_query, packed_s = lax.optimization_barrier((grad_query, packed_s))
    grad_w_output = own_part(grad_w_output, 0).reshape(groups, slab, D)
    grad_w_output = scatter_fsdp(grad_w_output, groups)
    lanes = jnp.arange(WIDE, dtype=jnp.int32)
    keep_q = (lanes // ((DN + DR) // copies) == copy_index).astype(f32)[None, :]
    keep_e = (lanes // ((DN + DV) // copies) == copy_index).astype(f32)[None, :]
    partial, grad_w_cat, grad_w_expand = project_back(
        grad_query,
        grad_keys,
        grad_values,
        latent_raw,
        latent,
        act_one,
        cosine,
        sine,
        w_cat,
        w_expand,
        gain_latent,
        keep_q,
        keep_e,
        scale,
        copies,
    )
    if fast:
        first, slim = finish(
            grad_w_cat, grad_w_expand, w_cat, w_expand, grad_gain_two[:, None], cycle, slab
        )
    else:
        grad_gain_one = jnp.sum(grad_w_cat * w_cat.astype(f32), axis=1)
        grad_gain_latent = jnp.sum(grad_w_expand * w_expand.astype(f32), axis=1)
        turned = grad_w_cat[:, 2 * DN : 3 * DN]
        grad_ropes = grad_w_cat[:, DN : 2 * DN] - jnp.concatenate(
            [swap(turned[:, :DR]), swap(turned[:, DR:])], axis=1
        )
        grad_w_query = jnp.concatenate([grad_w_cat[:, :DN], grad_ropes[:, :DR]], axis=1)
        grad_we = own_part(grad_w_expand).reshape(cycle * groups, slab_latent, part_e)
        first = jnp.concatenate(
            [own_part(grad_w_query), grad_we.reshape(D, -1)], axis=1
        ).astype(bf16)
        spare = jnp.zeros((cycle * groups, slab - slab_latent), f32)
        grad_gain_latent = jnp.concatenate(
            [grad_gain_latent.reshape(cycle * groups, slab_latent), spare], axis=1
        ).reshape(-1)
        slim = jnp.concatenate(
            [
                grad_w_cat[:, 3 * DN :],
                grad_ropes[:, DR:],
                grad_gain_one[:, None],
                grad_gain_two[:, None],
                grad_gain_latent[:, None],
                jnp.zeros((D, -(KVR + DR + 3) % 128), f32),
            ],
            axis=1,
        ).astype(bf16)

    slim = by_owner(slim)
    first = padded(by_owner(first), block_q)
    packed = exchange(first)
    grad_act_one, grad_narrow = scatter_ctx(
        [partial.reshape(cycle, tokens, D), slim], bits, 4
    )
    if fast:
        own_grads = spread(
            packed,
            packed_s,
            [w.shape[1] for w in (query_weight, expand_weight, shared_gate, shared_up)],
        )
    else:
        spots = (
            (packed, 0, part_q, query_weight),
            (packed, part_q, expand_pieces.shape[2], expand_weight),
            (packed_s, 0, part_s, shared_gate),
            (packed_s, shared_width, part_s, shared_up),
        )
        own_grads = []
        for item, start, width, like in spots:
            item = item[:, :, start : start + width].reshape(cycle, like.shape[0], -1)
            own_grads.append(jnp.transpose(item, (1, 0, 2)).reshape(like.shape).astype(f32))
    _, factor_one = norm_forward(residual, gain_one)
    grad_input = grad_mixed + norm_back_rows(residual, factor_one, gain_one, grad_act_one)
    return (
        result.astype(bf16)[None],
        loss_value,
        grad_input[None],
        grad_narrow[:, KVR + DR] / input_gain.astype(f32),
        own_grads[0],
        grad_narrow[:, : KVR + DR],
        grad_narrow[:slab_latent, KVR + DR + 2] / latent_gain.astype(f32),
        own_grads[1],
        grad_w_output,
        grad_narrow[:, KVR + DR + 1],
        own_grads[2],
        own_grads[3],
        grad_w_down,
        expert_grads[0].astype(f32).T[None],
        expert_grads[1].astype(f32).T[None],
        expert_grads[2].astype(f32)[None],
    )


def solution(mesh):
    tokens = P("fsdp", "ctx", None)
    rows = P(("ctx", "fsdp"), None)
    gain = P(("ctx", "fsdp"))
    wide = P("ctx", None, "fsdp")
    deep = P("ctx", "fsdp", None)
    in_specs = (
        tokens,
        tokens,
        P("fsdp", None),
        tokens,
        tokens,
        gain,
        rows,
        rows,
        gain,
        rows,
        rows,
        gain,
        rows,
        rows,
        rows,
        wide,
        wide,
        deep,
    )
    out_specs = (
        tokens,
        P(),
        tokens,
        gain,
        rows,
        rows,
        gain,
        rows,
        rows,
        gain,
        rows,
        rows,
        rows,
        wide,
        wide,
        deep,
    )
    return jax.shard_map(shards, mesh=mesh, in_specs=in_specs, out_specs=out_specs, check_vma=False)
```

```python
import functools
import math

import jax
import jax.numpy as jnp
from jax import lax
from jax.experimental import pallas as pl
from jax.experimental.pallas import tpu as pltpu
from jax.sharding import PartitionSpec as P

D = 2048
H = 16
DN = 128
DR = 64
DV = 128
KVR = 512
TOPK = 6
WIDE = 256

EPS = 1e-06
NEG = -1e30
MESH = pl.DeviceIdType.MESH
f32 = jnp.float32
bf16 = jnp.bfloat16


def norm_forward(rows, gain):
    factor = lax.rsqrt(jnp.mean(rows * rows, axis=-1, keepdims=True) + EPS)
    return (rows * factor * gain, factor)


def norm_back_rows(rows, factor, gain, grad_out):
    scaled = grad_out * gain
    normed = rows * factor
    return factor * (scaled - normed * jnp.mean(scaled * normed, axis=-1, keepdims=True))


def rotate(values, cosine, sine):
    half = values.shape[-1] // 2
    first = values[..., :half]
    second = values[..., half:]
    return jnp.concatenate(
        [first * cosine - second * sine, second * cosine + first * sine], axis=-1
    )


def rope_tables(offsets):
    freqs = 10000.0 ** (-(jnp.arange(DR // 2, dtype=f32) * 2.0) / DR)
    angle = offsets.astype(f32)[:, None] * freqs[None, :]
    return (jnp.cos(angle), jnp.sin(angle))


def silu_grads(gate_val, up_val, grad_hidden):
    sigma = jax.nn.sigmoid(gate_val)
    grad_gate = grad_hidden * up_val * sigma * (1.0 + gate_val * (1.0 - sigma))
    grad_up = grad_hidden * gate_val * sigma
    return (grad_gate.astype(bf16), grad_up.astype(bf16))


def dot(left, right):
    return jnp.dot(left, right, preferred_element_type=f32)


def dot_first(left, right):
    return lax.dot_general(left, right, (((0,), (0,)), ((), ())), preferred_element_type=f32)


def dot_last(left, right):
    return lax.dot_general(left, right, (((1,), (1,)), ((), ())), preferred_element_type=f32)


def flip(me, mask):
    out = me
    bit = 1
    while bit <= mask:
        if mask & bit:
            out = out + bit * (1 - 2 * ((me // bit) % 2))
        bit *= 2
    return out


def row_parts(rows, bits):
    low, high = [1, 2], [1 << k for k in range(bits - 1, 1, -1)]
    orders = (high + low, high + low[::-1], low + high)
    units = rows // 16
    if units < 3:
        return ((0, rows, tuple(orders[0])),)
    third = max(1, units // 4)
    first = (units - third) // 2
    counts = (first * 16, (units - third - first) * 16, third * 16)
    parts, start = [], 0
    for count, order in zip(counts, orders):
        parts.append((start, count, tuple(order)))
        start += count
    return tuple(parts)


def all_parts(shapes, bits):
    return tuple(
        (a,) + part for a, shape in enumerate(shapes) for part in row_parts(shape[-2], bits)
    )


def greet(bits):
    me = lax.axis_index("ctx")
    barrier = pltpu.get_barrier_semaphore()
    for k in range(bits):
        pl.semaphore_signal(
            barrier, inc=1, device_id={"ctx": flip(me, 1 << k)}, device_id_type=MESH
        )
    pl.semaphore_wait(barrier, bits)


def gather_events(parts, bits):
    events = []
    for p, (_, _, _, order) in enumerate(parts):
        for slot in range(1 << bits):
            hops = [k for k, b in enumerate(order) if slot & b]
            for k in range(hops[-1] + 1 if hops else 0, bits):
                events.append((len(hops), k, p, slot, order[k]))
    return tuple(sorted(events))


def gather_kernel(parts, bits, events, count, *refs):
    x_refs, o_refs = refs[:count], refs[count : 2 * count]
    send_sem, recv_sem, own_sem = refs[2 * count :]
    me = lax.axis_index("ctx")
    own = [
        pltpu.make_async_copy(x_refs[a], o_refs[a].at[me], own_sem.at[a]) for a in range(count)
    ]
    for item in own:
        item.start()
    greet(bits)

    def copy(p, slot, bit, index):
        a, start, size, _ = parts[p]
        rows = pl.ds(start, size)
        block = flip(me, slot)
        return pltpu.make_async_remote_copy(
            src_ref=x_refs[a].at[rows] if slot == 0 else o_refs[a].at[block, rows],
            dst_ref=o_refs[a].at[block, rows],
            send_sem=send_sem.at[index],
            recv_sem=recv_sem.at[p, slot ^ bit],
            device_id={"ctx": flip(me, bit)},
            device_id_type=MESH,
        )

    def arrived(p, slot):
        a, start, size, order = parts[p]
        rows = pl.ds(start, size)
        bit = [b for b in order if slot & b][-1]
        pltpu.make_async_remote_copy(
            src_ref=x_refs[a].at[rows],
            dst_ref=o_refs[a].at[flip(me, slot), rows],
            send_sem=send_sem.at[0],
            recv_sem=recv_sem.at[p, slot],
            device_id={"ctx": flip(me, bit)},
            device_id_type=MESH,
        ).wait_recv()

    seen = set()
    started = []
    for index, (_, _, p, slot, bit) in enumerate(events):
        if slot and (p, slot) not in seen:
            arrived(p, slot)
            seen.add((p, slot))
        sent = copy(p, slot, bit, index)
        sent.start()
        started.append(sent)
    for p in range(len(parts)):
        for slot in range(1, 1 << bits):
            if (p, slot) not in seen:
                arrived(p, slot)
    for sent in started:
        sent.wait_send()
    for item in own:
        item.wait()


def gather_ctx(arrays, bits, collective):
    parts = all_parts([item.shape for item in arrays], bits)
    events = gather_events(parts, bits)
    count = len(arrays)
    return pl.pallas_call(
        functools.partial(gather_kernel, parts, bits, events, count),
        name="gather_ctx",
        out_shape=[jax.ShapeDtypeStruct((1 << bits,) + item.shape, item.dtype) for item in arrays],
        in_specs=[pl.BlockSpec(memory_space=pl.ANY)] * count,
        out_specs=[pl.BlockSpec(memory_space=pl.ANY)] * count,
        scratch_shapes=[
            pltpu.SemaphoreType.DMA((len(events),)),
            pltpu.SemaphoreType.DMA((len(parts), 1 << bits)),
            pltpu.SemaphoreType.DMA((count,)),
        ],
        compiler_params=pltpu.CompilerParams(collective_id=collective, has_side_effects=True),
    )(*arrays)


def gather_multiply_kernel(
    parts, bits, events, shares, tile, x_ref, rows_ref, dy_ref, *refs
):
    lefts, refs = refs[: 3 * shares], refs[3 * shares :]
    o_ref, outs, refs = refs[0], refs[1:4], refs[4:]
    rows, dy, left, sent, got, stage = refs[:6]
    send_sem, recv_sem, own_sem, load_sem, out_sem, far_sem, near_sem = refs[6:]
    me, place = lax.axis_index("ctx"), lax.axis_index("fsdp")
    half, width = left.shape[2], rows.shape[1]
    tiles = width // tile
    loads = [pltpu.make_async_copy(rows_ref, rows, load_sem.at[3 * shares])]
    loads.append(pltpu.make_async_copy(dy_ref, dy, load_sem.at[3 * shares + 1]))
    order = list(range(3, 3 * shares)) + [0, 1, 2]
    for i in range(3 * shares):
        loads.append(pltpu.make_async_copy(lefts[i], left.at[i], load_sem.at[i]))
    own = pltpu.make_async_copy(x_ref, o_ref.at[me], own_sem)
    own.start()
    barrier = pltpu.get_barrier_semaphore()
    for k in range(bits):
        pl.semaphore_signal(
            barrier, inc=1, device_id={"ctx": flip(me, 1 << k)}, device_id_type=MESH
        )
    for r in range(1, shares):
        pl.semaphore_signal(
            barrier, inc=1, device_id={"fsdp": (place + r) % shares}, device_id_type=MESH
        )
    pl.semaphore_wait(barrier, bits + shares - 1)
    for i in [0, 2 + 3 % (3 * shares), 1] if shares > 1 else [0, 2, 1]:
        loads[i].start()
    for i in range(2, len(loads)):
        if i != 2 + 3 % (3 * shares):
            loads[i].start()
    ready = set()

    def need(i):
        if i not in ready:
            loads[i].wait()
            ready.add(i)

    def copy(p, slot, bit, index):
        _, start, size, _ = parts[p]
        part = pl.ds(start, size)
        block = flip(me, slot)
        return pltpu.make_async_remote_copy(
            src_ref=x_ref.at[part] if slot == 0 else o_ref.at[block, part],
            dst_ref=o_ref.at[block, part],
            send_sem=send_sem.at[index],
            recv_sem=recv_sem.at[p, slot ^ bit],
            device_id={"ctx": flip(me, bit)},
            device_id_type=MESH,
        )

    def arrived(p, slot):
        _, start, size, path = parts[p]
        part = pl.ds(start, size)
        bit = [b for b in path if slot & b][-1]
        pltpu.make_async_remote_copy(
            src_ref=x_ref.at[part],
            dst_ref=o_ref.at[flip(me, slot), part],
            send_sem=send_sem.at[0],
            recv_sem=recv_sem.at[p, slot],
            device_id={"ctx": flip(me, bit)},
            device_id_type=MESH,
        ).wait_recv()

    def far(i, t):
        spot = (i - 3, slice(None), pl.ds(t * tile, tile))
        return pltpu.make_async_remote_copy(
            src_ref=sent.at[spot],
            dst_ref=got.at[spot],
            send_sem=far_sem.at[i - 3, t],
            recv_sem=near_sem.at[i - 3, t],
            device_id={"fsdp": (place + shares - i // 3) % shares},
            device_id_type=MESH,
        )

    def store(i, t):
        buffer = (i * tiles + t) % 2
        return pltpu.make_async_copy(
            stage.at[buffer], outs[i].at[:, pl.ds(t * tile, tile)], out_sem.at[i, t]
        )

    def multiply(i, t):
        need(2 + i)
        need(1 if i % 3 == 2 else 0)
        right = dy if i % 3 == 2 else rows
        total = dot_first(left[i], right[:, t * tile : (t + 1) * tile])
        if i >= 3:
            sent[i - 3, :, t * tile : (t + 1) * tile] = total.astype(bf16)
            far(i, t).start()
            return
        for r in range(1, shares):
            far(i + 3 * r, t).wait_recv()
            total = total + got[i + 3 * r - 3, :, t * tile : (t + 1) * tile].astype(f32)
        last = i * tiles + t - 2
        if last >= 0:
            store(last // tiles, last % tiles).wait()
        stage[(i * tiles + t) % 2] = total.astype(bf16)
        store(i, t).start()

    work = [(i, t) for i in order for t in range(tiles)]
    done = 0
    seen = set()
    started = []
    for index, (_, _, p, slot, bit) in enumerate(events):
        if slot and (p, slot) not in seen:
            arrived(p, slot)
            seen.add((p, slot))
        item = copy(p, slot, bit, index)
        item.start()
        started.append(item)
        first = bits * len(parts)
        if index >= first:
            while done < len(work) * (index - first + 1) // (len(events) - first):
                multiply(*work[done])
                done += 1
    for p in range(len(parts)):
        for slot in range(1, 1 << bits):
            if (p, slot) not in seen:
                arrived(p, slot)
    for item in started:
        item.wait_send()
    own.wait()
    for i in range(3, 3 * shares):
        for t in range(tiles):
            far(i, t).wait_send()
    for last in range(max(0, 3 * tiles - 2), 3 * tiles):
        store(last // tiles, last % tiles).wait()


def gather_multiply(x, rows, dy, lefts, bits, collective):
    parts = all_parts([x.shape], bits)
    events = gather_events(parts, bits)
    shares = len(lefts) // 3
    count, half = lefts[0].shape
    width = rows.shape[1]
    tile = width // 2
    anywhere = pl.BlockSpec(memory_space=pl.ANY)
    others = max(1, 3 * shares - 3)
    return pl.pallas_call(
        functools.partial(gather_multiply_kernel, parts, bits, events, shares, tile),
        name="gather_multiply",
        out_shape=[jax.ShapeDtypeStruct((1 << bits,) + x.shape, x.dtype)]
        + [jax.ShapeDtypeStruct((half, width), bf16)] * 3,
        in_specs=[anywhere] * (3 + 3 * shares),
        out_specs=[anywhere] * 4,
        scratch_shapes=[
            pltpu.VMEM((count, width), bf16),
            pltpu.VMEM((count, width), bf16),
            pltpu.VMEM((3 * shares, count, half), bf16),
            pltpu.VMEM((others, half, width), bf16),
            pltpu.VMEM((others, half, width), bf16),
            pltpu.VMEM((2, half, tile), bf16),
            pltpu.SemaphoreType.DMA((len(events),)),
            pltpu.SemaphoreType.DMA((len(parts), 1 << bits)),
            pltpu.SemaphoreType.DMA,
            pltpu.SemaphoreType.DMA((3 * shares + 2,)),
            pltpu.SemaphoreType.DMA((3, width // tile)),
            pltpu.SemaphoreType.DMA((others, width // tile)),
            pltpu.SemaphoreType.DMA((others, width // tile)),
        ],
        compiler_params=pltpu.CompilerParams(
            collective_id=collective, has_side_effects=True, vmem_limit_bytes=60 << 20
        ),
    )(x, rows, dy, *lefts)


def scatter_events(parts, bits):
    events = []
    for p, (_, _, _, order) in enumerate(parts):
        for slot in range(1, 1 << bits):
            k = [i for i, b in enumerate(order) if slot & b][0]
            later = tuple(-int(bool(slot & b)) for b in order[k + 1 :])
            events.append((k, later, p, slot))
    return tuple((k, p, slot) for k, _, p, slot in sorted(events))


def scatter_kernel(parts, bits, events, count, *refs):
    x_refs, o_refs = refs[:count], refs[count : 2 * count]
    recvs, sends, owns = (refs[(2 + i) * count : (3 + i) * count] for i in range(3))
    send_sem, recv_sem, own_sem = refs[5 * count :]
    me = lax.axis_index("ctx")
    later = [sorted({s for k, p, s in events if k and parts[p][0] == a}) for a in range(count)]

    def load(a, slot):
        place = later[a].index(slot) + 1 if slot else 0
        return pltpu.make_async_copy(
            x_refs[a].at[flip(me, slot)], owns[a].at[place], own_sem.at[a, place]
        )

    greet(bits)

    def copy(p, slot, k, src):
        a, start, size, order = parts[p]
        return pltpu.make_async_remote_copy(
            src_ref=src,
            dst_ref=recvs[a].at[slot - 1, pl.ds(start, size)],
            send_sem=send_sem.at[p, slot - 1],
            recv_sem=recv_sem.at[p, slot - 1],
            device_id={"ctx": flip(me, order[k])},
            device_id_type=MESH,
        )

    loaded = set()

    def add_up(p, slot, k):
        a, start, size, order = parts[p]
        place = later[a].index(slot) + 1 if slot else 0
        if (a, slot) not in loaded:
            load(a, slot).wait()
            loaded.add((a, slot))
        for e in range(k):
            other = slot | order[e]
            copy(p, other, e, recvs[a].at[other - 1, pl.ds(start, size)]).wait_recv()
        target = sends[a].at[place - 1] if slot else o_refs[a]

        @pl.loop(0, size // 16)
        def _(t):
            part = pl.ds(pl.multiple_of(start + t * 16, 16), 16)
            total = owns[a][place, part].astype(f32)
            for e in range(k):
                total = total + recvs[a][(slot | order[e]) - 1, part].astype(f32)
            target[part] = total.astype(target.dtype)

    started = []
    first = [event for event in events if event[0] == 0]
    for index, (k, p, slot) in enumerate(events):
        a, start, size, order = parts[p]
        rows = pl.ds(start, size)
        if k == 0:
            src = x_refs[a].at[flip(me, slot), rows]
        else:
            add_up(p, slot, k)
            src = sends[a].at[later[a].index(slot), rows]
        sent = copy(p, slot, k, src)
        sent.start()
        started.append(sent)
        if index == len(first) // 2:
            for a in range(count):
                for own in [0] + later[a]:
                    load(a, own).start()
    for p in range(len(parts)):
        add_up(p, 0, bits)
    for sent in started:
        sent.wait_send()


def scatter_ctx(arrays, bits, collective):
    shapes = [item.shape[1:] for item in arrays]
    parts = all_parts(shapes, bits)
    parts = tuple((a, start, size, order[::-1]) for a, start, size, order in parts)
    events = scatter_events(parts, bits)
    count = len(arrays)
    others = (1 << bits) - 1
    held = [
        1 + len({s for k, p, s in events if k and parts[p][0] == a}) for a in range(count)
    ]
    return pl.pallas_call(
        functools.partial(scatter_kernel, parts, bits, events, count),
        name="scatter_ctx",
        out_shape=[jax.ShapeDtypeStruct(shape, f32) for shape in shapes],
        in_specs=[pl.BlockSpec(memory_space=pl.ANY)] * count,
        out_specs=[pl.BlockSpec(memory_space=pltpu.VMEM)] * count,
        scratch_shapes=[pltpu.VMEM((others,) + shape, bf16) for shape in shapes]
        + [pltpu.VMEM((n - 1,) + shape, bf16) for n, shape in zip(held, shapes)]
        + [pltpu.VMEM((n,) + shape, bf16) for n, shape in zip(held, shapes)]
        + [
            pltpu.SemaphoreType.DMA((len(parts), others)),
            pltpu.SemaphoreType.DMA((len(parts), others)),
            pltpu.SemaphoreType.DMA((count, max(held))),
        ],
        compiler_params=pltpu.CompilerParams(
            collective_id=collective, has_side_effects=True, vmem_limit_bytes=58 << 20
        ),
    )(*arrays)


def attend_kernel(block, count, q_ref, k_ref, v_ref, first_ref, wo_ref, o_ref, log_ref, part_ref):
    step = pl.program_id(0)
    for i in range(count):

        @pl.when(step == i)
        def _(i=i):
            extent = (i + 1) * block
            scores = dot_last(q_ref[...], k_ref[:extent, :])
            key_pos = lax.broadcasted_iota(jnp.int32, (block, extent), 1)
            query_pos = i * block + lax.broadcasted_iota(jnp.int32, (block, extent), 0)
            allowed = (key_pos >= first_ref[...]) & (key_pos <= query_pos)
            scores = jnp.where(allowed, scores, NEG)
            top = jnp.max(scores, axis=-1, keepdims=True)
            weights = jnp.exp(scores - top)
            total = jnp.sum(weights, axis=-1, keepdims=True)
            summed = dot(weights.astype(bf16), v_ref[:extent, :])
            o_ref[...] = summed / total
            log_ref[...] = top + jnp.log(total)
            part_ref[...] = dot((summed / total).astype(bf16), wo_ref[...]).astype(bf16)


def attend(queries, keys, values, first, w_output):
    length = queries.shape[0]
    block = min(256, length)
    count = length // block
    return pl.pallas_call(
        functools.partial(attend_kernel, block, count),
        name="attend",
        grid=(count,),
        out_shape=(
            jax.ShapeDtypeStruct((length, DV), f32),
            jax.ShapeDtypeStruct((length, 1), f32),
            jax.ShapeDtypeStruct((length, D), bf16),
        ),
        in_specs=[
            pl.BlockSpec((block, WIDE), lambda i: (i, 0)),
            pl.BlockSpec((length, WIDE), lambda i: (0, 0)),
            pl.BlockSpec((length, DV), lambda i: (0, 0)),
            pl.BlockSpec((block, 1), lambda i: (i, 0)),
            pl.BlockSpec((DV, D), lambda i: (0, 0)),
        ],
        out_specs=(
            pl.BlockSpec((block, DV), lambda i: (i, 0)),
            pl.BlockSpec((block, 1), lambda i: (i, 0)),
            pl.BlockSpec((block, D), lambda i: (i, 0)),
        ),
        compiler_params=pltpu.CompilerParams(vmem_limit_bytes=60 << 20),
        cost_estimate=pl.CostEstimate(
            flops=length * length * (DN + DR + DV),
            bytes_accessed=length * 2000,
            transcendentals=length * length // 2,
        ),
    )(queries, keys, values, first, w_output)


def attend_back_kernel(
    block, count, q_ref, k_ref, v_ref, m_ref, att_ref, wo_ref, first_ref, log_ref,
    dq_ref, dk_ref, dv_ref, gwo_ref,
):
    step = pl.program_id(0)

    @pl.when(step == 0)
    def _():
        dk_ref[...] = jnp.zeros_like(dk_ref)
        dv_ref[...] = jnp.zeros_like(dv_ref)
        gwo_ref[...] = jnp.zeros_like(gwo_ref)

    grad = dot_last(m_ref[...], wo_ref[...]).astype(bf16)
    gwo_ref[...] += dot_first(att_ref[...].astype(bf16), m_ref[...])
    delta = jnp.sum((grad.astype(f32) * att_ref[...]).T, axis=0, keepdims=True)
    for i in range(count):

        @pl.when(step == i)
        def _(i=i):
            extent = (i + 1) * block
            keys = k_ref[:extent, :]
            scores = dot_last(keys, q_ref[...])
            key_pos = lax.broadcasted_iota(jnp.int32, (extent, block), 0)
            query_pos = i * block + lax.broadcasted_iota(jnp.int32, (extent, block), 1)
            allowed = (key_pos >= first_ref[...]) & (key_pos <= query_pos)
            weights = jnp.where(allowed, jnp.exp(scores - log_ref[...]), 0.0)
            grad_weights = dot_last(v_ref[:extent, :], grad)
            grad_scores = (weights * (grad_weights - delta)).astype(bf16)
            dv_ref[:extent, :] += dot(weights.astype(bf16), grad)
            dk_ref[:extent, :] += dot(grad_scores, q_ref[...])
            dq_ref[...] = dot_first(grad_scores, keys)


def attend_back(queries, keys, values, grad_mixed, attended, w_output, first, log_total):
    length = queries.shape[0]
    block = min(256, length)
    count = length // block
    row = lambda: pl.BlockSpec((1, block), lambda i: (0, i))
    whole = lambda height, width: pl.BlockSpec((height, width), lambda i: (0, 0))
    part = lambda width: pl.BlockSpec((block, width), lambda i: (i, 0))
    return pl.pallas_call(
        functools.partial(attend_back_kernel, block, count),
        name="attend_back",
        grid=(count,),
        out_shape=(
            jax.ShapeDtypeStruct((length, WIDE), f32),
            jax.ShapeDtypeStruct((length, WIDE), f32),
            jax.ShapeDtypeStruct((length, DV), f32),
            jax.ShapeDtypeStruct((DV, D), f32),
        ),
        in_specs=[
            part(WIDE),
            whole(length, WIDE),
            whole(length, DV),
            part(D),
            part(DV),
            whole(DV, D),
            row(),
            row(),
        ],
        out_specs=(part(WIDE), whole(length, WIDE), whole(length, DV), whole(DV, D)),
        compiler_params=pltpu.CompilerParams(vmem_limit_bytes=60 << 20),
        cost_estimate=pl.CostEstimate(
            flops=length * length * (3 * (DN + DR) + 2 * DV),
            bytes_accessed=length * 4000,
            transcendentals=length * length // 2,
        ),
    )(queries, keys, values, grad_mixed, attended, w_output, first, log_total)


def lanes_of(value):
    return lax.broadcasted_iota(jnp.int32, value.shape, len(value.shape) - 1)


def swap_lanes(ropes):
    return jnp.where(
        lanes_of(ropes) % DR < DR // 2, -pltpu.roll(ropes, 96, 1), pltpu.roll(ropes, 32, 1)
    )


def assemble_kernel(
    cycle, slab, mine_ref, other_ref, mine_n_ref, other_n_ref,
    w_ref, we_ref, gains_ref, narrow_ref, expand_ref,
):
    me = lax.axis_index("fsdp")
    for f, (pack_ref, slim_ref) in enumerate(((mine_ref, mine_n_ref), (other_ref, other_n_ref))):
        owner = me if f == 0 else 1 - me

        @pl.loop(0, cycle)
        def _(c):
            rows = pl.ds(pl.multiple_of((c * 2 + owner) * slab, slab), slab)
            w_ref[rows, :DN] = pack_ref[c, :, :DN]
            w_ref[rows, 3 * DN :] = slim_ref[c, :, :KVR]
            tail = pack_ref[c, :, DN:256].astype(f32)
            slim = slim_ref[c, :, KVR:].astype(f32)
            ropes = jnp.where(lanes_of(tail) < DR, tail, pltpu.roll(slim, DR, 1))
            w_ref[rows, DN : 2 * DN] = ropes.astype(bf16)
            w_ref[rows, 2 * DN : 3 * DN] = swap_lanes(ropes).astype(bf16)
            narrow_ref[rows, :] = slim
            quarter = slab // 4
            for q in range(2):
                left = tail[2 * q * quarter : (2 * q + 1) * quarter]
                right = tail[(2 * q + 1) * quarter : (2 * q + 2) * quarter]
                both = jnp.where(lanes_of(left) < DR, pltpu.roll(left, DR, 1), right)
                spot = pl.ds(pl.multiple_of((c * 2 + owner) * quarter, quarter), quarter)
                expand_ref[spot, q * DN : (q + 1) * DN] = both

    we_ref[...] = expand_ref[...].astype(bf16)
    gains_ref[...] = narrow_ref[...].T[DR : DR + 8, :]


def assemble(mine, other, mine_n, other_n):
    cycle, slab, _ = mine.shape
    return pl.pallas_call(
        functools.partial(assemble_kernel, cycle, slab),
        name="assemble",
        out_shape=(
            jax.ShapeDtypeStruct((D, 3 * DN + KVR), bf16),
            jax.ShapeDtypeStruct((KVR, DN + DV), bf16),
            jax.ShapeDtypeStruct((8, D), f32),
        ),
        scratch_shapes=[pltpu.VMEM((D, DN), f32), pltpu.VMEM((KVR, DN + DV), f32)],
        compiler_params=pltpu.CompilerParams(vmem_limit_bytes=60 << 20),
    )(mine, other, mine_n, other_n)


def finish_kernel(cycle, slab, gw_ref, gwe_ref, w_ref, we_ref, extra_ref, first_ref, slim_ref):
    quarter = slab // 4
    turned = gw_ref[:, 2 * DN : 3 * DN]
    ropes = gw_ref[:, DN : 2 * DN] - swap_lanes(turned)
    gain_one = jnp.sum(gw_ref[...] * w_ref[...].astype(f32), axis=1, keepdims=True)
    gain_latent = jnp.sum(gwe_ref[...] * we_ref[...].astype(f32), axis=1, keepdims=True)
    lanes = lanes_of(ropes)
    first_ref[:, :DN] = gw_ref[:, :DN].astype(bf16)
    slim_ref[:, :KVR] = gw_ref[:, 3 * DN :].astype(bf16)
    tail = jnp.where(lanes < DR, pltpu.roll(ropes, DR, 1), 0.0)
    tail = jnp.where(lanes == DR, gain_one, tail)
    tail = jnp.where(lanes == DR + 1, extra_ref[...], tail)
    for part in range(cycle * 2):
        rows = slice(part * slab, (part + 1) * slab)
        some = slice(part * quarter, (part + 1) * quarter)
        expand = gwe_ref[some, :]
        pieces = [
            pltpu.roll(expand[:, :DN], DR, 1),
            expand[:, :DN],
            pltpu.roll(expand[:, DN:], DR, 1),
            expand[:, DN:],
        ]
        pieces = jnp.concatenate(pieces, axis=0)
        first_ref[rows, DN:] = jnp.where(lanes[rows] < DR, ropes[rows], pieces).astype(bf16)
        column = jnp.concatenate(
            [gain_latent[some], jnp.zeros((slab - quarter, 1), f32)], axis=0
        )
        slim_ref[rows, KVR:] = jnp.where(lanes[rows] == DR + 2, column, tail[rows]).astype(bf16)


def finish(grad_w, grad_we, w_cat, w_expand, extra, cycle, slab):
    return pl.pallas_call(
        functools.partial(finish_kernel, cycle, slab),
        name="finish",
        out_shape=(
            jax.ShapeDtypeStruct((D, 256), bf16),
            jax.ShapeDtypeStruct((D, KVR + DN), bf16),
        ),
        compiler_params=pltpu.CompilerParams(vmem_limit_bytes=60 << 20),
    )(grad_w, grad_we, w_cat, w_expand, extra)


def place_lanes(out_ref, pieces, width):
    total = width * len(pieces)
    for start in range(0, total, DN):
        tile = None
        for c in range(start // width, min(len(pieces), -(-(start + DN) // width))):
            moved = pieces[c]
            shift = (c * width - start) % 256
            if shift:
                moved = pltpu.roll(moved, shift, 1)
            moved = moved[:, :DN]
            lanes = lanes_of(moved) + start
            inside = (lanes >= c * width) & (lanes < (c + 1) * width)
            tile = jnp.where(inside, moved, 0.0 if tile is None else tile)
        out_ref[:, start : start + DN] = tile


def spread_kernel(cycle, slab, pack_ref, pack_s_ref, gq_ref, gwe_ref, gg_ref, gu_ref):
    quarter = slab // 4
    for ref, out_ref, start in (
        (pack_ref, gq_ref, 0),
        (pack_s_ref, gg_ref, 0),
        (pack_s_ref, gu_ref, 256),
    ):
        pieces = [ref[c, :, start : start + 256].astype(f32) for c in range(cycle)]
        place_lanes(out_ref, pieces, out_ref.shape[1] // cycle)
    for c in range(cycle):
        tail = pack_ref[c, :, DN:256].astype(f32)
        for q in range(2):
            left = tail[2 * q * quarter : (2 * q + 1) * quarter]
            right = tail[(2 * q + 1) * quarter : (2 * q + 2) * quarter]
            both = jnp.where(lanes_of(left) < DR, pltpu.roll(left, DR, 1), right)
            at = c * 2 * DN + q * DN
            gwe_ref[:, at : at + DN] = both


def spread(packed, packed_s, widths):
    cycle, slab, _ = packed.shape
    return pl.pallas_call(
        functools.partial(spread_kernel, cycle, slab),
        name="spread",
        out_shape=(
            jax.ShapeDtypeStruct((slab, widths[0]), f32),
            jax.ShapeDtypeStruct((slab // 4, widths[1]), f32),
            jax.ShapeDtypeStruct((slab, widths[2]), f32),
            jax.ShapeDtypeStruct((slab, widths[3]), f32),
        ),
        compiler_params=pltpu.CompilerParams(vmem_limit_bytes=60 << 20),
    )(packed, packed_s)


def fixed(shape):
    return pl.BlockSpec(shape, lambda i: (0,) * len(shape), pipeline_mode=pl.Buffered(1))


def second(shape):
    return pl.BlockSpec(shape, lambda i: (0, 1), pipeline_mode=pl.Buffered(1))


def by_rows(rows, cols):
    return pl.BlockSpec((rows, cols), lambda i: (i, 0))


def project_kernel(
    scale, x_ref, gain_ref, w_ref, gain_l_ref, we_ref, cos_ref, sin_ref,
    act_ref, q_ref, k_ref, v_ref, latent_ref, raw_ref,
):
    act = norm_forward(x_ref[...].astype(f32), gain_ref[...])[0].astype(bf16)
    act_ref[...] = act
    raw = dot(act, w_ref[...])
    turned = raw[:, DN : 2 * DN] * cos_ref[...] + raw[:, 2 * DN : 3 * DN] * sin_ref[...]
    low = lax.broadcasted_iota(jnp.int32, turned.shape, 1) < DR
    q_ref[:, :DN] = (raw[:, :DN] * scale).astype(bf16)
    q_ref[:, DN:] = jnp.where(low, turned * scale, 0.0).astype(bf16)
    raw_latent = raw[:, 3 * DN :]
    raw_ref[...] = raw_latent
    latent = norm_forward(raw_latent, gain_l_ref[...])[0].astype(bf16)
    latent_ref[...] = latent
    expanded = dot(latent, we_ref[...]).astype(bf16)
    k_ref[:, :DN] = expanded[:, :DN]
    k_ref[:, DN:] = jnp.where(low, pltpu.roll(turned, DR, 1), 0.0).astype(bf16)
    v_ref[...] = expanded[:, DN:]


def project(x, gain, w_cat, gain_latent, w_expand, cosine, sine, scale):
    length = x.shape[0]
    block = min(256, length)
    width = w_cat.shape[1]
    return pl.pallas_call(
        functools.partial(project_kernel, scale),
        name="project",
        grid=(length // block,),
        out_shape=(
            jax.ShapeDtypeStruct((length, D), bf16),
            jax.ShapeDtypeStruct((length, WIDE), bf16),
            jax.ShapeDtypeStruct((length, WIDE), bf16),
            jax.ShapeDtypeStruct((length, DV), bf16),
            jax.ShapeDtypeStruct((length, KVR), bf16),
            jax.ShapeDtypeStruct((length, KVR), f32),
        ),
        in_specs=[
            by_rows(block, D),
            fixed((1, D)),
            fixed((D, width)),
            fixed((1, KVR)),
            fixed((KVR, DN + DV)),
            by_rows(block, DN),
            by_rows(block, DN),
        ],
        out_specs=(
            by_rows(block, D),
            by_rows(block, WIDE),
            by_rows(block, WIDE),
            by_rows(block, DV),
            by_rows(block, KVR),
            by_rows(block, KVR),
        ),
        compiler_params=pltpu.CompilerParams(vmem_limit_bytes=60 << 20),
        cost_estimate=pl.CostEstimate(
            flops=2 * length * D * width, bytes_accessed=length * D * 6, transcendentals=0
        ),
    )(x, gain[None, :], w_cat, gain_latent[None, :], w_expand, cosine, sine)


def project_back_kernel(
    scale, copies, dq_ref, dk_ref, dv_ref, raw_ref, latent_ref, act_ref, cos_ref, sin_ref,
    w_ref, we_ref, gain_l_ref, keep_q_ref, keep_e_ref, part_ref, gw_ref, gwe_ref,
):
    @pl.when(pl.program_id(0) == 0)
    def _():
        gw_ref[...] = jnp.zeros_like(gw_ref)
        gwe_ref[...] = jnp.zeros_like(gwe_ref)

    grad_q = dq_ref[...] * scale
    grad_k = dk_ref[:, :DN]
    grad_v = dv_ref[...]
    if copies > 1:
        grad_q = grad_q * keep_q_ref[...]
        grad_k = grad_k * keep_e_ref[:, :DN]
        grad_v = grad_v * keep_e_ref[:, DN:]
    rope_q = grad_q[:, DN:]
    low = lax.broadcasted_iota(jnp.int32, rope_q.shape, 1) < DR
    rope_k = jnp.where(low, dk_ref[:, DN:] * (1.0 / copies), 0.0)
    ropes = jnp.where(low, rope_q, pltpu.roll(rope_k, DR, 1))
    expanded = jnp.concatenate([grad_k, grad_v], axis=-1).astype(bf16)
    grad_latent = dot_last(expanded, we_ref[...])
    raw = raw_ref[...]
    factor = lax.rsqrt(jnp.mean(raw * raw, axis=-1, keepdims=True) + EPS)
    grad_latent = norm_back_rows(raw, factor, gain_l_ref[...], grad_latent)
    grads = jnp.concatenate(
        [
            grad_q[:, :DN].astype(bf16),
            (ropes * cos_ref[...]).astype(bf16),
            (ropes * sin_ref[...]).astype(bf16),
            grad_latent.astype(bf16),
        ],
        axis=-1,
    )
    part_ref[...] = dot_last(grads, w_ref[...]).astype(bf16)
    gw_ref[...] += dot_first(act_ref[...], grads)
    gwe_ref[...] += dot_first(latent_ref[...], expanded)


def project_back(
    grad_q, grad_k, grad_v, raw, latent, act, cosine, sine, w_cat, w_expand, gain_latent, keep_q,
    keep_e, scale, copies,
):
    length = act.shape[0]
    block = min(256, length)
    width = w_cat.shape[1]
    return pl.pallas_call(
        functools.partial(project_back_kernel, scale, copies),
        name="project_back",
        grid=(length // block,),
        out_shape=(
            jax.ShapeDtypeStruct((length, D), bf16),
            jax.ShapeDtypeStruct((D, width), f32),
            jax.ShapeDtypeStruct((KVR, DN + DV), f32),
        ),
        in_specs=[
            by_rows(block, WIDE),
            by_rows(block, WIDE),
            by_rows(block, DV),
            by_rows(block, KVR),
            by_rows(block, KVR),
            by_rows(block, D),
            by_rows(block, DN),
            by_rows(block, DN),
            fixed((D, width)),
            fixed((KVR, DN + DV)),
            fixed((1, KVR)),
            fixed((1, WIDE)),
            fixed((1, DN + DV)),
        ],
        out_specs=(
            by_rows(block, D),
            pl.BlockSpec((D, width), lambda i: (0, 0)),
            pl.BlockSpec((KVR, DN + DV), lambda i: (0, 0)),
        ),
        compiler_params=pltpu.CompilerParams(vmem_limit_bytes=60 << 20),
        cost_estimate=pl.CostEstimate(
            flops=4 * length * D * width, bytes_accessed=length * D * 6, transcendentals=0
        ),
    )(
        grad_q, grad_k, grad_v, raw, latent, act, cosine, sine, w_cat, w_expand,
        gain_latent[None, :], keep_q, keep_e,
    )


class Gather:
    def __init__(self, parts, bits, events, x_ref, o_ref, send_sem, recv_sem, own_sem):
        self.parts, self.bits, self.events = parts, bits, events
        self.x_ref, self.o_ref = x_ref, o_ref
        self.send_sem, self.recv_sem = send_sem, recv_sem
        self.me = lax.axis_index("ctx")
        self.own = pltpu.make_async_copy(x_ref, o_ref.at[self.me], own_sem)
        self.seen = set()
        self.started = []

    def send(self, index):
        _, _, p, slot, bit = self.events[index]
        if slot:
            self.arrived(p, slot)
        _, start, size, _ = self.parts[p]
        rows = pl.ds(start, size)
        block = flip(self.me, slot)
        item = pltpu.make_async_remote_copy(
            src_ref=self.x_ref.at[rows] if slot == 0 else self.o_ref.at[block, rows],
            dst_ref=self.o_ref.at[block, rows],
            send_sem=self.send_sem.at[index],
            recv_sem=self.recv_sem.at[p, slot ^ bit],
            device_id={"ctx": flip(self.me, bit)},
            device_id_type=MESH,
        )
        item.start()
        self.started.append(item)

    def arrived(self, p, slot):
        if (p, slot) in self.seen:
            return
        self.seen.add((p, slot))
        _, start, size, order = self.parts[p]
        rows = pl.ds(start, size)
        bit = [b for b in order if slot & b][-1]
        pltpu.make_async_remote_copy(
            src_ref=self.x_ref.at[rows],
            dst_ref=self.o_ref.at[flip(self.me, slot), rows],
            send_sem=self.send_sem.at[0],
            recv_sem=self.recv_sem.at[p, slot],
            device_id={"ctx": flip(self.me, bit)},
            device_id_type=MESH,
        ).wait_recv()

    def block(self, slot):
        if slot == 0:
            return self.x_ref
        for p in range(len(self.parts)):
            self.arrived(p, slot)
        return self.o_ref.at[flip(self.me, slot)]

    def finish(self):
        for slot in range(1, 1 << self.bits):
            self.block(slot)
        for item in self.started:
            item.wait_send()
        self.own.wait()


def gather_order(parts, bits, events, span):
    at = {}
    for index, (_, _, p, slot, bit) in enumerate(events):
        at[p, slot ^ bit] = span * (index + 1) / len(events)
    whole = {0: 0.0}
    for slot in range(1, 1 << bits):
        whole[slot] = max(at[p, slot] for p in range(len(parts)))
    return whole, at


def gather_plan(parts, bits, events, span, size, pieces, cost):
    whole, at = gather_order(parts, bits, events, span)
    slots = sorted(whole, key=lambda slot: (whole[slot], slot))
    groups = [slots[i : i + size] for i in range(0, len(slots), size)]
    ready = [max(whole[slot] for slot in group) for group in groups]
    work = [(g, k) for g in range(len(groups)) for k in range(pieces)]
    plan, now, e, w = [], 0.0, 0, 0
    while e < len(events) or w < len(work):
        _, _, p, slot, _ = events[e] if e < len(events) else (0, 0, 0, 0, 0)
        when = (at[p, slot] if slot else 0.0) if e < len(events) else math.inf
        then = ready[work[w][0]] if w < len(work) else math.inf
        if when <= now or when <= then:
            plan.append(("send", e))
            now = max(now, when) + 0.1
            e += 1
        else:
            plan.append(("work", work[w]))
            now = max(now, then) + cost / pieces
            w += 1
    return groups, plan


def expert_sizes(capacity, tokens, cycle):
    unit = 1
    while unit * capacity % 16:
        unit *= 2
    blocks = max(4, unit)
    return unit, blocks


def pick_rows(me, slots, unit, capacity, row_ref):
    tokens = row_ref.shape[2]
    places = []
    for q, slot in enumerate(slots):
        place = row_ref[flip(me, slot)]
        places.append(jnp.where(place >= 0, place + q * capacity, -1))
    place = jnp.concatenate(places, axis=1)
    shape = (unit * capacity, unit * tokens)
    return lax.broadcasted_iota(jnp.int32, shape, 0) == place


def as_bf16(mask):
    return mask.astype(f32).astype(bf16)


def experts_kernel(
    groups, plan, parts, bits, events, shares, unit, capacity, x_ref, row_ref, prob_ref, *refs
):
    weights, both_ref, down_ref = refs[: 3 * shares], refs[3 * shares], refs[3 * shares + 1]
    refs = refs[3 * shares + 2 :]
    o_ref, part_out, rows_out, gs_out, us_out, hs_out = refs[:6]
    kept_out, refs = refs[6 : 6 + 3 * shares], refs[6 + 3 * shares :]
    w, wb, wd, xg, rows, part, shared, kept = refs[:8]
    send_sem, recv_sem, own_sem, w_sem, x_sem, out_sem, part_sem = refs[8:]
    me = lax.axis_index("ctx")
    tokens = x_ref.shape[0]
    size = len(groups[0])
    tall, short = unit * tokens, unit * capacity
    width = wd.shape[0]
    gather = Gather(parts, bits, events, x_ref, o_ref, send_sem, recv_sem, own_sem)
    gather.own.start()
    loads = [pltpu.make_async_copy(weights[i], w.at[i], w_sem.at[i]) for i in range(3 * shares)]
    loads.append(pltpu.make_async_copy(both_ref, wb, w_sem.at[3 * shares]))
    loads.append(pltpu.make_async_copy(down_ref, wd, w_sem.at[3 * shares + 1]))
    greet(bits)
    ready = set()

    def need(i):
        if i not in ready:
            loads[i].wait()
            ready.add(i)
        return w[i] if i < 3 * shares else (wb if i == 3 * shares else wd)

    def outs(g):
        span = pl.ds(g * size * capacity, size * capacity)
        wide = pl.ds(g * size * tokens, size * tokens)
        items = [pltpu.make_async_copy(rows, rows_out.at[span], out_sem.at[0])]
        for i, ref in enumerate((gs_out, us_out, hs_out)):
            items.append(pltpu.make_async_copy(shared.at[i], ref.at[wide], out_sem.at[1 + i]))
        for i in range(3 * shares):
            items.append(
                pltpu.make_async_copy(kept.at[i], kept_out[i].at[span], out_sem.at[4 + i])
            )
        return items

    def part_outs(g, first=0, count=size):
        return [
            pltpu.make_async_copy(
                part.at[pl.ds(q * tokens, tokens)],
                part_out.at[flip(me, groups[g][q])],
                part_sem.at[q],
            )
            for q in range(first, first + count)
        ]

    state = {}

    def begin(g):
        copies = [
            pltpu.make_async_copy(
                gather.block(slot), xg.at[pl.ds(q * tokens, tokens)], x_sem.at[q]
            )
            for q, slot in enumerate(groups[g])
        ]
        for item in copies:
            item.start()
        if g:
            for item in outs(g - 1):
                item.wait()
        picks, scales = [], []
        for j in range(size // unit):
            slots = groups[g][j * unit : (j + 1) * unit]
            mask = pick_rows(me, slots, unit, capacity, row_ref)
            prob = jnp.concatenate([prob_ref[flip(me, slot)] for slot in slots], axis=1)
            scales.append(jnp.sum(jnp.where(mask, prob, 0.0), axis=1, keepdims=True))
            picks.append(as_bf16(mask))
        for item in copies:
            item.wait()
        for j, pick in enumerate(picks):
            chosen = dot(pick, xg[j * tall : (j + 1) * tall, :]).astype(bf16)
            rows[j * short : (j + 1) * short, :] = chosen
        state.update(picks=picks, scale=jnp.concatenate(scales, axis=0), total=0.0)

    def gate(s):
        state["gate"] = dot_last(rows[...], need(3 * s))

    def up(s):
        gated, upper = state["gate"], dot_last(rows[...], need(3 * s + 1))
        hidden = (gated * jax.nn.sigmoid(gated) * upper).astype(bf16)
        for i, value in enumerate((gated, upper, hidden)):
            kept[3 * s + i] = value.astype(bf16)

    def down(s):
        state["total"] = state["total"] + dot(kept[3 * s + 2], need(3 * s + 2))

    def shared_hidden(g):
        gated = dot(xg[...], need(3 * shares)[:, :width])
        upper = dot(xg[...], need(3 * shares)[:, width:])
        hidden = (gated * jax.nn.sigmoid(gated) * upper).astype(bf16)
        for i, value in enumerate((gated, upper, hidden)):
            shared[i] = value.astype(bf16)
        state["rows"] = (state["total"] * state["scale"]).astype(bf16)
        for item in outs(g):
            item.start()
        if g:
            for item in part_outs(g - 1):
                item.wait()

    def combine(g, j):
        inside = slice(j * tall, (j + 1) * tall)
        part[inside, :] = (
            dot_first(state["picks"][j], state["rows"][j * short : (j + 1) * short, :])
            + dot(shared[2, inside, :], need(3 * shares + 1)[...])
        ).astype(bf16)
        for item in part_outs(g, j * unit, unit):
            item.start()

    def piece(g, k):
        if k == 0:
            begin(g)
        elif k <= 3 * shares:
            (gate, up, down)[(k - 1) % 3]((k - 1) // 3)
        elif k == 3 * shares + 1:
            shared_hidden(g)
        else:
            combine(g, k - 3 * shares - 2)

    sent = 0
    for kind, item in plan:
        if kind == "send":
            gather.send(item)
            sent += 1
            if sent == bits * len(parts):
                for load in loads:
                    load.start()
        else:
            piece(*item)
    gather.finish()
    for item in outs(len(groups) - 1) + part_outs(len(groups) - 1):
        item.wait()


def experts(x, place, prob, weights, shared, capacity, bits, collective):
    tokens = x.shape[0]
    cycle = 1 << bits
    unit, size = expert_sizes(capacity, tokens, cycle)
    parts = all_parts([x.shape], bits)
    events = gather_events(parts, bits)
    shares = len(weights) // 3
    half = weights[0].shape[0]
    width = shared[1].shape[0]
    pieces = 3 * shares + 2 + size // unit
    groups, plan = gather_plan(parts, bits, events, 66.0, size, pieces, 10.5)
    anywhere = pl.BlockSpec(memory_space=pl.ANY)
    inside = pl.BlockSpec(memory_space=pltpu.VMEM)
    return pl.pallas_call(
        functools.partial(
            experts_kernel, groups, plan, parts, bits, events, shares, unit, capacity
        ),
        name="experts",
        out_shape=[
            jax.ShapeDtypeStruct((cycle, tokens, D), bf16),
            jax.ShapeDtypeStruct((cycle, tokens, D), bf16),
            jax.ShapeDtypeStruct((cycle * capacity, D), bf16),
        ]
        + [jax.ShapeDtypeStruct((cycle * tokens, width), bf16)] * 3
        + [jax.ShapeDtypeStruct((cycle * capacity, half), bf16)] * (3 * shares),
        in_specs=[anywhere, inside, inside] + [anywhere] * (3 * shares + 2),
        out_specs=[anywhere] * (6 + 3 * shares),
        scratch_shapes=[
            pltpu.VMEM((3 * shares, half, D), bf16),
            pltpu.VMEM((D, 2 * width), bf16),
            pltpu.VMEM((width, D), bf16),
            pltpu.VMEM((size * tokens, D), bf16),
            pltpu.VMEM((size * capacity, D), bf16),
            pltpu.VMEM((size * tokens, D), bf16),
            pltpu.VMEM((3, size * tokens, width), bf16),
            pltpu.VMEM((3 * shares, size * capacity, half), bf16),
            pltpu.SemaphoreType.DMA((len(events),)),
            pltpu.SemaphoreType.DMA((len(parts), cycle)),
            pltpu.SemaphoreType.DMA,
            pltpu.SemaphoreType.DMA((3 * shares + 2,)),
            pltpu.SemaphoreType.DMA((size,)),
            pltpu.SemaphoreType.DMA((4 + 3 * shares,)),
            pltpu.SemaphoreType.DMA((size,)),
        ],
        compiler_params=pltpu.CompilerParams(
            collective_id=collective, has_side_effects=True, vmem_limit_bytes=60 << 20
        ),
    )(x, place, prob, *weights, *shared)


def experts_back_kernel(
    groups, plan, parts, bits, events, shares, unit, capacity, x_ref, act_ref, row_ref, prob_ref,
    gs_in, us_in, hs_in, *refs,
):
    kept_in, refs = refs[: 2 * shares], refs[2 * shares :]
    weights, both_ref, down_ref = refs[: 3 * shares], refs[3 * shares], refs[3 * shares + 1]
    refs = refs[3 * shares + 2 :]
    o_ref, part_out, dy_out = refs[:3]
    grads_out, refs = refs[3 : 3 + 2 * shares], refs[3 + 2 * shares :]
    gws_ref, gwd_ref = refs[:2]
    w, wb, wd, dg, ag, dy, part, shared, kept, grads, gwg, gwu = refs[2:14]
    send_sem, recv_sem, own_sem, w_sem, x_sem, a_sem, k_sem, out_sem, part_sem = refs[14:]
    me = lax.axis_index("ctx")
    tokens = x_ref.shape[0]
    size = len(groups[0])
    tall, short = unit * tokens, unit * capacity
    width = wd.shape[0]
    gather = Gather(parts, bits, events, x_ref, o_ref, send_sem, recv_sem, own_sem)
    gather.own.start()
    loads = [pltpu.make_async_copy(weights[i], w.at[i], w_sem.at[i]) for i in range(3 * shares)]
    loads.append(pltpu.make_async_copy(both_ref, wb, w_sem.at[3 * shares]))
    loads.append(pltpu.make_async_copy(down_ref, wd, w_sem.at[3 * shares + 1]))
    greet(bits)
    for ref in (gwg, gwu, gwd_ref):
        ref[...] = jnp.zeros_like(ref)
    ready = set()

    def need(i):
        if i not in ready:
            loads[i].wait()
            ready.add(i)
        return w[i] if i < 3 * shares else (wb if i == 3 * shares else wd)

    def old(g):
        span = pl.ds(g * size * capacity, size * capacity)
        wide = pl.ds(g * size * tokens, size * tokens)
        items = [
            pltpu.make_async_copy(
                act_ref.at[flip(me, slot)], ag.at[pl.ds(q * tokens, tokens)], a_sem.at[q]
            )
            for q, slot in enumerate(groups[g])
        ]
        for i, ref in enumerate((gs_in, us_in, hs_in)):
            items.append(pltpu.make_async_copy(ref.at[wide], shared.at[i], k_sem.at[i]))
        for i in range(2 * shares):
            items.append(pltpu.make_async_copy(kept_in[i].at[span], kept.at[i], k_sem.at[3 + i]))
        return items

    def outs(g):
        span = pl.ds(g * size * capacity, size * capacity)
        items = [pltpu.make_async_copy(dy, dy_out.at[span], out_sem.at[0])]
        for i in range(2 * shares):
            items.append(
                pltpu.make_async_copy(grads.at[i], grads_out[i].at[span], out_sem.at[1 + i])
            )
        return items

    def part_outs(g, first=0, count=size):
        return [
            pltpu.make_async_copy(
                part.at[pl.ds(q * tokens, tokens)],
                part_out.at[flip(me, groups[g][q])],
                part_sem.at[q],
            )
            for q in range(first, first + count)
        ]

    state = {}

    def begin(g):
        copies = [
            pltpu.make_async_copy(
                gather.block(slot), dg.at[pl.ds(q * tokens, tokens)], x_sem.at[q]
            )
            for q, slot in enumerate(groups[g])
        ]
        for item in copies:
            item.start()
        if g:
            for item in outs(g - 1):
                item.wait()
        picks, scales = [], []
        for j in range(size // unit):
            slots = groups[g][j * unit : (j + 1) * unit]
            mask = pick_rows(me, slots, unit, capacity, row_ref)
            prob = jnp.concatenate([prob_ref[flip(me, slot)] for slot in slots], axis=1)
            scales.append(jnp.sum(jnp.where(mask, prob, 0.0), axis=1, keepdims=True))
            picks.append(as_bf16(mask))
        for item in copies:
            item.wait()
        for j, pick in enumerate(picks):
            chosen = dot(pick, dg[j * tall : (j + 1) * tall, :]) * scales[j]
            dy[j * short : (j + 1) * short, :] = chosen.astype(bf16)
        for item in old(g):
            item.wait()
        state.update(picks=picks, total=0.0)

    def hidden_back(s):
        grad_hidden = dot_last(dy[...], need(3 * s + 2))
        grad_gate, grad_up = silu_grads(
            kept[2 * s].astype(f32), kept[2 * s + 1].astype(f32), grad_hidden
        )
        grads[2 * s] = grad_gate
        grads[2 * s + 1] = grad_up

    def rows_back(s, i):
        state["total"] = state["total"] + dot(grads[2 * s + i], need(3 * s + i))

    def shared_back(g):
        for item in outs(g):
            item.start()
        grad_hidden = dot_last(dg[...], need(3 * shares + 1)[...])
        grad_gate, grad_up = silu_grads(
            shared[0].astype(f32), shared[1].astype(f32), grad_hidden
        )
        gwg[...] += dot_first(grad_gate, ag[...])
        state.update(gate=grad_gate, up=grad_up, rows=state["total"].astype(bf16))

    def shared_more(g):
        gwu[...] += dot_first(state["up"], ag[...])
        gwd_ref[...] += dot_first(shared[2], dg[...])
        if g + 1 < len(groups):
            for item in old(g + 1):
                item.start()
        if g:
            for item in part_outs(g - 1):
                item.wait()

    def combine(g, j):
        inside = slice(j * tall, (j + 1) * tall)
        both = need(3 * shares)
        part[inside, :] = (
            dot_first(state["picks"][j], state["rows"][j * short : (j + 1) * short, :])
            + dot_last(state["gate"][inside, :], both[:, :width])
            + dot_last(state["up"][inside, :], both[:, width:])
        ).astype(bf16)
        for item in part_outs(g, j * unit, unit):
            item.start()

    def piece(g, k):
        if k == 0:
            begin(g)
        elif k <= 3 * shares:
            s, i = (k - 1) // 3, (k - 1) % 3
            hidden_back(s) if i == 0 else rows_back(s, i - 1)
        elif k == 3 * shares + 1:
            shared_back(g)
        elif k == 3 * shares + 2:
            shared_more(g)
        else:
            combine(g, k - 3 * shares - 3)

    sent = 0
    for kind, item in plan:
        if kind == "send":
            gather.send(item)
            sent += 1
            if sent == bits * len(parts):
                for load in loads + old(0):
                    load.start()
        else:
            piece(*item)
    gws_ref[:, :width] = gwg[...].T.astype(bf16)
    gws_ref[:, width:] = gwu[...].T.astype(bf16)
    gather.finish()
    for item in outs(len(groups) - 1) + part_outs(len(groups) - 1):
        item.wait()


def experts_back(x, act, place, prob, saved, kept, weights, shared, capacity, bits, collective):
    tokens = x.shape[0]
    cycle = 1 << bits
    unit, size = expert_sizes(capacity, tokens, cycle)
    parts = all_parts([x.shape], bits)
    events = gather_events(parts, bits)
    shares = len(weights) // 3
    half = weights[0].shape[0]
    width = shared[1].shape[0]
    pieces = 3 * shares + 3 + size // unit
    groups, plan = gather_plan(parts, bits, events, 66.0, size, pieces, 15.0)
    anywhere = pl.BlockSpec(memory_space=pl.ANY)
    inside = pl.BlockSpec(memory_space=pltpu.VMEM)
    return pl.pallas_call(
        functools.partial(
            experts_back_kernel, groups, plan, parts, bits, events, shares, unit, capacity
        ),
        name="experts_back",
        out_shape=[
            jax.ShapeDtypeStruct((cycle, tokens, D), bf16),
            jax.ShapeDtypeStruct((cycle, tokens, D), bf16),
            jax.ShapeDtypeStruct((cycle * capacity, D), bf16),
        ]
        + [jax.ShapeDtypeStruct((cycle * capacity, half), bf16)] * (2 * shares)
        + [jax.ShapeDtypeStruct((D, 2 * width), bf16), jax.ShapeDtypeStruct((width, D), f32)],
        in_specs=[anywhere, anywhere, inside, inside] + [anywhere] * (5 + 5 * shares),
        out_specs=[anywhere] * (3 + 2 * shares) + [inside, inside],
        scratch_shapes=[
            pltpu.VMEM((3 * shares, half, D), bf16),
            pltpu.VMEM((D, 2 * width), bf16),
            pltpu.VMEM((width, D), bf16),
            pltpu.VMEM((size * tokens, D), bf16),
            pltpu.VMEM((size * tokens, D), bf16),
            pltpu.VMEM((size * capacity, D), bf16),
            pltpu.VMEM((size * tokens, D), bf16),
            pltpu.VMEM((3, size * tokens, width), bf16),
            pltpu.VMEM((2 * shares, size * capacity, half), bf16),
            pltpu.VMEM((2 * shares, size * capacity, half), bf16),
            pltpu.VMEM((width, D), f32),
            pltpu.VMEM((width, D), f32),
            pltpu.SemaphoreType.DMA((len(events),)),
            pltpu.SemaphoreType.DMA((len(parts), cycle)),
            pltpu.SemaphoreType.DMA,
            pltpu.SemaphoreType.DMA((3 * shares + 2,)),
            pltpu.SemaphoreType.DMA((size,)),
            pltpu.SemaphoreType.DMA((size,)),
            pltpu.SemaphoreType.DMA((3 + 2 * shares,)),
            pltpu.SemaphoreType.DMA((1 + 2 * shares,)),
            pltpu.SemaphoreType.DMA((size,)),
        ],
        compiler_params=pltpu.CompilerParams(
            collective_id=collective, has_side_effects=True, vmem_limit_bytes=61 << 20
        ),
    )(x, act, place, prob, *saved, *kept, *weights, *shared)


def shift_fsdp(x, groups, by):
    return lax.ppermute(x, "fsdp", [(i, (i + by) % groups) for i in range(groups)])


def gather_fsdp(x, groups):
    if groups != 2:
        return lax.all_gather(x, "fsdp", axis=0)
    other = shift_fsdp(x, groups, 1)
    mine_first = lax.axis_index("fsdp") == 0
    return jnp.stack([jnp.where(mine_first, x, other), jnp.where(mine_first, other, x)])


def scatter_fsdp(x, groups):
    if groups != 2:
        return lax.psum_scatter(x.astype(bf16), "fsdp", scatter_dimension=0).astype(f32)
    me = lax.axis_index("fsdp")
    away = lax.dynamic_index_in_dim(x, 1 - me, 0, keepdims=False).astype(bf16)
    mine = lax.dynamic_index_in_dim(x, me, 0, keepdims=False).astype(f32)
    return mine + shift_fsdp(away, groups, 1).astype(f32)


def shards(
    hidden_in,
    teacher,
    doc_starts,
    routes,
    gate_logits,
    input_gain,
    query_weight,
    latent_weight,
    latent_gain,
    expand_weight,
    output_weight,
    mixer_gain,
    shared_gate,
    shared_up,
    shared_down,
    expert_gate,
    expert_up,
    expert_down,
):
    cycle = lax.axis_size("ctx")
    groups = lax.axis_size("fsdp")
    bits = cycle.bit_length() - 1
    tokens = hidden_in.shape[1]
    length = tokens * cycle
    capacity = min(tokens, 3 * tokens * TOPK // (2 * cycle))
    scale = (DN + DR) ** (-0.5)
    copies = max(1, cycle // H)
    ctx_index = lax.axis_index("ctx")
    copy_index = ctx_index % copies
    slab = query_weight.shape[0]
    slab_latent = expand_weight.shape[0]

    def pieces(weight):
        rows, width = weight.shape
        return jnp.transpose(weight.reshape(rows, cycle, width // cycle), (1, 0, 2))

    def padded(item, width):
        return jnp.pad(item, ((0, 0), (0, 0), (0, width - item.shape[2])))

    def exchange(packed):
        return lax.all_to_all(packed, "ctx", split_axis=0, concat_axis=0, tiled=True)

    def same_head(part, axis):
        if copies == 1:
            return part
        teams = [[i * copies + j for j in range(copies)] for i in range(H)]
        return lax.all_gather(part, "ctx", axis=axis, tiled=True, axis_index_groups=teams)

    def own_part(full, axis=1):
        if copies == 1:
            return full
        width = full.shape[axis] // copies
        return lax.dynamic_slice_in_dim(full, copy_index * width, width, axis)

    def swap(pair):
        half = pair.shape[1] // 2
        return jnp.concatenate([-pair[:, half:], pair[:, :half]], axis=1)

    def all_rows(item):
        both = jnp.transpose(gather_fsdp(item, groups), (1, 0, 2, 3))
        return both.reshape(-1, item.shape[2])

    fast = copies == 1 and groups == 2 and cycle * groups * slab == D and slab == 64
    part_q, part_e = H * (DN + DR) // cycle, H * (DN + DV) // cycle
    part_s = shared_gate.shape[1] // cycle
    shared_width = -(-part_s // 128) * 128

    probs = jax.nn.softmax(gate_logits[0], axis=-1)
    chosen = routes[0][:, :, None] == jnp.arange(cycle, dtype=jnp.int32)[None, None, :]
    dense_probs = jnp.sum(jnp.where(chosen, probs[:, :, None], 0.0), axis=1).T
    high = lax.reduce_precision(dense_probs, 8, 7)
    dense_probs = jnp.concatenate([high, dense_probs - high], axis=1).astype(bf16)
    prob_width = 2 * tokens // slab
    dense_probs = dense_probs.reshape(cycle, slab, prob_width)
    expand_pieces = pieces(expand_weight)
    if fast:
        quarter = part_e // 4
        expand_pieces = jnp.concatenate(
            [expand_pieces[:, :, q * quarter : (q + 1) * quarter] for q in range(4)], axis=1
        )
    else:
        expand_pieces = expand_pieces.reshape(cycle, slab, -1)
    block_q = -(-(part_q + expand_pieces.shape[2]) // 128) * 128
    block_s = -(-(part_s + prob_width) // 128) * 128
    packed = padded(jnp.concatenate([pieces(query_weight), expand_pieces], axis=2), block_q)
    packed = exchange(packed)
    packed_s = jnp.concatenate(
        [
            padded(jnp.concatenate([pieces(shared_gate), dense_probs], axis=2), block_s),
            padded(pieces(shared_up), block_s),
        ],
        axis=2,
    )
    narrow = jnp.concatenate(
        [
            latent_weight,
            input_gain[:, None],
            mixer_gain[:, None],
            jnp.concatenate([latent_gain, jnp.zeros((slab - slab_latent,), bf16)])[:, None],
            jnp.zeros((slab, -(KVR + DR + 3) % 128), bf16),
        ],
        axis=1,
    )
    w_down_s = gather_fsdp(shared_down, groups).reshape(-1, D)
    w_down_s = jnp.pad(w_down_s, ((0, shared_width - w_down_s.shape[0]), (0, 0)))
    w_output = gather_fsdp(output_weight, groups).reshape(-1, D)
    if copies > 1:
        rows_o = w_output.shape[0]
        own_output = lax.dynamic_update_slice_in_dim(
            jnp.zeros((DV, D), bf16), w_output, copy_index * rows_o, 0
        )
        w_output = same_head(w_output, 0)
    else:
        own_output = w_output
    weights = [expert_gate[0].T, expert_up[0].T, expert_down[0]]
    for r in range(1, groups):
        weights += [shift_fsdp(item, groups, r) for item in weights[:3]]
    starts = doc_starts[0]
    positions = jnp.arange(length, dtype=jnp.int32)
    inside = starts[None, :] <= positions[:, None]
    first_pos = jnp.max(jnp.where(inside, starts[None, :], 0), axis=1)
    cosine, sine = rope_tables(positions - first_pos)
    cosine = jnp.tile(cosine, (1, 4))
    sine = jnp.tile(sine, (1, 4))

    all_hidden, narrow = gather_ctx([hidden_in[0], narrow], bits, 1)
    packed_s, _ = lax.optimization_barrier((packed_s, all_hidden))
    packed_s = exchange(packed_s)
    my_probs = packed_s[:, :, part_s : part_s + prob_width]
    my_probs = my_probs.reshape(cycle, 2, tokens).astype(f32)
    my_probs = my_probs[:, 0] + my_probs[:, 1]
    if fast:
        w_cat, w_expand, gains = assemble(
            packed, shift_fsdp(packed, groups, 1), narrow, shift_fsdp(narrow, groups, 1)
        )
        gain_one, gain_two = gains[0], gains[1]
        gain_latent = gains[2].reshape(-1, slab)[:, :slab_latent].reshape(-1)
    else:
        narrow, packed = all_rows(narrow), all_rows(packed)
        gain_one = narrow[:, KVR + DR].astype(f32)
        gain_two = narrow[:, KVR + DR + 1].astype(f32)
        gain_latent = narrow[:, KVR + DR + 2].reshape(-1, slab)[:, :slab_latent]
        gain_latent = gain_latent.reshape(-1).astype(f32)
        w_query = same_head(packed[:, :part_q], 1)
        w_expand = packed[:, part_q : part_q + expand_pieces.shape[2]].reshape(KVR, part_e)
        w_expand = same_head(w_expand, 1)
        rope_k = narrow[:, KVR : KVR + DR]
        w_cat = jnp.concatenate(
            [w_query, rope_k, swap(w_query[:, DN:]), swap(rope_k), narrow[:, :KVR]], axis=1
        )

    w_both_s = all_rows(packed_s)

    residual = hidden_in[0].astype(f32)
    act_one, queries, keys, values, latent, latent_raw = project(
        all_hidden.reshape(length, D), gain_one, w_cat, gain_latent, w_expand, cosine, sine, scale
    )
    attended, log_total, partial = attend(
        queries, keys, values, first_pos[:, None], own_output
    )
    (mixing,) = scatter_ctx([partial.reshape(cycle, tokens, D)], bits, 3)
    mixed = residual + mixing

    normed_two, factor_two = norm_forward(mixed, gain_two)
    used = my_probs > 0.0
    place = jnp.cumsum(used.astype(jnp.int32), axis=1) - 1
    routing = (jnp.where(used, place, -1)[:, None, :], my_probs[:, None, :])
    shared = [w_both_s, w_down_s]
    all_act, partial, rows, gate_s, up_s, hidden_s, *kept = experts(
        normed_two.astype(bf16), *routing, weights, shared, capacity, bits, 2
    )
    (routed,) = scatter_ctx([partial], bits, 3)
    result = mixed + routed
    diff = result - teacher[0].astype(f32)
    share = jnp.sum(gather_fsdp(0.5 * jnp.sum(diff * diff, keepdims=True), groups))

    gates = [item for s in range(groups) for item in kept[3 * s : 3 * s + 2]]
    _, partial, grad_rows, *grads, grad_shared, grad_w_down = experts_back(
        diff.astype(bf16),
        all_act,
        *routing,
        [gate_s, up_s, hidden_s],
        gates,
        weights,
        shared,
        capacity,
        bits,
        6,
    )
    (grad_act_two,) = scatter_ctx([partial], bits, 3)
    grad_w_down = scatter_fsdp(grad_w_down[:part_s].reshape(groups, -1, D), groups)

    grad_gain_two = jnp.sum(grad_act_two * mixed * factor_two, axis=0)
    grad_mixed = diff + norm_back_rows(mixed, factor_two, gain_two, grad_act_two)
    lefts = []
    for r in range(groups):
        lefts += [grads[2 * r], grads[2 * r + 1], kept[3 * r + 2]]
    all_mixed, *expert_grads = gather_multiply(
        grad_mixed.astype(bf16), rows, grad_rows, lefts, bits, 5
    )
    def by_owner(grad):
        cut = jnp.transpose(grad.reshape(cycle, groups, slab, -1), (1, 0, 2, 3))
        return scatter_fsdp(cut, groups).astype(bf16)

    grad_shared, _ = lax.optimization_barrier((grad_shared, all_mixed))
    grad_shared = by_owner(grad_shared)
    high = lax.reduce_precision(share, 8, 7)
    mid = lax.reduce_precision(share - high, 8, 7)
    loss_parts = jnp.stack([high, mid, share - high - mid]).astype(bf16)
    spot = jnp.arange(grad_shared.shape[2], dtype=jnp.int32) - part_s
    loss_row = sum(jnp.where(spot == i, loss_parts[i], bf16(0)) for i in range(3))
    grad_shared = jnp.where(((spot >= 0) & (spot < 3))[None, None, :], loss_row, grad_shared)
    packed_s = exchange(grad_shared)
    loss_parts = packed_s[:, 0, part_s : part_s + 3].astype(f32)
    loss_value = jnp.sum(loss_parts) / (length * groups * D)
    grad_query, grad_keys, grad_values, grad_w_output = attend_back(
        queries,
        keys,
        values,
        all_mixed.reshape(length, D),
        attended,
        w_output,
        first_pos[None, :],
        log_total.reshape(1, length),
    )
    grad_query, packed_s = lax.optimization_barrier((grad_query, packed_s))
    grad_w_output = own_part(grad_w_output, 0).reshape(groups, slab, D)
    grad_w_output = scatter_fsdp(grad_w_output, groups)
    lanes = jnp.arange(WIDE, dtype=jnp.int32)
    keep_q = (lanes // ((DN + DR) // copies) == copy_index).astype(f32)[None, :]
    keep_e = (lanes // ((DN + DV) // copies) == copy_index).astype(f32)[None, :]
    partial, grad_w_cat, grad_w_expand = project_back(
        grad_query,
        grad_keys,
        grad_values,
        latent_raw,
        latent,
        act_one,
        cosine,
        sine,
        w_cat,
        w_expand,
        gain_latent,
        keep_q,
        keep_e,
        scale,
        copies,
    )
    if fast:
        first, slim = finish(
            grad_w_cat, grad_w_expand, w_cat, w_expand, grad_gain_two[:, None], cycle, slab
        )
    else:
        grad_gain_one = jnp.sum(grad_w_cat * w_cat.astype(f32), axis=1)
        grad_gain_latent = jnp.sum(grad_w_expand * w_expand.astype(f32), axis=1)
        turned = grad_w_cat[:, 2 * DN : 3 * DN]
        grad_ropes = grad_w_cat[:, DN : 2 * DN] - jnp.concatenate(
            [swap(turned[:, :DR]), swap(turned[:, DR:])], axis=1
        )
        grad_w_query = jnp.concatenate([grad_w_cat[:, :DN], grad_ropes[:, :DR]], axis=1)
        grad_we = own_part(grad_w_expand).reshape(cycle * groups, slab_latent, part_e)
        first = jnp.concatenate(
            [own_part(grad_w_query), grad_we.reshape(D, -1)], axis=1
        ).astype(bf16)
        spare = jnp.zeros((cycle * groups, slab - slab_latent), f32)
        grad_gain_latent = jnp.concatenate(
            [grad_gain_latent.reshape(cycle * groups, slab_latent), spare], axis=1
        ).reshape(-1)
        slim = jnp.concatenate(
            [
                grad_w_cat[:, 3 * DN :],
                grad_ropes[:, DR:],
                grad_gain_one[:, None],
                grad_gain_two[:, None],
                grad_gain_latent[:, None],
                jnp.zeros((D, -(KVR + DR + 3) % 128), f32),
            ],
            axis=1,
        ).astype(bf16)

    slim = by_owner(slim)
    first = padded(by_owner(first), block_q)
    packed = exchange(first)
    grad_act_one, grad_narrow = scatter_ctx(
        [partial.reshape(cycle, tokens, D), slim], bits, 4
    )
    if fast:
        own_grads = spread(
            packed,
            packed_s,
            [w.shape[1] for w in (query_weight, expand_weight, shared_gate, shared_up)],
        )
    else:
        spots = (
            (packed, 0, part_q, query_weight),
            (packed, part_q, expand_pieces.shape[2], expand_weight),
            (packed_s, 0, part_s, shared_gate),
            (packed_s, shared_width, part_s, shared_up),
        )
        own_grads = []
        for item, start, width, like in spots:
            item = item[:, :, start : start + width].reshape(cycle, like.shape[0], -1)
            own_grads.append(jnp.transpose(item, (1, 0, 2)).reshape(like.shape).astype(f32))
    _, factor_one = norm_forward(residual, gain_one)
    grad_input = grad_mixed + norm_back_rows(residual, factor_one, gain_one, grad_act_one)
    return (
        result.astype(bf16)[None],
        loss_value,
        grad_input[None],
        grad_narrow[:, KVR + DR] / input_gain.astype(f32),
        own_grads[0],
        grad_narrow[:, : KVR + DR],
        grad_narrow[:slab_latent, KVR + DR + 2] / latent_gain.astype(f32),
        own_grads[1],
        grad_w_output,
        grad_narrow[:, KVR + DR + 1],
        own_grads[2],
        own_grads[3],
        grad_w_down,
        expert_grads[0].astype(f32).T[None],
        expert_grads[1].astype(f32).T[None],
        expert_grads[2].astype(f32)[None],
    )


def solution(mesh):
    tokens = P("fsdp", "ctx", None)
    rows = P(("ctx", "fsdp"), None)
    gain = P(("ctx", "fsdp"))
    wide = P("ctx", None, "fsdp")
    deep = P("ctx", "fsdp", None)
    in_specs = (
        tokens,
        tokens,
        P("fsdp", None),
        tokens,
        tokens,
        gain,
        rows,
        rows,
        gain,
        rows,
        rows,
        gain,
        rows,
        rows,
        rows,
        wide,
        wide,
        deep,
    )
    out_specs = (
        tokens,
        P(),
        tokens,
        gain,
        rows,
        rows,
        gain,
        rows,
        rows,
        gain,
        rows,
        rows,
        rows,
        wide,
        wide,
        deep,
    )
    return jax.shard_map(shards, mesh=mesh, in_specs=in_specs, out_specs=out_specs, check_vma=False)
```

```python
import functools
import math

import jax
import jax.numpy as jnp
from jax import lax
from jax.experimental import pallas as pl
from jax.experimental.pallas import tpu as pltpu
from jax.sharding import PartitionSpec as P

D = 2048
H = 16
DN = 128
DR = 64
DV = 128
KVR = 512
TOPK = 6
WIDE = 256

EPS = 1e-06
NEG = -1e30
MESH = pl.DeviceIdType.MESH
f32 = jnp.float32
bf16 = jnp.bfloat16


def norm_forward(rows, gain):
    factor = lax.rsqrt(jnp.mean(rows * rows, axis=-1, keepdims=True) + EPS)
    return (rows * factor * gain, factor)


def norm_back_rows(rows, factor, gain, grad_out):
    scaled = grad_out * gain
    normed = rows * factor
    return factor * (scaled - normed * jnp.mean(scaled * normed, axis=-1, keepdims=True))


def rotate(values, cosine, sine):
    half = values.shape[-1] // 2
    first = values[..., :half]
    second = values[..., half:]
    return jnp.concatenate(
        [first * cosine - second * sine, second * cosine + first * sine], axis=-1
    )


def rope_tables(offsets):
    spot = (jnp.arange(2 * DR, dtype=jnp.int32) % (DR // 2)).astype(f32)
    freqs = 10000.0 ** (-(spot * 2.0) / DR)
    angle = offsets.astype(f32)[:, None] * freqs[None, :]
    return (jnp.cos(angle), jnp.sin(angle))


def silu_grads(gate_val, up_val, grad_hidden):
    sigma = jax.nn.sigmoid(gate_val)
    grad_gate = grad_hidden * up_val * sigma * (1.0 + gate_val * (1.0 - sigma))
    grad_up = grad_hidden * gate_val * sigma
    return (grad_gate.astype(bf16), grad_up.astype(bf16))


def dot(left, right):
    return jnp.dot(left, right, preferred_element_type=f32)


def dot_first(left, right):
    return lax.dot_general(left, right, (((0,), (0,)), ((), ())), preferred_element_type=f32)


def dot_last(left, right):
    return lax.dot_general(left, right, (((1,), (1,)), ((), ())), preferred_element_type=f32)


def flip(me, mask):
    out = me
    bit = 1
    while bit <= mask:
        if mask & bit:
            out = out + bit * (1 - 2 * ((me // bit) % 2))
        bit *= 2
    return out


def row_parts(rows, bits):
    low, high = [1, 2], [1 << k for k in range(bits - 1, 1, -1)]
    orders = (high + low, high + low[::-1], low + high)
    units = rows // 16
    if units < 3:
        return ((0, rows, tuple(orders[0])),)
    third = max(1, units // 4)
    first = (units - third) // 2
    counts = (first * 16, (units - third - first) * 16, third * 16)
    parts, start = [], 0
    for count, order in zip(counts, orders):
        parts.append((start, count, tuple(order)))
        start += count
    return tuple(parts)


def all_parts(shapes, bits):
    return tuple(
        (a,) + part for a, shape in enumerate(shapes) for part in row_parts(shape[-2], bits)
    )


def greet(bits):
    me = lax.axis_index("ctx")
    barrier = pltpu.get_barrier_semaphore()
    for k in range(bits):
        pl.semaphore_signal(
            barrier, inc=1, device_id={"ctx": flip(me, 1 << k)}, device_id_type=MESH
        )
    pl.semaphore_wait(barrier, bits)


def gather_events(parts, bits):
    events = []
    for p, (_, _, _, order) in enumerate(parts):
        for slot in range(1 << bits):
            hops = [k for k, b in enumerate(order) if slot & b]
            for k in range(hops[-1] + 1 if hops else 0, bits):
                events.append((len(hops), k, p, slot, order[k]))
    return tuple(sorted(events))


def gather_kernel(parts, bits, events, count, *refs):
    x_refs, o_refs = refs[:count], refs[count : 2 * count]
    send_sem, recv_sem, own_sem = refs[2 * count :]
    me = lax.axis_index("ctx")
    own = [
        pltpu.make_async_copy(x_refs[a], o_refs[a].at[me], own_sem.at[a]) for a in range(count)
    ]
    for item in own:
        item.start()
    greet(bits)

    def copy(p, slot, bit, index):
        a, start, size, _ = parts[p]
        rows = pl.ds(start, size)
        block = flip(me, slot)
        return pltpu.make_async_remote_copy(
            src_ref=x_refs[a].at[rows] if slot == 0 else o_refs[a].at[block, rows],
            dst_ref=o_refs[a].at[block, rows],
            send_sem=send_sem.at[index],
            recv_sem=recv_sem.at[p, slot ^ bit],
            device_id={"ctx": flip(me, bit)},
            device_id_type=MESH,
        )

    def arrived(p, slot):
        a, start, size, order = parts[p]
        rows = pl.ds(start, size)
        bit = [b for b in order if slot & b][-1]
        pltpu.make_async_remote_copy(
            src_ref=x_refs[a].at[rows],
            dst_ref=o_refs[a].at[flip(me, slot), rows],
            send_sem=send_sem.at[0],
            recv_sem=recv_sem.at[p, slot],
            device_id={"ctx": flip(me, bit)},
            device_id_type=MESH,
        ).wait_recv()

    seen = set()
    started = []
    for index, (_, _, p, slot, bit) in enumerate(events):
        if slot and (p, slot) not in seen:
            arrived(p, slot)
            seen.add((p, slot))
        sent = copy(p, slot, bit, index)
        sent.start()
        started.append(sent)
    for p in range(len(parts)):
        for slot in range(1, 1 << bits):
            if (p, slot) not in seen:
                arrived(p, slot)
    for sent in started:
        sent.wait_send()
    for item in own:
        item.wait()


def gather_ctx(arrays, bits, collective):
    parts = all_parts([item.shape for item in arrays], bits)
    events = gather_events(parts, bits)
    count = len(arrays)
    return pl.pallas_call(
        functools.partial(gather_kernel, parts, bits, events, count),
        name="gather_ctx",
        out_shape=[jax.ShapeDtypeStruct((1 << bits,) + item.shape, item.dtype) for item in arrays],
        in_specs=[pl.BlockSpec(memory_space=pl.ANY)] * count,
        out_specs=[pl.BlockSpec(memory_space=pl.ANY)] * count,
        scratch_shapes=[
            pltpu.SemaphoreType.DMA((len(events),)),
            pltpu.SemaphoreType.DMA((len(parts), 1 << bits)),
            pltpu.SemaphoreType.DMA((count,)),
        ],
        compiler_params=pltpu.CompilerParams(collective_id=collective, has_side_effects=True),
    )(*arrays)


def gather_multiply_kernel(
    parts, bits, events, shares, tile, x_ref, rows_ref, dy_ref, *refs
):
    lefts, refs = refs[: 3 * shares], refs[3 * shares :]
    o_ref, outs, refs = refs[0], refs[1:4], refs[4:]
    rows, dy, left, sent, got, stage = refs[:6]
    send_sem, recv_sem, own_sem, load_sem, out_sem, far_sem, near_sem = refs[6:]
    me, place = lax.axis_index("ctx"), lax.axis_index("fsdp")
    half, width = left.shape[2], rows.shape[1]
    tiles = width // tile
    loads = [pltpu.make_async_copy(rows_ref, rows, load_sem.at[3 * shares])]
    loads.append(pltpu.make_async_copy(dy_ref, dy, load_sem.at[3 * shares + 1]))
    order = list(range(3, 3 * shares)) + [0, 1, 2]
    for i in range(3 * shares):
        loads.append(pltpu.make_async_copy(lefts[i], left.at[i], load_sem.at[i]))
    own = pltpu.make_async_copy(x_ref, o_ref.at[me], own_sem)
    own.start()
    barrier = pltpu.get_barrier_semaphore()
    for k in range(bits):
        pl.semaphore_signal(
            barrier, inc=1, device_id={"ctx": flip(me, 1 << k)}, device_id_type=MESH
        )
    for r in range(1, shares):
        pl.semaphore_signal(
            barrier, inc=1, device_id={"fsdp": (place + r) % shares}, device_id_type=MESH
        )
    pl.semaphore_wait(barrier, bits + shares - 1)
    for i in [0, 2 + 3 % (3 * shares), 1] if shares > 1 else [0, 2, 1]:
        loads[i].start()
    for i in range(2, len(loads)):
        if i != 2 + 3 % (3 * shares):
            loads[i].start()
    ready = set()

    def need(i):
        if i not in ready:
            loads[i].wait()
            ready.add(i)

    def copy(p, slot, bit, index):
        _, start, size, _ = parts[p]
        part = pl.ds(start, size)
        block = flip(me, slot)
        return pltpu.make_async_remote_copy(
            src_ref=x_ref.at[part] if slot == 0 else o_ref.at[block, part],
            dst_ref=o_ref.at[block, part],
            send_sem=send_sem.at[index],
            recv_sem=recv_sem.at[p, slot ^ bit],
            device_id={"ctx": flip(me, bit)},
            device_id_type=MESH,
        )

    def arrived(p, slot):
        _, start, size, path = parts[p]
        part = pl.ds(start, size)
        bit = [b for b in path if slot & b][-1]
        pltpu.make_async_remote_copy(
            src_ref=x_ref.at[part],
            dst_ref=o_ref.at[flip(me, slot), part],
            send_sem=send_sem.at[0],
            recv_sem=recv_sem.at[p, slot],
            device_id={"ctx": flip(me, bit)},
            device_id_type=MESH,
        ).wait_recv()

    def far(i, t):
        spot = (i - 3, slice(None), pl.ds(t * tile, tile))
        return pltpu.make_async_remote_copy(
            src_ref=sent.at[spot],
            dst_ref=got.at[spot],
            send_sem=far_sem.at[i - 3, t],
            recv_sem=near_sem.at[i - 3, t],
            device_id={"fsdp": (place + shares - i // 3) % shares},
            device_id_type=MESH,
        )

    def store(i, t):
        buffer = (i * tiles + t) % 2
        return pltpu.make_async_copy(
            stage.at[buffer], outs[i].at[:, pl.ds(t * tile, tile)], out_sem.at[i, t]
        )

    def multiply(i, t):
        need(2 + i)
        need(1 if i % 3 == 2 else 0)
        right = dy if i % 3 == 2 else rows
        total = dot_first(left[i], right[:, t * tile : (t + 1) * tile])
        if i >= 3:
            sent[i - 3, :, t * tile : (t + 1) * tile] = total.astype(bf16)
            far(i, t).start()
            return
        for r in range(1, shares):
            far(i + 3 * r, t).wait_recv()
            total = total + got[i + 3 * r - 3, :, t * tile : (t + 1) * tile].astype(f32)
        last = i * tiles + t - 2
        if last >= 0:
            store(last // tiles, last % tiles).wait()
        stage[(i * tiles + t) % 2] = total.astype(bf16)
        store(i, t).start()

    work = [(i, t) for i in order for t in range(tiles)]
    done = 0
    seen = set()
    started = []
    for index, (_, _, p, slot, bit) in enumerate(events):
        if slot and (p, slot) not in seen:
            arrived(p, slot)
            seen.add((p, slot))
        item = copy(p, slot, bit, index)
        item.start()
        started.append(item)
        first = bits * len(parts)
        if index >= first:
            while done < len(work) * (index - first + 1) // (len(events) - first):
                multiply(*work[done])
                done += 1
    for p in range(len(parts)):
        for slot in range(1, 1 << bits):
            if (p, slot) not in seen:
                arrived(p, slot)
    for item in started:
        item.wait_send()
    own.wait()
    for i in range(3, 3 * shares):
        for t in range(tiles):
            far(i, t).wait_send()
    for last in range(max(0, 3 * tiles - 2), 3 * tiles):
        store(last // tiles, last % tiles).wait()


def gather_multiply(x, rows, dy, lefts, bits, collective):
    parts = all_parts([x.shape], bits)
    events = gather_events(parts, bits)
    shares = len(lefts) // 3
    count, half = lefts[0].shape
    width = rows.shape[1]
    tile = width // 2
    anywhere = pl.BlockSpec(memory_space=pl.ANY)
    others = max(1, 3 * shares - 3)
    return pl.pallas_call(
        functools.partial(gather_multiply_kernel, parts, bits, events, shares, tile),
        name="gather_multiply",
        out_shape=[jax.ShapeDtypeStruct((1 << bits,) + x.shape, x.dtype)]
        + [jax.ShapeDtypeStruct((half, width), bf16)] * 3,
        in_specs=[anywhere] * (3 + 3 * shares),
        out_specs=[anywhere] * 4,
        scratch_shapes=[
            pltpu.VMEM((count, width), bf16),
            pltpu.VMEM((count, width), bf16),
            pltpu.VMEM((3 * shares, count, half), bf16),
            pltpu.VMEM((others, half, width), bf16),
            pltpu.VMEM((others, half, width), bf16),
            pltpu.VMEM((2, half, tile), bf16),
            pltpu.SemaphoreType.DMA((len(events),)),
            pltpu.SemaphoreType.DMA((len(parts), 1 << bits)),
            pltpu.SemaphoreType.DMA,
            pltpu.SemaphoreType.DMA((3 * shares + 2,)),
            pltpu.SemaphoreType.DMA((3, width // tile)),
            pltpu.SemaphoreType.DMA((others, width // tile)),
            pltpu.SemaphoreType.DMA((others, width // tile)),
        ],
        compiler_params=pltpu.CompilerParams(
            collective_id=collective, has_side_effects=True, vmem_limit_bytes=60 << 20
        ),
    )(x, rows, dy, *lefts)


def scatter_events(parts, bits):
    events = []
    for p, (_, _, _, order) in enumerate(parts):
        for slot in range(1, 1 << bits):
            k = [i for i, b in enumerate(order) if slot & b][0]
            later = tuple(-int(bool(slot & b)) for b in order[k + 1 :])
            events.append((k, later, p, slot))
    return tuple((k, p, slot) for k, _, p, slot in sorted(events))


def scatter_kernel(parts, bits, events, count, *refs):
    x_refs, o_refs = refs[:count], refs[count : 2 * count]
    recvs, sends, owns = (refs[(2 + i) * count : (3 + i) * count] for i in range(3))
    send_sem, recv_sem, own_sem = refs[5 * count :]
    me = lax.axis_index("ctx")
    later = [sorted({s for k, p, s in events if k and parts[p][0] == a}) for a in range(count)]

    def load(a, slot):
        place = later[a].index(slot) + 1 if slot else 0
        return pltpu.make_async_copy(
            x_refs[a].at[flip(me, slot)], owns[a].at[place], own_sem.at[a, place]
        )

    greet(bits)

    def copy(p, slot, k, src):
        a, start, size, order = parts[p]
        return pltpu.make_async_remote_copy(
            src_ref=src,
            dst_ref=recvs[a].at[slot - 1, pl.ds(start, size)],
            send_sem=send_sem.at[p, slot - 1],
            recv_sem=recv_sem.at[p, slot - 1],
            device_id={"ctx": flip(me, order[k])},
            device_id_type=MESH,
        )

    loaded = set()

    def add_up(p, slot, k):
        a, start, size, order = parts[p]
        place = later[a].index(slot) + 1 if slot else 0
        if (a, slot) not in loaded:
            load(a, slot).wait()
            loaded.add((a, slot))
        for e in range(k):
            other = slot | order[e]
            copy(p, other, e, recvs[a].at[other - 1, pl.ds(start, size)]).wait_recv()
        target = sends[a].at[place - 1] if slot else o_refs[a]

        @pl.loop(0, size // 16)
        def _(t):
            part = pl.ds(pl.multiple_of(start + t * 16, 16), 16)
            total = owns[a][place, part].astype(f32)
            for e in range(k):
                total = total + recvs[a][(slot | order[e]) - 1, part].astype(f32)
            target[part] = total.astype(target.dtype)

    started = []
    first = [event for event in events if event[0] == 0]
    for index, (k, p, slot) in enumerate(events):
        a, start, size, order = parts[p]
        rows = pl.ds(start, size)
        if k == 0:
            src = x_refs[a].at[flip(me, slot), rows]
        else:
            add_up(p, slot, k)
            src = sends[a].at[later[a].index(slot), rows]
        sent = copy(p, slot, k, src)
        sent.start()
        started.append(sent)
        if index == len(first) // 2:
            for a in range(count):
                for own in [0] + later[a]:
                    load(a, own).start()
    for p in range(len(parts)):
        add_up(p, 0, bits)
    for sent in started:
        sent.wait_send()


def scatter_ctx(arrays, bits, collective):
    shapes = [item.shape[1:] for item in arrays]
    parts = all_parts(shapes, bits)
    parts = tuple((a, start, size, order[::-1]) for a, start, size, order in parts)
    events = scatter_events(parts, bits)
    count = len(arrays)
    others = (1 << bits) - 1
    held = [
        1 + len({s for k, p, s in events if k and parts[p][0] == a}) for a in range(count)
    ]
    return pl.pallas_call(
        functools.partial(scatter_kernel, parts, bits, events, count),
        name="scatter_ctx",
        out_shape=[jax.ShapeDtypeStruct(shape, f32) for shape in shapes],
        in_specs=[pl.BlockSpec(memory_space=pl.ANY)] * count,
        out_specs=[pl.BlockSpec(memory_space=pltpu.VMEM)] * count,
        scratch_shapes=[pltpu.VMEM((others,) + shape, bf16) for shape in shapes]
        + [pltpu.VMEM((n - 1,) + shape, bf16) for n, shape in zip(held, shapes)]
        + [pltpu.VMEM((n,) + shape, bf16) for n, shape in zip(held, shapes)]
        + [
            pltpu.SemaphoreType.DMA((len(parts), others)),
            pltpu.SemaphoreType.DMA((len(parts), others)),
            pltpu.SemaphoreType.DMA((count, max(held))),
        ],
        compiler_params=pltpu.CompilerParams(
            collective_id=collective, has_side_effects=True, vmem_limit_bytes=58 << 20
        ),
    )(*arrays)


def attend_kernel(block, count, q_ref, k_ref, v_ref, first_ref, wo_ref, o_ref, log_ref, part_ref):
    step = pl.program_id(0)
    for i in range(count):

        @pl.when(step == i)
        def _(i=i):
            extent = (i + 1) * block
            scores = dot_last(q_ref[...], k_ref[:extent, :])
            key_pos = lax.broadcasted_iota(jnp.int32, (block, extent), 1)
            query_pos = i * block + lax.broadcasted_iota(jnp.int32, (block, extent), 0)
            allowed = (key_pos >= first_ref[...]) & (key_pos <= query_pos)
            scores = jnp.where(allowed, scores, NEG)
            top = jnp.max(scores, axis=-1, keepdims=True)
            weights = jnp.exp(scores - top)
            total = jnp.sum(weights, axis=-1, keepdims=True)
            summed = dot(weights.astype(bf16), v_ref[:extent, :])
            o_ref[...] = summed / total
            column = jnp.broadcast_to(top + jnp.log(total), (block, 128))
            log_ref[...] = column.T[:1, :]
            part_ref[...] = dot((summed / total).astype(bf16), wo_ref[...]).astype(bf16)


def attend(queries, keys, values, first, w_output):
    length = queries.shape[0]
    block = min(256, length)
    count = length // block
    return pl.pallas_call(
        functools.partial(attend_kernel, block, count),
        name="attend",
        grid=(count,),
        out_shape=(
            jax.ShapeDtypeStruct((length, DV), f32),
            jax.ShapeDtypeStruct((1, length), f32),
            jax.ShapeDtypeStruct((length, D), bf16),
        ),
        in_specs=[
            pl.BlockSpec((block, WIDE), lambda i: (i, 0)),
            pl.BlockSpec((length, WIDE), lambda i: (0, 0)),
            pl.BlockSpec((length, DV), lambda i: (0, 0)),
            pl.BlockSpec((block, 1), lambda i: (i, 0)),
            pl.BlockSpec((DV, D), lambda i: (0, 0)),
        ],
        out_specs=(
            pl.BlockSpec((block, DV), lambda i: (i, 0)),
            pl.BlockSpec((1, block), lambda i: (0, i)),
            pl.BlockSpec((block, D), lambda i: (i, 0)),
        ),
        compiler_params=pltpu.CompilerParams(vmem_limit_bytes=60 << 20),
        cost_estimate=pl.CostEstimate(
            flops=length * length * (DN + DR + DV),
            bytes_accessed=length * 2000,
            transcendentals=length * length // 2,
        ),
    )(queries, keys, values, first, w_output)


def attend_back_kernel(
    block, count, q_ref, k_ref, v_ref, m_ref, att_ref, wo_ref, first_ref, log_ref,
    *refs,
):
    lows, (dq_ref, dk_ref, dv_ref, gwo_ref), wides = refs[:3], refs[3:7], refs[7:]
    step = pl.program_id(0)
    for low_ref, wide_ref in zip(lows, wides):
        wide_ref[...] = low_ref[...].astype(f32)

    @pl.when(step == 0)
    def _():
        dk_ref[...] = jnp.zeros_like(dk_ref)
        dv_ref[...] = jnp.zeros_like(dv_ref)
        gwo_ref[...] = jnp.zeros_like(gwo_ref)

    grad = dot_last(m_ref[...], wo_ref[...]).astype(bf16)
    gwo_ref[...] += dot_first(att_ref[...].astype(bf16), m_ref[...])
    delta = jnp.sum((grad.astype(f32) * att_ref[...]).T, axis=0, keepdims=True)
    for i in range(count):

        @pl.when(step == i)
        def _(i=i):
            extent = (i + 1) * block
            keys = k_ref[:extent, :]
            scores = dot_last(keys, q_ref[...])
            key_pos = lax.broadcasted_iota(jnp.int32, (extent, block), 0)
            query_pos = i * block + lax.broadcasted_iota(jnp.int32, (extent, block), 1)
            allowed = (key_pos >= first_ref[...]) & (key_pos <= query_pos)
            weights = jnp.where(allowed, jnp.exp(scores - log_ref[...]), 0.0)
            grad_weights = dot_last(v_ref[:extent, :], grad)
            grad_scores = (weights * (grad_weights - delta)).astype(bf16)
            dv_ref[:extent, :] += dot(weights.astype(bf16), grad)
            dk_ref[:extent, :] += dot(grad_scores, q_ref[...])
            dq_ref[...] = dot_first(grad_scores, keys)


def attend_back(queries, keys, values, grad_mixed, attended, w_output, first, log_total, lows):
    length = queries.shape[0]
    block = min(256, length)
    count = length // block
    row = lambda: pl.BlockSpec((1, block), lambda i: (0, i))
    whole = lambda height, width: pl.BlockSpec((height, width), lambda i: (0, 0))
    part = lambda width: pl.BlockSpec((block, width), lambda i: (i, 0))
    tall, wide = lows[0].shape
    piece = 176 if tall % 176 == 0 else tall
    steps = tall // piece
    some = pl.BlockSpec((piece, wide), lambda i: (i * steps // count, 0))
    return pl.pallas_call(
        functools.partial(attend_back_kernel, block, count),
        name="attend_back",
        grid=(count,),
        out_shape=(
            jax.ShapeDtypeStruct((length, WIDE), f32),
            jax.ShapeDtypeStruct((length, WIDE), f32),
            jax.ShapeDtypeStruct((length, DV), f32),
            jax.ShapeDtypeStruct((DV, D), f32),
        )
        + tuple(jax.ShapeDtypeStruct((tall, wide), f32) for _ in lows),
        in_specs=[
            part(WIDE),
            whole(length, WIDE),
            whole(length, DV),
            part(D),
            part(DV),
            whole(DV, D),
            row(),
            row(),
        ]
        + [some] * 3,
        out_specs=(part(WIDE), whole(length, WIDE), whole(length, DV), whole(DV, D)) + (some,) * 3,
        compiler_params=pltpu.CompilerParams(vmem_limit_bytes=60 << 20),
        cost_estimate=pl.CostEstimate(
            flops=length * length * (3 * (DN + DR) + 2 * DV),
            bytes_accessed=length * 4000,
            transcendentals=length * length // 2,
        ),
    )(queries, keys, values, grad_mixed, attended, w_output, first, log_total, *lows)


def lanes_of(value):
    return lax.broadcasted_iota(jnp.int32, value.shape, len(value.shape) - 1)


def swap_lanes(ropes):
    return jnp.where(
        lanes_of(ropes) % DR < DR // 2, -pltpu.roll(ropes, 96, 1), pltpu.roll(ropes, 32, 1)
    )


def assemble_kernel(
    cycle, slab, mine_ref, other_ref, mine_n_ref, other_n_ref,
    w_ref, we_ref, gains_ref, narrow_ref, expand_ref,
):
    me = lax.axis_index("fsdp")
    for f, (pack_ref, slim_ref) in enumerate(((mine_ref, mine_n_ref), (other_ref, other_n_ref))):
        owner = me if f == 0 else 1 - me

        @pl.loop(0, cycle)
        def _(c):
            rows = pl.ds(pl.multiple_of((c * 2 + owner) * slab, slab), slab)
            w_ref[rows, :DN] = pack_ref[c, :, :DN]
            w_ref[rows, 3 * DN :] = slim_ref[c, :, :KVR]
            tail = pack_ref[c, :, DN:256].astype(f32)
            slim = slim_ref[c, :, KVR:].astype(f32)
            ropes = jnp.where(lanes_of(tail) < DR, tail, pltpu.roll(slim, DR, 1))
            w_ref[rows, DN : 2 * DN] = ropes.astype(bf16)
            w_ref[rows, 2 * DN : 3 * DN] = swap_lanes(ropes).astype(bf16)
            narrow_ref[rows, :] = slim
            quarter = slab // 4
            for q in range(2):
                left = tail[2 * q * quarter : (2 * q + 1) * quarter]
                right = tail[(2 * q + 1) * quarter : (2 * q + 2) * quarter]
                both = jnp.where(lanes_of(left) < DR, pltpu.roll(left, DR, 1), right)
                spot = pl.ds(pl.multiple_of((c * 2 + owner) * quarter, quarter), quarter)
                expand_ref[spot, q * DN : (q + 1) * DN] = both

    we_ref[...] = expand_ref[...].astype(bf16)
    gains_ref[...] = narrow_ref[...].T[DR : DR + 8, :]


def assemble(mine, other, mine_n, other_n):
    cycle, slab, _ = mine.shape
    return pl.pallas_call(
        functools.partial(assemble_kernel, cycle, slab),
        name="assemble",
        out_shape=(
            jax.ShapeDtypeStruct((D, 3 * DN + KVR), bf16),
            jax.ShapeDtypeStruct((KVR, DN + DV), bf16),
            jax.ShapeDtypeStruct((8, D), f32),
        ),
        scratch_shapes=[pltpu.VMEM((D, DN), f32), pltpu.VMEM((KVR, DN + DV), f32)],
        compiler_params=pltpu.CompilerParams(vmem_limit_bytes=60 << 20),
    )(mine, other, mine_n, other_n)


def finish_kernel(
    cycle, slab, gw_ref, gwe_ref, w_ref, we_ref, extra_ref, first_ref, slim_ref,
    away_first, away_slim, got_first, got_slim, send_sem, recv_sem,
):
    me = lax.axis_index("fsdp")
    quarter = slab // 4
    barrier = pltpu.get_barrier_semaphore()
    pl.semaphore_signal(barrier, inc=1, device_id={"fsdp": 1 - me}, device_id_type=MESH)

    def by_slab(owner, first_out, slim_out):
        @pl.loop(0, cycle)
        def _(c):
            rows = pl.ds(pl.multiple_of((c * 2 + owner) * slab, slab), slab)
            some = pl.ds(pl.multiple_of((c * 2 + owner) * quarter, quarter), quarter)
            grad, expand = gw_ref[rows, :], gwe_ref[some, :]
            ropes = grad[:, DN : 2 * DN] - swap_lanes(grad[:, 2 * DN : 3 * DN])
            gain_one = jnp.sum(grad * w_ref[rows, :].astype(f32), axis=1, keepdims=True)
            gain_latent = jnp.sum(expand * we_ref[some, :].astype(f32), axis=1, keepdims=True)
            lanes = lanes_of(ropes)
            tail = jnp.where(lanes < DR, pltpu.roll(ropes, DR, 1), 0.0)
            tail = jnp.where(lanes == DR, gain_one, tail)
            tail = jnp.where(lanes == DR + 1, extra_ref[rows, :], tail)
            column = jnp.concatenate([gain_latent, jnp.zeros((slab - quarter, 1), f32)], axis=0)
            tail = jnp.where(lanes == DR + 2, column, tail)
            pieces = jnp.concatenate(
                [
                    pltpu.roll(expand[:, :DN], DR, 1),
                    expand[:, :DN],
                    pltpu.roll(expand[:, DN:], DR, 1),
                    expand[:, DN:],
                ],
                axis=0,
            )
            first_out[c, :, :DN] = grad[:, :DN].astype(bf16)
            first_out[c, :, DN:] = jnp.where(lanes < DR, ropes, pieces).astype(bf16)
            slim_out[c, :, :KVR] = grad[:, 3 * DN :].astype(bf16)
            slim_out[c, :, KVR:] = tail.astype(bf16)

    by_slab(1 - me, away_first, away_slim)
    pl.semaphore_wait(barrier, 1)
    copies = [
        pltpu.make_async_remote_copy(
            src_ref=src,
            dst_ref=dst,
            send_sem=send_sem.at[i],
            recv_sem=recv_sem.at[i],
            device_id={"fsdp": 1 - me},
            device_id_type=MESH,
        )
        for i, (src, dst) in enumerate(((away_first, got_first), (away_slim, got_slim)))
    ]
    for item in copies:
        item.start()
    by_slab(me, first_ref, slim_ref)
    for item in copies:
        item.wait()

    @pl.loop(0, cycle)
    def _(c):
        first_ref[c] = (first_ref[c].astype(f32) + got_first[c].astype(f32)).astype(bf16)
        slim_ref[c] = (slim_ref[c].astype(f32) + got_slim[c].astype(f32)).astype(bf16)


def finish(grad_w, grad_we, w_cat, w_expand, extra, cycle, slab, collective):
    shapes = [(cycle, slab, 256), (cycle, slab, KVR + DN)]
    return pl.pallas_call(
        functools.partial(finish_kernel, cycle, slab),
        name="finish",
        out_shape=tuple(jax.ShapeDtypeStruct(shape, bf16) for shape in shapes),
        in_specs=[pl.BlockSpec(memory_space=pltpu.VMEM)] * 5,
        out_specs=(pl.BlockSpec(memory_space=pltpu.VMEM),) * 2,
        scratch_shapes=[pltpu.VMEM(shape, bf16) for shape in shapes * 2]
        + [pltpu.SemaphoreType.DMA((2,)), pltpu.SemaphoreType.DMA((2,))],
        compiler_params=pltpu.CompilerParams(
            collective_id=collective, has_side_effects=True, vmem_limit_bytes=60 << 20
        ),
    )(grad_w, grad_we, w_cat, w_expand, extra)


def place_lanes(out_ref, pieces, width):
    total = width * len(pieces)
    for start in range(0, total, DN):
        tile = None
        for c in range(start // width, min(len(pieces), -(-(start + DN) // width))):
            moved = pieces[c]
            shift = (c * width - start) % 256
            if shift:
                moved = pltpu.roll(moved, shift, 1)
            moved = moved[:, :DN]
            lanes = lanes_of(moved) + start
            inside = (lanes >= c * width) & (lanes < (c + 1) * width)
            tile = jnp.where(inside, moved, 0.0 if tile is None else tile)
        out_ref[:, start : start + DN] = tile


def spread_kernel(cycle, slab, pack_ref, pack_s_ref, gq_ref, gwe_ref, gg_ref, gu_ref):
    quarter = slab // 4
    for ref, out_ref, start in (
        (pack_ref, gq_ref, 0),
        (pack_s_ref, gg_ref, 0),
        (pack_s_ref, gu_ref, 256),
    ):
        pieces = [ref[c, :, start : start + 256].astype(f32) for c in range(cycle)]
        place_lanes(out_ref, pieces, out_ref.shape[1] // cycle)
    for c in range(cycle):
        tail = pack_ref[c, :, DN:256].astype(f32)
        for q in range(2):
            left = tail[2 * q * quarter : (2 * q + 1) * quarter]
            right = tail[(2 * q + 1) * quarter : (2 * q + 2) * quarter]
            both = jnp.where(lanes_of(left) < DR, pltpu.roll(left, DR, 1), right)
            at = c * 2 * DN + q * DN
            gwe_ref[:, at : at + DN] = both


def spread(packed, packed_s, widths):
    cycle, slab, _ = packed.shape
    return pl.pallas_call(
        functools.partial(spread_kernel, cycle, slab),
        name="spread",
        out_shape=(
            jax.ShapeDtypeStruct((slab, widths[0]), f32),
            jax.ShapeDtypeStruct((slab // 4, widths[1]), f32),
            jax.ShapeDtypeStruct((slab, widths[2]), f32),
            jax.ShapeDtypeStruct((slab, widths[3]), f32),
        ),
        compiler_params=pltpu.CompilerParams(vmem_limit_bytes=60 << 20),
    )(packed, packed_s)


def fixed(shape):
    return pl.BlockSpec(shape, lambda i: (0,) * len(shape), pipeline_mode=pl.Buffered(1))


def second(shape):
    return pl.BlockSpec(shape, lambda i: (0, 1), pipeline_mode=pl.Buffered(1))


def by_rows(rows, cols):
    return pl.BlockSpec((rows, cols), lambda i: (i, 0))


def project_kernel(
    scale, x_ref, gain_ref, w_ref, gain_l_ref, we_ref, cos_ref, sin_ref,
    act_ref, q_ref, k_ref, v_ref, latent_ref, raw_ref,
):
    act = norm_forward(x_ref[...].astype(f32), gain_ref[...])[0].astype(bf16)
    act_ref[...] = act
    raw = dot(act, w_ref[...])
    turned = raw[:, DN : 2 * DN] * cos_ref[...] + raw[:, 2 * DN : 3 * DN] * sin_ref[...]
    low = lax.broadcasted_iota(jnp.int32, turned.shape, 1) < DR
    q_ref[:, :DN] = (raw[:, :DN] * scale).astype(bf16)
    q_ref[:, DN:] = jnp.where(low, turned * scale, 0.0).astype(bf16)
    raw_latent = raw[:, 3 * DN :]
    raw_ref[...] = raw_latent
    latent = norm_forward(raw_latent, gain_l_ref[...])[0].astype(bf16)
    latent_ref[...] = latent
    expanded = dot(latent, we_ref[...]).astype(bf16)
    k_ref[:, :DN] = expanded[:, :DN]
    k_ref[:, DN:] = jnp.where(low, pltpu.roll(turned, DR, 1), 0.0).astype(bf16)
    v_ref[...] = expanded[:, DN:]


def project(x, gain, w_cat, gain_latent, w_expand, cosine, sine, scale):
    length = x.shape[0]
    block = min(512, length)
    width = w_cat.shape[1]
    return pl.pallas_call(
        functools.partial(project_kernel, scale),
        name="project",
        grid=(length // block,),
        out_shape=(
            jax.ShapeDtypeStruct((length, D), bf16),
            jax.ShapeDtypeStruct((length, WIDE), bf16),
            jax.ShapeDtypeStruct((length, WIDE), bf16),
            jax.ShapeDtypeStruct((length, DV), bf16),
            jax.ShapeDtypeStruct((length, KVR), bf16),
            jax.ShapeDtypeStruct((length, KVR), f32),
        ),
        in_specs=[
            by_rows(block, D),
            fixed((1, D)),
            fixed((D, width)),
            fixed((1, KVR)),
            fixed((KVR, DN + DV)),
            by_rows(block, DN),
            by_rows(block, DN),
        ],
        out_specs=(
            by_rows(block, D),
            by_rows(block, WIDE),
            by_rows(block, WIDE),
            by_rows(block, DV),
            by_rows(block, KVR),
            by_rows(block, KVR),
        ),
        compiler_params=pltpu.CompilerParams(vmem_limit_bytes=60 << 20),
        cost_estimate=pl.CostEstimate(
            flops=2 * length * D * width, bytes_accessed=length * D * 6, transcendentals=0
        ),
    )(x, gain[None, :], w_cat, gain_latent[None, :], w_expand, cosine, sine)


def project_back_kernel(
    scale, copies, dq_ref, dk_ref, dv_ref, raw_ref, latent_ref, act_ref, cos_ref, sin_ref,
    we_ref, gain_l_ref, keep_q_ref, keep_e_ref, grads_ref, gw_ref, gwe_ref,
):
    @pl.when(pl.program_id(0) == 0)
    def _():
        gw_ref[...] = jnp.zeros_like(gw_ref)
        gwe_ref[...] = jnp.zeros_like(gwe_ref)

    grad_q = dq_ref[...] * scale
    grad_k = dk_ref[:, :DN]
    grad_v = dv_ref[...]
    if copies > 1:
        grad_q = grad_q * keep_q_ref[...]
        grad_k = grad_k * keep_e_ref[:, :DN]
        grad_v = grad_v * keep_e_ref[:, DN:]
    rope_q = grad_q[:, DN:]
    low = lax.broadcasted_iota(jnp.int32, rope_q.shape, 1) < DR
    rope_k = jnp.where(low, dk_ref[:, DN:] * (1.0 / copies), 0.0)
    ropes = jnp.where(low, rope_q, pltpu.roll(rope_k, DR, 1))
    expanded = jnp.concatenate([grad_k, grad_v], axis=-1).astype(bf16)
    grad_latent = dot_last(expanded, we_ref[...])
    raw = raw_ref[...]
    factor = lax.rsqrt(jnp.mean(raw * raw, axis=-1, keepdims=True) + EPS)
    grad_latent = norm_back_rows(raw, factor, gain_l_ref[...], grad_latent)
    grads = jnp.concatenate(
        [
            grad_q[:, :DN].astype(bf16),
            (ropes * cos_ref[...]).astype(bf16),
            (ropes * sin_ref[...]).astype(bf16),
            grad_latent.astype(bf16),
        ],
        axis=-1,
    )
    grads_ref[...] = grads
    gw_ref[...] += dot_first(act_ref[...], grads)
    gwe_ref[...] += dot_first(latent_ref[...], expanded)


def project_back(
    grad_q, grad_k, grad_v, raw, latent, act, cosine, sine, w_expand, gain_latent, keep_q,
    keep_e, scale, copies,
):
    length = act.shape[0]
    block = min(512, length)
    width = 3 * DN + KVR
    return pl.pallas_call(
        functools.partial(project_back_kernel, scale, copies),
        name="project_back",
        grid=(length // block,),
        out_shape=(
            jax.ShapeDtypeStruct((length, width), bf16),
            jax.ShapeDtypeStruct((D, width), f32),
            jax.ShapeDtypeStruct((KVR, DN + DV), f32),
        ),
        in_specs=[
            by_rows(block, WIDE),
            by_rows(block, WIDE),
            by_rows(block, DV),
            by_rows(block, KVR),
            by_rows(block, KVR),
            by_rows(block, D),
            by_rows(block, DN),
            by_rows(block, DN),
            fixed((KVR, DN + DV)),
            fixed((1, KVR)),
            fixed((1, WIDE)),
            fixed((1, DN + DV)),
        ],
        out_specs=(
            by_rows(block, width),
            pl.BlockSpec((D, width), lambda i: (0, 0)),
            pl.BlockSpec((KVR, DN + DV), lambda i: (0, 0)),
        ),
        compiler_params=pltpu.CompilerParams(vmem_limit_bytes=60 << 20),
        cost_estimate=pl.CostEstimate(
            flops=4 * length * D * width, bytes_accessed=length * D * 6, transcendentals=0
        ),
    )(
        grad_q, grad_k, grad_v, raw, latent, act, cosine, sine, w_expand, gain_latent[None, :],
        keep_q, keep_e,
    )


def rows_kernel(grads_ref, w_ref, part_ref):
    part_ref[...] = dot_last(grads_ref[...], w_ref[...]).astype(bf16)


def project_back_rows(grads, w_cat):
    length, width = grads.shape
    block = min(512, length)
    return pl.pallas_call(
        rows_kernel,
        name="project_back_rows",
        grid=(length // block,),
        out_shape=jax.ShapeDtypeStruct((length, D), bf16),
        in_specs=[by_rows(block, width), fixed((D, width))],
        out_specs=by_rows(block, D),
        compiler_params=pltpu.CompilerParams(vmem_limit_bytes=60 << 20),
        cost_estimate=pl.CostEstimate(
            flops=2 * length * D * width, bytes_accessed=length * D * 4, transcendentals=0
        ),
    )(grads, w_cat)


class Gather:
    def __init__(self, parts, bits, events, x_ref, o_ref, send_sem, recv_sem, own_sem):
        self.parts, self.bits, self.events = parts, bits, events
        self.x_ref, self.o_ref = x_ref, o_ref
        self.send_sem, self.recv_sem = send_sem, recv_sem
        self.me = lax.axis_index("ctx")
        self.own = pltpu.make_async_copy(x_ref, o_ref.at[self.me], own_sem)
        self.seen = set()
        self.started = []

    def send(self, index):
        _, _, p, slot, bit = self.events[index]
        if slot:
            self.arrived(p, slot)
        _, start, size, _ = self.parts[p]
        rows = pl.ds(start, size)
        block = flip(self.me, slot)
        item = pltpu.make_async_remote_copy(
            src_ref=self.x_ref.at[rows] if slot == 0 else self.o_ref.at[block, rows],
            dst_ref=self.o_ref.at[block, rows],
            send_sem=self.send_sem.at[index],
            recv_sem=self.recv_sem.at[p, slot ^ bit],
            device_id={"ctx": flip(self.me, bit)},
            device_id_type=MESH,
        )
        item.start()
        self.started.append(item)

    def arrived(self, p, slot):
        if (p, slot) in self.seen:
            return
        self.seen.add((p, slot))
        _, start, size, order = self.parts[p]
        rows = pl.ds(start, size)
        bit = [b for b in order if slot & b][-1]
        pltpu.make_async_remote_copy(
            src_ref=self.x_ref.at[rows],
            dst_ref=self.o_ref.at[flip(self.me, slot), rows],
            send_sem=self.send_sem.at[0],
            recv_sem=self.recv_sem.at[p, slot],
            device_id={"ctx": flip(self.me, bit)},
            device_id_type=MESH,
        ).wait_recv()

    def block(self, slot):
        if slot == 0:
            return self.x_ref
        for p in range(len(self.parts)):
            self.arrived(p, slot)
        return self.o_ref.at[flip(self.me, slot)]

    def finish(self):
        for slot in range(1, 1 << self.bits):
            self.block(slot)
        for item in self.started:
            item.wait_send()
        self.own.wait()


def gather_order(parts, bits, events, span):
    at = {}
    for index, (_, _, p, slot, bit) in enumerate(events):
        at[p, slot ^ bit] = span * (index + 1) / len(events)
    whole = {0: 0.0}
    for slot in range(1, 1 << bits):
        whole[slot] = max(at[p, slot] for p in range(len(parts)))
    return whole, at


def gather_plan(parts, bits, events, span, size, pieces, cost):
    whole, at = gather_order(parts, bits, events, span)
    slots = sorted(whole, key=lambda slot: (whole[slot], slot))
    groups = [slots[i : i + size] for i in range(0, len(slots), size)]
    ready = [max(whole[slot] for slot in group) for group in groups]
    work = [(g, k) for g in range(len(groups)) for k in range(pieces)]
    plan, now, e, w = [], 0.0, 0, 0
    while e < len(events) or w < len(work):
        _, _, p, slot, _ = events[e] if e < len(events) else (0, 0, 0, 0, 0)
        when = (at[p, slot] if slot else 0.0) if e < len(events) else math.inf
        then = ready[work[w][0]] if w < len(work) else math.inf
        if when <= now or when <= then:
            plan.append(("send", e))
            now = max(now, when) + 0.1
            e += 1
        else:
            plan.append(("work", work[w]))
            now = max(now, then) + cost / pieces
            w += 1
    return groups, plan


def expert_sizes(capacity, tokens, cycle):
    unit = 1
    while unit * capacity % 16:
        unit *= 2
    blocks = max(4, unit)
    return unit, blocks


def pick_rows(me, slots, unit, capacity, row_ref):
    tokens = row_ref.shape[2]
    places = []
    for q, slot in enumerate(slots):
        place = row_ref[flip(me, slot)]
        places.append(jnp.where(place >= 0, place + q * capacity, -1))
    place = jnp.concatenate(places, axis=1)
    shape = (unit * capacity, unit * tokens)
    return lax.broadcasted_iota(jnp.int32, shape, 0) == place


def as_bf16(mask):
    return mask.astype(f32).astype(bf16)


def experts_kernel(
    groups, plan, parts, bits, events, shares, unit, capacity, x_ref, row_ref, prob_ref, *refs
):
    weights, both_ref, down_ref = refs[: 3 * shares], refs[3 * shares], refs[3 * shares + 1]
    refs = refs[3 * shares + 2 :]
    o_ref, part_out, rows_out, gs_out, us_out, hs_out = refs[:6]
    kept_out, refs = refs[6 : 6 + 3 * shares], refs[6 + 3 * shares :]
    w, wb, wd, xg, rows, part, shared, kept = refs[:8]
    send_sem, recv_sem, own_sem, w_sem, x_sem, out_sem, part_sem = refs[8:]
    me = lax.axis_index("ctx")
    tokens = x_ref.shape[0]
    size = len(groups[0])
    tall, short = unit * tokens, unit * capacity
    width = wd.shape[0]
    gather = Gather(parts, bits, events, x_ref, o_ref, send_sem, recv_sem, own_sem)
    gather.own.start()
    loads = [pltpu.make_async_copy(weights[i], w.at[i], w_sem.at[i]) for i in range(3 * shares)]
    loads.append(pltpu.make_async_copy(both_ref, wb, w_sem.at[3 * shares]))
    loads.append(pltpu.make_async_copy(down_ref, wd, w_sem.at[3 * shares + 1]))
    greet(bits)
    ready = set()

    def need(i):
        if i not in ready:
            loads[i].wait()
            ready.add(i)
        return w[i] if i < 3 * shares else (wb if i == 3 * shares else wd)

    def outs(g):
        span = pl.ds(g * size * capacity, size * capacity)
        wide = pl.ds(g * size * tokens, size * tokens)
        items = [pltpu.make_async_copy(rows, rows_out.at[span], out_sem.at[0])]
        for i, ref in enumerate((gs_out, us_out, hs_out)):
            items.append(pltpu.make_async_copy(shared.at[i], ref.at[wide], out_sem.at[1 + i]))
        for i in range(3 * shares):
            items.append(
                pltpu.make_async_copy(kept.at[i], kept_out[i].at[span], out_sem.at[4 + i])
            )
        return items

    def part_outs(g, first=0, count=size):
        return [
            pltpu.make_async_copy(
                part.at[pl.ds(q * tokens, tokens)],
                part_out.at[flip(me, groups[g][q])],
                part_sem.at[q],
            )
            for q in range(first, first + count)
        ]

    state = {}

    def begin(g):
        copies = [
            pltpu.make_async_copy(
                gather.block(slot), xg.at[pl.ds(q * tokens, tokens)], x_sem.at[q]
            )
            for q, slot in enumerate(groups[g])
        ]
        for item in copies:
            item.start()
        if g:
            for item in outs(g - 1):
                item.wait()
        picks, scales = [], []
        for j in range(size // unit):
            slots = groups[g][j * unit : (j + 1) * unit]
            mask = pick_rows(me, slots, unit, capacity, row_ref)
            prob = jnp.concatenate([prob_ref[flip(me, slot)] for slot in slots], axis=1)
            scales.append(jnp.sum(jnp.where(mask, prob, 0.0), axis=1, keepdims=True))
            picks.append(as_bf16(mask))
        for item in copies:
            item.wait()
        for j, pick in enumerate(picks):
            chosen = dot(pick, xg[j * tall : (j + 1) * tall, :]).astype(bf16)
            rows[j * short : (j + 1) * short, :] = chosen
        state.update(picks=picks, scale=jnp.concatenate(scales, axis=0), total=0.0)

    def gate(s):
        state["gate"] = dot_last(rows[...], need(3 * s))

    def up(s):
        gated, upper = state["gate"], dot_last(rows[...], need(3 * s + 1))
        hidden = (gated * jax.nn.sigmoid(gated) * upper).astype(bf16)
        for i, value in enumerate((gated, upper, hidden)):
            kept[3 * s + i] = value.astype(bf16)

    def down(s):
        state["total"] = state["total"] + dot(kept[3 * s + 2], need(3 * s + 2))

    def shared_hidden(g):
        gated = dot(xg[...], need(3 * shares)[:, :width])
        upper = dot(xg[...], need(3 * shares)[:, width:])
        hidden = (gated * jax.nn.sigmoid(gated) * upper).astype(bf16)
        for i, value in enumerate((gated, upper, hidden)):
            shared[i] = value.astype(bf16)
        state["rows"] = (state["total"] * state["scale"]).astype(bf16)
        for item in outs(g):
            item.start()
        if g:
            for item in part_outs(g - 1):
                item.wait()

    def combine(g, j):
        inside = slice(j * tall, (j + 1) * tall)
        part[inside, :] = (
            dot_first(state["picks"][j], state["rows"][j * short : (j + 1) * short, :])
            + dot(shared[2, inside, :], need(3 * shares + 1)[...])
        ).astype(bf16)
        for item in part_outs(g, j * unit, unit):
            item.start()

    def piece(g, k):
        if k == 0:
            begin(g)
        elif k <= 3 * shares:
            (gate, up, down)[(k - 1) % 3]((k - 1) // 3)
        elif k == 3 * shares + 1:
            shared_hidden(g)
        else:
            combine(g, k - 3 * shares - 2)

    sent = 0
    for kind, item in plan:
        if kind == "send":
            gather.send(item)
            sent += 1
            if sent == bits * len(parts):
                for load in loads:
                    load.start()
        else:
            piece(*item)
    gather.finish()
    for item in outs(len(groups) - 1) + part_outs(len(groups) - 1):
        item.wait()


def experts(x, place, prob, weights, shared, capacity, bits, collective):
    tokens = x.shape[0]
    cycle = 1 << bits
    unit, size = expert_sizes(capacity, tokens, cycle)
    parts = all_parts([x.shape], bits)
    events = gather_events(parts, bits)
    shares = len(weights) // 3
    half = weights[0].shape[0]
    width = shared[1].shape[0]
    pieces = 3 * shares + 2 + size // unit
    groups, plan = gather_plan(parts, bits, events, 90.0, size, pieces, 10.5)
    anywhere = pl.BlockSpec(memory_space=pl.ANY)
    inside = pl.BlockSpec(memory_space=pltpu.VMEM)
    return pl.pallas_call(
        functools.partial(
            experts_kernel, groups, plan, parts, bits, events, shares, unit, capacity
        ),
        name="experts",
        out_shape=[
            jax.ShapeDtypeStruct((cycle, tokens, D), bf16),
            jax.ShapeDtypeStruct((cycle, tokens, D), bf16),
            jax.ShapeDtypeStruct((cycle * capacity, D), bf16),
        ]
        + [jax.ShapeDtypeStruct((cycle * tokens, width), bf16)] * 3
        + [jax.ShapeDtypeStruct((cycle * capacity, half), bf16)] * (3 * shares),
        in_specs=[anywhere, inside, inside] + [anywhere] * (3 * shares + 2),
        out_specs=[anywhere] * (6 + 3 * shares),
        scratch_shapes=[
            pltpu.VMEM((3 * shares, half, D), bf16),
            pltpu.VMEM((D, 2 * width), bf16),
            pltpu.VMEM((width, D), bf16),
            pltpu.VMEM((size * tokens, D), bf16),
            pltpu.VMEM((size * capacity, D), bf16),
            pltpu.VMEM((size * tokens, D), bf16),
            pltpu.VMEM((3, size * tokens, width), bf16),
            pltpu.VMEM((3 * shares, size * capacity, half), bf16),
            pltpu.SemaphoreType.DMA((len(events),)),
            pltpu.SemaphoreType.DMA((len(parts), cycle)),
            pltpu.SemaphoreType.DMA,
            pltpu.SemaphoreType.DMA((3 * shares + 2,)),
            pltpu.SemaphoreType.DMA((size,)),
            pltpu.SemaphoreType.DMA((4 + 3 * shares,)),
            pltpu.SemaphoreType.DMA((size,)),
        ],
        compiler_params=pltpu.CompilerParams(
            collective_id=collective, has_side_effects=True, vmem_limit_bytes=60 << 20
        ),
    )(x, place, prob, *weights, *shared)


def experts_back_kernel(
    groups, plan, parts, bits, events, shares, unit, capacity, x_ref, act_ref, row_ref, prob_ref,
    gs_in, us_in, hs_in, *refs,
):
    kept_in, refs = refs[: 2 * shares], refs[2 * shares :]
    weights, both_ref, down_ref = refs[: 3 * shares], refs[3 * shares], refs[3 * shares + 1]
    refs = refs[3 * shares + 2 :]
    o_ref, part_out, dy_out = refs[:3]
    grads_out, refs = refs[3 : 3 + 2 * shares], refs[3 + 2 * shares :]
    gws_ref, gwd_ref = refs[:2]
    w, wb, wd, dg, ag, dy, part, shared, kept, grads, gwg, gwu = refs[2:14]
    send_sem, recv_sem, own_sem, w_sem, x_sem, a_sem, k_sem, out_sem, part_sem = refs[14:]
    me = lax.axis_index("ctx")
    tokens = x_ref.shape[0]
    size = len(groups[0])
    tall, short = unit * tokens, unit * capacity
    width = wd.shape[0]
    gather = Gather(parts, bits, events, x_ref, o_ref, send_sem, recv_sem, own_sem)
    gather.own.start()
    loads = [pltpu.make_async_copy(weights[i], w.at[i], w_sem.at[i]) for i in range(3 * shares)]
    loads.append(pltpu.make_async_copy(both_ref, wb, w_sem.at[3 * shares]))
    loads.append(pltpu.make_async_copy(down_ref, wd, w_sem.at[3 * shares + 1]))
    greet(bits)
    for ref in (gwg, gwu, gwd_ref):
        ref[...] = jnp.zeros_like(ref)
    ready = set()

    def need(i):
        if i not in ready:
            loads[i].wait()
            ready.add(i)
        return w[i] if i < 3 * shares else (wb if i == 3 * shares else wd)

    def old(g):
        span = pl.ds(g * size * capacity, size * capacity)
        wide = pl.ds(g * size * tokens, size * tokens)
        items = [
            pltpu.make_async_copy(
                act_ref.at[flip(me, slot)], ag.at[pl.ds(q * tokens, tokens)], a_sem.at[q]
            )
            for q, slot in enumerate(groups[g])
        ]
        for i, ref in enumerate((gs_in, us_in, hs_in)):
            items.append(pltpu.make_async_copy(ref.at[wide], shared.at[i], k_sem.at[i]))
        for i in range(2 * shares):
            items.append(pltpu.make_async_copy(kept_in[i].at[span], kept.at[i], k_sem.at[3 + i]))
        return items

    def outs(g):
        span = pl.ds(g * size * capacity, size * capacity)
        items = [pltpu.make_async_copy(dy, dy_out.at[span], out_sem.at[0])]
        for i in range(2 * shares):
            items.append(
                pltpu.make_async_copy(grads.at[i], grads_out[i].at[span], out_sem.at[1 + i])
            )
        return items

    def part_outs(g, first=0, count=size):
        return [
            pltpu.make_async_copy(
                part.at[pl.ds(q * tokens, tokens)],
                part_out.at[flip(me, groups[g][q])],
                part_sem.at[q],
            )
            for q in range(first, first + count)
        ]

    state = {}

    def begin(g):
        copies = [
            pltpu.make_async_copy(
                gather.block(slot), dg.at[pl.ds(q * tokens, tokens)], x_sem.at[q]
            )
            for q, slot in enumerate(groups[g])
        ]
        for item in copies:
            item.start()
        if g:
            for item in outs(g - 1):
                item.wait()
        picks, scales = [], []
        for j in range(size // unit):
            slots = groups[g][j * unit : (j + 1) * unit]
            mask = pick_rows(me, slots, unit, capacity, row_ref)
            prob = jnp.concatenate([prob_ref[flip(me, slot)] for slot in slots], axis=1)
            scales.append(jnp.sum(jnp.where(mask, prob, 0.0), axis=1, keepdims=True))
            picks.append(as_bf16(mask))
        for item in copies:
            item.wait()
        for j, pick in enumerate(picks):
            chosen = dot(pick, dg[j * tall : (j + 1) * tall, :]) * scales[j]
            dy[j * short : (j + 1) * short, :] = chosen.astype(bf16)
        for item in old(g):
            item.wait()
        state.update(picks=picks, total=0.0)

    def hidden_back(s):
        grad_hidden = dot_last(dy[...], need(3 * s + 2))
        grad_gate, grad_up = silu_grads(
            kept[2 * s].astype(f32), kept[2 * s + 1].astype(f32), grad_hidden
        )
        grads[2 * s] = grad_gate
        grads[2 * s + 1] = grad_up

    def rows_back(s, i):
        state["total"] = state["total"] + dot(grads[2 * s + i], need(3 * s + i))

    def shared_back(g):
        for item in outs(g):
            item.start()
        grad_hidden = dot_last(dg[...], need(3 * shares + 1)[...])
        grad_gate, grad_up = silu_grads(
            shared[0].astype(f32), shared[1].astype(f32), grad_hidden
        )
        gwg[...] += dot_first(grad_gate, ag[...])
        state.update(gate=grad_gate, up=grad_up, rows=state["total"].astype(bf16))

    def shared_more(g):
        gwu[...] += dot_first(state["up"], ag[...])
        gwd_ref[...] += dot_first(shared[2], dg[...])
        if g + 1 < len(groups):
            for item in old(g + 1):
                item.start()
        if g:
            for item in part_outs(g - 1):
                item.wait()

    def combine(g, j):
        inside = slice(j * tall, (j + 1) * tall)
        both = need(3 * shares)
        part[inside, :] = (
            dot_first(state["picks"][j], state["rows"][j * short : (j + 1) * short, :])
            + dot_last(state["gate"][inside, :], both[:, :width])
            + dot_last(state["up"][inside, :], both[:, width:])
        ).astype(bf16)
        for item in part_outs(g, j * unit, unit):
            item.start()

    def piece(g, k):
        if k == 0:
            begin(g)
        elif k <= 3 * shares:
            s, i = (k - 1) // 3, (k - 1) % 3
            hidden_back(s) if i == 0 else rows_back(s, i - 1)
        elif k == 3 * shares + 1:
            shared_back(g)
        elif k == 3 * shares + 2:
            shared_more(g)
        else:
            combine(g, k - 3 * shares - 3)

    sent = 0
    for kind, item in plan:
        if kind == "send":
            gather.send(item)
            sent += 1
            if sent == bits * len(parts):
                for load in loads + old(0):
                    load.start()
        else:
            piece(*item)
    gws_ref[:, :width] = gwg[...].T.astype(bf16)
    gws_ref[:, width:] = gwu[...].T.astype(bf16)
    gather.finish()
    for item in outs(len(groups) - 1) + part_outs(len(groups) - 1):
        item.wait()


def experts_back(x, act, place, prob, saved, kept, weights, shared, capacity, bits, collective):
    tokens = x.shape[0]
    cycle = 1 << bits
    unit, size = expert_sizes(capacity, tokens, cycle)
    parts = all_parts([x.shape], bits)
    events = gather_events(parts, bits)
    shares = len(weights) // 3
    half = weights[0].shape[0]
    width = shared[1].shape[0]
    pieces = 3 * shares + 3 + size // unit
    groups, plan = gather_plan(parts, bits, events, 90.0, size, pieces, 15.0)
    anywhere = pl.BlockSpec(memory_space=pl.ANY)
    inside = pl.BlockSpec(memory_space=pltpu.VMEM)
    return pl.pallas_call(
        functools.partial(
            experts_back_kernel, groups, plan, parts, bits, events, shares, unit, capacity
        ),
        name="experts_back",
        out_shape=[
            jax.ShapeDtypeStruct((cycle, tokens, D), bf16),
            jax.ShapeDtypeStruct((cycle, tokens, D), bf16),
            jax.ShapeDtypeStruct((cycle * capacity, D), bf16),
        ]
        + [jax.ShapeDtypeStruct((cycle * capacity, half), bf16)] * (2 * shares)
        + [jax.ShapeDtypeStruct((D, 2 * width), bf16), jax.ShapeDtypeStruct((width, D), f32)],
        in_specs=[anywhere, anywhere, inside, inside] + [anywhere] * (5 + 5 * shares),
        out_specs=[anywhere] * (3 + 2 * shares) + [inside, inside],
        scratch_shapes=[
            pltpu.VMEM((3 * shares, half, D), bf16),
            pltpu.VMEM((D, 2 * width), bf16),
            pltpu.VMEM((width, D), bf16),
            pltpu.VMEM((size * tokens, D), bf16),
            pltpu.VMEM((size * tokens, D), bf16),
            pltpu.VMEM((size * capacity, D), bf16),
            pltpu.VMEM((size * tokens, D), bf16),
            pltpu.VMEM((3, size * tokens, width), bf16),
            pltpu.VMEM((2 * shares, size * capacity, half), bf16),
            pltpu.VMEM((2 * shares, size * capacity, half), bf16),
            pltpu.VMEM((width, D), f32),
            pltpu.VMEM((width, D), f32),
            pltpu.SemaphoreType.DMA((len(events),)),
            pltpu.SemaphoreType.DMA((len(parts), cycle)),
            pltpu.SemaphoreType.DMA,
            pltpu.SemaphoreType.DMA((3 * shares + 2,)),
            pltpu.SemaphoreType.DMA((size,)),
            pltpu.SemaphoreType.DMA((size,)),
            pltpu.SemaphoreType.DMA((3 + 2 * shares,)),
            pltpu.SemaphoreType.DMA((1 + 2 * shares,)),
            pltpu.SemaphoreType.DMA((size,)),
        ],
        compiler_params=pltpu.CompilerParams(
            collective_id=collective, has_side_effects=True, vmem_limit_bytes=61 << 20
        ),
    )(x, act, place, prob, *saved, *kept, *weights, *shared)


def shift_fsdp(x, groups, by):
    return lax.ppermute(x, "fsdp", [(i, (i + by) % groups) for i in range(groups)])


def gather_fsdp(x, groups):
    if groups != 2:
        return lax.all_gather(x, "fsdp", axis=0)
    other = shift_fsdp(x, groups, 1)
    mine_first = lax.axis_index("fsdp") == 0
    return jnp.stack([jnp.where(mine_first, x, other), jnp.where(mine_first, other, x)])


def scatter_fsdp(x, groups):
    if groups != 2:
        return lax.psum_scatter(x.astype(bf16), "fsdp", scatter_dimension=0).astype(f32)
    me = lax.axis_index("fsdp")
    away = lax.dynamic_index_in_dim(x, 1 - me, 0, keepdims=False).astype(bf16)
    mine = lax.dynamic_index_in_dim(x, me, 0, keepdims=False).astype(f32)
    return mine + shift_fsdp(away, groups, 1).astype(f32)


def shards(
    hidden_in,
    teacher,
    doc_starts,
    routes,
    gate_logits,
    input_gain,
    query_weight,
    latent_weight,
    latent_gain,
    expand_weight,
    output_weight,
    mixer_gain,
    shared_gate,
    shared_up,
    shared_down,
    expert_gate,
    expert_up,
    expert_down,
):
    cycle = lax.axis_size("ctx")
    groups = lax.axis_size("fsdp")
    bits = cycle.bit_length() - 1
    tokens = hidden_in.shape[1]
    length = tokens * cycle
    capacity = min(tokens, 3 * tokens * TOPK // (2 * cycle))
    scale = (DN + DR) ** (-0.5)
    copies = max(1, cycle // H)
    ctx_index = lax.axis_index("ctx")
    copy_index = ctx_index % copies
    slab = query_weight.shape[0]
    slab_latent = expand_weight.shape[0]

    def pieces(weight):
        rows, width = weight.shape
        return jnp.transpose(weight.reshape(rows, cycle, width // cycle), (1, 0, 2))

    def padded(item, width):
        return jnp.pad(item, ((0, 0), (0, 0), (0, width - item.shape[2])))

    def exchange(packed):
        return lax.all_to_all(packed, "ctx", split_axis=0, concat_axis=0, tiled=True)

    def same_head(part, axis):
        if copies == 1:
            return part
        teams = [[i * copies + j for j in range(copies)] for i in range(H)]
        return lax.all_gather(part, "ctx", axis=axis, tiled=True, axis_index_groups=teams)

    def own_part(full, axis=1):
        if copies == 1:
            return full
        width = full.shape[axis] // copies
        return lax.dynamic_slice_in_dim(full, copy_index * width, width, axis)

    def swap(pair):
        half = pair.shape[1] // 2
        return jnp.concatenate([-pair[:, half:], pair[:, :half]], axis=1)

    def all_rows(item):
        both = jnp.transpose(gather_fsdp(item, groups), (1, 0, 2, 3))
        return both.reshape(-1, item.shape[2])

    fast = copies == 1 and groups == 2 and cycle * groups * slab == D and slab == 64
    part_q, part_e = H * (DN + DR) // cycle, H * (DN + DV) // cycle
    part_s = shared_gate.shape[1] // cycle
    shared_width = -(-part_s // 128) * 128

    probs = jax.nn.softmax(gate_logits[0], axis=-1)
    chosen = routes[0][:, :, None] == jnp.arange(cycle, dtype=jnp.int32)[None, None, :]
    dense_probs = jnp.sum(jnp.where(chosen, probs[:, :, None], 0.0), axis=1).T
    high = lax.reduce_precision(dense_probs, 8, 7)
    dense_probs = jnp.concatenate([high, dense_probs - high], axis=1).astype(bf16)
    prob_width = 2 * tokens // slab
    dense_probs = dense_probs.reshape(cycle, slab, prob_width)
    expand_pieces = pieces(expand_weight)
    if fast:
        quarter = part_e // 4
        expand_pieces = jnp.concatenate(
            [expand_pieces[:, :, q * quarter : (q + 1) * quarter] for q in range(4)], axis=1
        )
    else:
        expand_pieces = expand_pieces.reshape(cycle, slab, -1)
    block_q = -(-(part_q + expand_pieces.shape[2]) // 128) * 128
    block_s = -(-(part_s + prob_width) // 128) * 128
    packed = padded(jnp.concatenate([pieces(query_weight), expand_pieces], axis=2), block_q)
    packed = exchange(packed)
    packed_s = jnp.concatenate(
        [
            padded(jnp.concatenate([pieces(shared_gate), dense_probs], axis=2), block_s),
            padded(pieces(shared_up), block_s),
        ],
        axis=2,
    )
    narrow = jnp.concatenate(
        [
            latent_weight,
            input_gain[:, None],
            mixer_gain[:, None],
            jnp.concatenate([latent_gain, jnp.zeros((slab - slab_latent,), bf16)])[:, None],
            jnp.zeros((slab, -(KVR + DR + 3) % 128), bf16),
        ],
        axis=1,
    )
    w_down_s = gather_fsdp(shared_down, groups).reshape(-1, D)
    w_down_s = jnp.pad(w_down_s, ((0, shared_width - w_down_s.shape[0]), (0, 0)))
    w_output = gather_fsdp(output_weight, groups).reshape(-1, D)
    if copies > 1:
        rows_o = w_output.shape[0]
        own_output = lax.dynamic_update_slice_in_dim(
            jnp.zeros((DV, D), bf16), w_output, copy_index * rows_o, 0
        )
        w_output = same_head(w_output, 0)
    else:
        own_output = w_output
    weights = [expert_gate[0].T, expert_up[0].T, expert_down[0]]
    for r in range(1, groups):
        weights += [shift_fsdp(item, groups, r) for item in weights[:3]]
    starts = doc_starts[0]
    positions = jnp.arange(length, dtype=jnp.int32)
    inside = starts[None, :] <= positions[:, None]
    first_pos = jnp.max(jnp.where(inside, starts[None, :], 0), axis=1)
    cosine, sine = rope_tables(positions - first_pos)
    first_col = first_pos[:, None]

    own_hidden, cosine, sine, first_col = lax.optimization_barrier(
        (hidden_in[0], cosine, sine, first_col)
    )
    all_hidden, narrow = gather_ctx([own_hidden, narrow], bits, 1)
    packed_s, _ = lax.optimization_barrier((packed_s, all_hidden))
    packed_s = exchange(packed_s)
    my_probs = packed_s[:, :, part_s : part_s + prob_width]
    my_probs = my_probs.reshape(cycle, 2, tokens).astype(f32)
    my_probs = my_probs[:, 0] + my_probs[:, 1]
    if fast:
        w_cat, w_expand, gains = assemble(
            packed, shift_fsdp(packed, groups, 1), narrow, shift_fsdp(narrow, groups, 1)
        )
        gain_one, gain_two = gains[0], gains[1]
        gain_latent = gains[2].reshape(-1, slab)[:, :slab_latent].reshape(-1)
    else:
        narrow, packed = all_rows(narrow), all_rows(packed)
        gain_one = narrow[:, KVR + DR].astype(f32)
        gain_two = narrow[:, KVR + DR + 1].astype(f32)
        gain_latent = narrow[:, KVR + DR + 2].reshape(-1, slab)[:, :slab_latent]
        gain_latent = gain_latent.reshape(-1).astype(f32)
        w_query = same_head(packed[:, :part_q], 1)
        w_expand = packed[:, part_q : part_q + expand_pieces.shape[2]].reshape(KVR, part_e)
        w_expand = same_head(w_expand, 1)
        rope_k = narrow[:, KVR : KVR + DR]
        w_cat = jnp.concatenate(
            [w_query, rope_k, swap(w_query[:, DN:]), swap(rope_k), narrow[:, :KVR]], axis=1
        )

    w_both_s = all_rows(packed_s)

    residual = hidden_in[0].astype(f32)
    act_one, queries, keys, values, latent, latent_raw = project(
        all_hidden.reshape(length, D), gain_one, w_cat, gain_latent, w_expand, cosine, sine, scale
    )
    attended, log_total, partial = attend(
        queries, keys, values, first_col, own_output
    )
    (mixing,) = scatter_ctx([partial.reshape(cycle, tokens, D)], bits, 3)
    mixed = residual + mixing

    normed_two, factor_two = norm_forward(mixed, gain_two)
    used = my_probs > 0.0
    place = jnp.cumsum(used.astype(jnp.int32), axis=1) - 1
    routing = (jnp.where(used, place, -1)[:, None, :], my_probs[:, None, :])
    shared = [w_both_s, w_down_s]
    all_act, partial, rows, gate_s, up_s, hidden_s, *kept = experts(
        normed_two.astype(bf16), *routing, weights, shared, capacity, bits, 2
    )
    (routed,) = scatter_ctx([partial], bits, 3)
    result = mixed + routed
    diff = result - teacher[0].astype(f32)
    share = jnp.sum(gather_fsdp(0.5 * jnp.sum(diff * diff, keepdims=True), groups))

    gates = [item for s in range(groups) for item in kept[3 * s : 3 * s + 2]]
    _, partial, grad_rows, *grads, grad_shared, grad_w_down = experts_back(
        diff.astype(bf16),
        all_act,
        *routing,
        [gate_s, up_s, hidden_s],
        gates,
        weights,
        shared,
        capacity,
        bits,
        6,
    )
    (grad_act_two,) = scatter_ctx([partial], bits, 3)
    grad_w_down = scatter_fsdp(grad_w_down[:part_s].reshape(groups, -1, D), groups)

    grad_gain_two = jnp.sum(grad_act_two * mixed * factor_two, axis=0)
    grad_mixed = diff + norm_back_rows(mixed, factor_two, gain_two, grad_act_two)
    def by_owner(grad):
        cut = jnp.transpose(grad.reshape(cycle, groups, slab, -1), (1, 0, 2, 3))
        return scatter_fsdp(cut, groups).astype(bf16)

    grad_shared = by_owner(grad_shared)
    high = lax.reduce_precision(share, 8, 7)
    mid = lax.reduce_precision(share - high, 8, 7)
    loss_parts = jnp.stack([high, mid, share - high - mid]).astype(bf16)
    spot = jnp.arange(grad_shared.shape[2], dtype=jnp.int32) - part_s
    loss_row = sum(jnp.where(spot == i, loss_parts[i], bf16(0)) for i in range(3))
    grad_shared = jnp.where(((spot >= 0) & (spot < 3))[None, None, :], loss_row, grad_shared)
    lefts = []
    for r in range(groups):
        lefts += [grads[2 * r], grads[2 * r + 1], kept[3 * r + 2]]
    all_mixed, *expert_grads = gather_multiply(
        grad_mixed.astype(bf16), rows, grad_rows, lefts, bits, 5
    )
    grad_shared, all_mixed = lax.optimization_barrier((grad_shared, all_mixed))
    packed_s = exchange(grad_shared)
    loss_parts = packed_s[:, 0, part_s : part_s + 3].astype(f32)
    loss_value = jnp.sum(loss_parts) / (length * groups * D)
    grad_query, grad_keys, grad_values, grad_w_output, *expert_grads = attend_back(
        queries,
        keys,
        values,
        all_mixed.reshape(length, D),
        attended,
        w_output,
        first_pos[None, :],
        log_total,
        expert_grads,
    )
    grad_query, packed_s = lax.optimization_barrier((grad_query, packed_s))
    grad_w_output = own_part(grad_w_output, 0).reshape(groups, slab, D)
    grad_w_output = scatter_fsdp(grad_w_output, groups)
    lanes = jnp.arange(WIDE, dtype=jnp.int32)
    keep_q = (lanes // ((DN + DR) // copies) == copy_index).astype(f32)[None, :]
    keep_e = (lanes // ((DN + DV) // copies) == copy_index).astype(f32)[None, :]
    grads_cat, grad_w_cat, grad_w_expand = project_back(
        grad_query,
        grad_keys,
        grad_values,
        latent_raw,
        latent,
        act_one,
        cosine,
        sine,
        w_expand,
        gain_latent,
        keep_q,
        keep_e,
        scale,
        copies,
    )
    if fast:
        first, slim = finish(
            grad_w_cat, grad_w_expand, w_cat, w_expand, grad_gain_two[:, None], cycle, slab, 7
        )
    else:
        grad_gain_one = jnp.sum(grad_w_cat * w_cat.astype(f32), axis=1)
        grad_gain_latent = jnp.sum(grad_w_expand * w_expand.astype(f32), axis=1)
        turned = grad_w_cat[:, 2 * DN : 3 * DN]
        grad_ropes = grad_w_cat[:, DN : 2 * DN] - jnp.concatenate(
            [swap(turned[:, :DR]), swap(turned[:, DR:])], axis=1
        )
        grad_w_query = jnp.concatenate([grad_w_cat[:, :DN], grad_ropes[:, :DR]], axis=1)
        grad_we = own_part(grad_w_expand).reshape(cycle * groups, slab_latent, part_e)
        first = jnp.concatenate(
            [own_part(grad_w_query), grad_we.reshape(D, -1)], axis=1
        ).astype(bf16)
        spare = jnp.zeros((cycle * groups, slab - slab_latent), f32)
        grad_gain_latent = jnp.concatenate(
            [grad_gain_latent.reshape(cycle * groups, slab_latent), spare], axis=1
        ).reshape(-1)
        slim = jnp.concatenate(
            [
                grad_w_cat[:, 3 * DN :],
                grad_ropes[:, DR:],
                grad_gain_one[:, None],
                grad_gain_two[:, None],
                grad_gain_latent[:, None],
                jnp.zeros((D, -(KVR + DR + 3) % 128), f32),
            ],
            axis=1,
        ).astype(bf16)
        slim, first = by_owner(slim), padded(by_owner(first), block_q)
    packed = exchange(first)
    partial = project_back_rows(grads_cat, w_cat)
    partial, packed = lax.optimization_barrier((partial, packed))
    grad_act_one, grad_narrow = scatter_ctx(
        [partial.reshape(cycle, tokens, D), slim], bits, 4
    )
    if fast:
        own_grads = spread(
            packed,
            packed_s,
            [w.shape[1] for w in (query_weight, expand_weight, shared_gate, shared_up)],
        )
    else:
        spots = (
            (packed, 0, part_q, query_weight),
            (packed, part_q, expand_pieces.shape[2], expand_weight),
            (packed_s, 0, part_s, shared_gate),
            (packed_s, shared_width, part_s, shared_up),
        )
        own_grads = []
        for item, start, width, like in spots:
            item = item[:, :, start : start + width].reshape(cycle, like.shape[0], -1)
            own_grads.append(jnp.transpose(item, (1, 0, 2)).reshape(like.shape).astype(f32))
    _, factor_one = norm_forward(residual, gain_one)
    grad_input = grad_mixed + norm_back_rows(residual, factor_one, gain_one, grad_act_one)
    return (
        result.astype(bf16)[None],
        loss_value,
        grad_input[None],
        grad_narrow[:, KVR + DR] / input_gain.astype(f32),
        own_grads[0],
        grad_narrow[:, : KVR + DR],
        grad_narrow[:slab_latent, KVR + DR + 2] / latent_gain.astype(f32),
        own_grads[1],
        grad_w_output,
        grad_narrow[:, KVR + DR + 1],
        own_grads[2],
        own_grads[3],
        grad_w_down,
        expert_grads[0].T[None],
        expert_grads[1].T[None],
        expert_grads[2][None],
    )


def solution(mesh):
    tokens = P("fsdp", "ctx", None)
    rows = P(("ctx", "fsdp"), None)
    gain = P(("ctx", "fsdp"))
    wide = P("ctx", None, "fsdp")
    deep = P("ctx", "fsdp", None)
    in_specs = (
        tokens,
        tokens,
        P("fsdp", None),
        tokens,
        tokens,
        gain,
        rows,
        rows,
        gain,
        rows,
        rows,
        gain,
        rows,
        rows,
        rows,
        wide,
        wide,
        deep,
    )
    out_specs = (
        tokens,
        P(),
        tokens,
        gain,
        rows,
        rows,
        gain,
        rows,
        rows,
        gain,
        rows,
        rows,
        rows,
        wide,
        wide,
        deep,
    )
    return jax.shard_map(shards, mesh=mesh, in_specs=in_specs, out_specs=out_specs, check_vma=False)
```

```python
import functools
import math

import jax
import jax.numpy as jnp
from jax import lax
from jax.experimental import pallas as pl
from jax.experimental.pallas import tpu as pltpu
from jax.sharding import PartitionSpec as P

D = 2048
H = 16
DN = 128
DR = 64
DV = 128
KVR = 512
TOPK = 6
WIDE = 256

EPS = 1e-06
NEG = -1e30
MESH = pl.DeviceIdType.MESH
f32 = jnp.float32
bf16 = jnp.bfloat16


def norm_forward(rows, gain):
    factor = lax.rsqrt(jnp.mean(rows * rows, axis=-1, keepdims=True) + EPS)
    return (rows * factor * gain, factor)


def norm_back_rows(rows, factor, gain, grad_out):
    scaled = grad_out * gain
    normed = rows * factor
    return factor * (scaled - normed * jnp.mean(scaled * normed, axis=-1, keepdims=True))


def rotate(values, cosine, sine):
    half = values.shape[-1] // 2
    first = values[..., :half]
    second = values[..., half:]
    return jnp.concatenate(
        [first * cosine - second * sine, second * cosine + first * sine], axis=-1
    )


def rope_tables(offsets):
    spot = (jnp.arange(2 * DR, dtype=jnp.int32) % (DR // 2)).astype(f32)
    freqs = 10000.0 ** (-(spot * 2.0) / DR)
    angle = offsets.astype(f32)[:, None] * freqs[None, :]
    return (jnp.cos(angle), jnp.sin(angle))


def silu_grads(gate_val, up_val, grad_hidden):
    sigma = jax.nn.sigmoid(gate_val)
    grad_gate = grad_hidden * up_val * sigma * (1.0 + gate_val * (1.0 - sigma))
    grad_up = grad_hidden * gate_val * sigma
    return (grad_gate.astype(bf16), grad_up.astype(bf16))


def dot(left, right):
    return jnp.dot(left, right, preferred_element_type=f32)


def dot_first(left, right):
    return lax.dot_general(left, right, (((0,), (0,)), ((), ())), preferred_element_type=f32)


def dot_last(left, right):
    return lax.dot_general(left, right, (((1,), (1,)), ((), ())), preferred_element_type=f32)


def flip(me, mask):
    out = me
    bit = 1
    while bit <= mask:
        if mask & bit:
            out = out + bit * (1 - 2 * ((me // bit) % 2))
        bit *= 2
    return out


def row_parts(rows, bits):
    low, high = [1, 2], [1 << k for k in range(bits - 1, 1, -1)]
    orders = (high + low, high + low[::-1], low + high)
    units = rows // 16
    if units < 3:
        return ((0, rows, tuple(orders[0])),)
    third = max(1, units // 4)
    first = (units - third) // 2
    counts = (first * 16, (units - third - first) * 16, third * 16)
    parts, start = [], 0
    for count, order in zip(counts, orders):
        parts.append((start, count, tuple(order)))
        start += count
    return tuple(parts)


def all_parts(shapes, bits):
    return tuple(
        (a,) + part for a, shape in enumerate(shapes) for part in row_parts(shape[-2], bits)
    )


def greet(bits):
    me = lax.axis_index("ctx")
    barrier = pltpu.get_barrier_semaphore()
    for k in range(bits):
        pl.semaphore_signal(
            barrier, inc=1, device_id={"ctx": flip(me, 1 << k)}, device_id_type=MESH
        )
    pl.semaphore_wait(barrier, bits)


def gather_events(parts, bits):
    events = []
    for p, (_, _, _, order) in enumerate(parts):
        for slot in range(1 << bits):
            hops = [k for k, b in enumerate(order) if slot & b]
            for k in range(hops[-1] + 1 if hops else 0, bits):
                events.append((len(hops), k, p, slot, order[k]))
    return tuple(sorted(events))


def gather_kernel(parts, bits, events, count, *refs):
    x_refs, o_refs = refs[:count], refs[count : 2 * count]
    send_sem, recv_sem, own_sem = refs[2 * count :]
    me = lax.axis_index("ctx")
    own = [
        pltpu.make_async_copy(x_refs[a], o_refs[a].at[me], own_sem.at[a]) for a in range(count)
    ]
    for item in own:
        item.start()
    greet(bits)

    def copy(p, slot, bit, index):
        a, start, size, _ = parts[p]
        rows = pl.ds(start, size)
        block = flip(me, slot)
        return pltpu.make_async_remote_copy(
            src_ref=x_refs[a].at[rows] if slot == 0 else o_refs[a].at[block, rows],
            dst_ref=o_refs[a].at[block, rows],
            send_sem=send_sem.at[index],
            recv_sem=recv_sem.at[p, slot ^ bit],
            device_id={"ctx": flip(me, bit)},
            device_id_type=MESH,
        )

    def arrived(p, slot):
        a, start, size, order = parts[p]
        rows = pl.ds(start, size)
        bit = [b for b in order if slot & b][-1]
        pltpu.make_async_remote_copy(
            src_ref=x_refs[a].at[rows],
            dst_ref=o_refs[a].at[flip(me, slot), rows],
            send_sem=send_sem.at[0],
            recv_sem=recv_sem.at[p, slot],
            device_id={"ctx": flip(me, bit)},
            device_id_type=MESH,
        ).wait_recv()

    seen = set()
    started = []
    for index, (_, _, p, slot, bit) in enumerate(events):
        if slot and (p, slot) not in seen:
            arrived(p, slot)
            seen.add((p, slot))
        sent = copy(p, slot, bit, index)
        sent.start()
        started.append(sent)
    for p in range(len(parts)):
        for slot in range(1, 1 << bits):
            if (p, slot) not in seen:
                arrived(p, slot)
    for sent in started:
        sent.wait_send()
    for item in own:
        item.wait()


def gather_ctx(arrays, bits, collective):
    parts = all_parts([item.shape for item in arrays], bits)
    events = gather_events(parts, bits)
    count = len(arrays)
    return pl.pallas_call(
        functools.partial(gather_kernel, parts, bits, events, count),
        name="gather_ctx",
        out_shape=[jax.ShapeDtypeStruct((1 << bits,) + item.shape, item.dtype) for item in arrays],
        in_specs=[pl.BlockSpec(memory_space=pl.ANY)] * count,
        out_specs=[pl.BlockSpec(memory_space=pl.ANY)] * count,
        scratch_shapes=[
            pltpu.SemaphoreType.DMA((len(events),)),
            pltpu.SemaphoreType.DMA((len(parts), 1 << bits)),
            pltpu.SemaphoreType.DMA((count,)),
        ],
        compiler_params=pltpu.CompilerParams(collective_id=collective, has_side_effects=True),
    )(*arrays)


def gather_multiply_kernel(
    parts, bits, events, shares, tile, x_ref, rows_ref, dy_ref, *refs
):
    lefts, refs = refs[: 3 * shares], refs[3 * shares :]
    o_ref, outs, refs = refs[0], refs[1:4], refs[4:]
    rows, dy, left, sent, got, stage = refs[:6]
    send_sem, recv_sem, own_sem, load_sem, out_sem, far_sem, near_sem = refs[6:]
    me, place = lax.axis_index("ctx"), lax.axis_index("fsdp")
    half, width = left.shape[2], rows.shape[1]
    tiles = width // tile
    loads = [pltpu.make_async_copy(rows_ref, rows, load_sem.at[3 * shares])]
    loads.append(pltpu.make_async_copy(dy_ref, dy, load_sem.at[3 * shares + 1]))
    order = list(range(3, 3 * shares)) + [0, 1, 2]
    for i in range(3 * shares):
        loads.append(pltpu.make_async_copy(lefts[i], left.at[i], load_sem.at[i]))
    own = pltpu.make_async_copy(x_ref, o_ref.at[me], own_sem)
    own.start()
    barrier = pltpu.get_barrier_semaphore()
    for k in range(bits):
        pl.semaphore_signal(
            barrier, inc=1, device_id={"ctx": flip(me, 1 << k)}, device_id_type=MESH
        )
    for r in range(1, shares):
        pl.semaphore_signal(
            barrier, inc=1, device_id={"fsdp": (place + r) % shares}, device_id_type=MESH
        )
    pl.semaphore_wait(barrier, bits + shares - 1)
    for i in [0, 2 + 3 % (3 * shares), 1] if shares > 1 else [0, 2, 1]:
        loads[i].start()
    for i in range(2, len(loads)):
        if i != 2 + 3 % (3 * shares):
            loads[i].start()
    ready = set()

    def need(i):
        if i not in ready:
            loads[i].wait()
            ready.add(i)

    def copy(p, slot, bit, index):
        _, start, size, _ = parts[p]
        part = pl.ds(start, size)
        block = flip(me, slot)
        return pltpu.make_async_remote_copy(
            src_ref=x_ref.at[part] if slot == 0 else o_ref.at[block, part],
            dst_ref=o_ref.at[block, part],
            send_sem=send_sem.at[index],
            recv_sem=recv_sem.at[p, slot ^ bit],
            device_id={"ctx": flip(me, bit)},
            device_id_type=MESH,
        )

    def arrived(p, slot):
        _, start, size, path = parts[p]
        part = pl.ds(start, size)
        bit = [b for b in path if slot & b][-1]
        pltpu.make_async_remote_copy(
            src_ref=x_ref.at[part],
            dst_ref=o_ref.at[flip(me, slot), part],
            send_sem=send_sem.at[0],
            recv_sem=recv_sem.at[p, slot],
            device_id={"ctx": flip(me, bit)},
            device_id_type=MESH,
        ).wait_recv()

    def far(i, t):
        spot = (i - 3, slice(None), pl.ds(t * tile, tile))
        return pltpu.make_async_remote_copy(
            src_ref=sent.at[spot],
            dst_ref=got.at[spot],
            send_sem=far_sem.at[i - 3, t],
            recv_sem=near_sem.at[i - 3, t],
            device_id={"fsdp": (place + shares - i // 3) % shares},
            device_id_type=MESH,
        )

    def store(i, t):
        buffer = (i * tiles + t) % 2
        return pltpu.make_async_copy(
            stage.at[buffer], outs[i].at[:, pl.ds(t * tile, tile)], out_sem.at[i, t]
        )

    def multiply(i, t):
        need(2 + i)
        need(1 if i % 3 == 2 else 0)
        right = dy if i % 3 == 2 else rows
        total = dot_first(left[i], right[:, t * tile : (t + 1) * tile])
        if i >= 3:
            sent[i - 3, :, t * tile : (t + 1) * tile] = total.astype(bf16)
            far(i, t).start()
            return
        for r in range(1, shares):
            far(i + 3 * r, t).wait_recv()
            total = total + got[i + 3 * r - 3, :, t * tile : (t + 1) * tile].astype(f32)
        last = i * tiles + t - 2
        if last >= 0:
            store(last // tiles, last % tiles).wait()
        stage[(i * tiles + t) % 2] = total.astype(bf16)
        store(i, t).start()

    work = [(i, t) for i in order for t in range(tiles)]
    done = 0
    seen = set()
    started = []
    for index, (_, _, p, slot, bit) in enumerate(events):
        if slot and (p, slot) not in seen:
            arrived(p, slot)
            seen.add((p, slot))
        item = copy(p, slot, bit, index)
        item.start()
        started.append(item)
        first = bits * len(parts)
        if index >= first:
            while done < len(work) * (index - first + 1) // (len(events) - first):
                multiply(*work[done])
                done += 1
    for p in range(len(parts)):
        for slot in range(1, 1 << bits):
            if (p, slot) not in seen:
                arrived(p, slot)
    for item in started:
        item.wait_send()
    own.wait()
    for i in range(3, 3 * shares):
        for t in range(tiles):
            far(i, t).wait_send()
    for last in range(max(0, 3 * tiles - 2), 3 * tiles):
        store(last // tiles, last % tiles).wait()


def gather_multiply(x, rows, dy, lefts, bits, collective):
    parts = all_parts([x.shape], bits)
    events = gather_events(parts, bits)
    shares = len(lefts) // 3
    count, half = lefts[0].shape
    width = rows.shape[1]
    tile = width // 2
    anywhere = pl.BlockSpec(memory_space=pl.ANY)
    others = max(1, 3 * shares - 3)
    return pl.pallas_call(
        functools.partial(gather_multiply_kernel, parts, bits, events, shares, tile),
        name="gather_multiply",
        out_shape=[jax.ShapeDtypeStruct((1 << bits,) + x.shape, x.dtype)]
        + [jax.ShapeDtypeStruct((half, width), bf16)] * 3,
        in_specs=[anywhere] * (3 + 3 * shares),
        out_specs=[anywhere] * 4,
        scratch_shapes=[
            pltpu.VMEM((count, width), bf16),
            pltpu.VMEM((count, width), bf16),
            pltpu.VMEM((3 * shares, count, half), bf16),
            pltpu.VMEM((others, half, width), bf16),
            pltpu.VMEM((others, half, width), bf16),
            pltpu.VMEM((2, half, tile), bf16),
            pltpu.SemaphoreType.DMA((len(events),)),
            pltpu.SemaphoreType.DMA((len(parts), 1 << bits)),
            pltpu.SemaphoreType.DMA,
            pltpu.SemaphoreType.DMA((3 * shares + 2,)),
            pltpu.SemaphoreType.DMA((3, width // tile)),
            pltpu.SemaphoreType.DMA((others, width // tile)),
            pltpu.SemaphoreType.DMA((others, width // tile)),
        ],
        compiler_params=pltpu.CompilerParams(
            collective_id=collective, has_side_effects=True, vmem_limit_bytes=60 << 20
        ),
    )(x, rows, dy, *lefts)


def scatter_events(parts, bits):
    events = []
    for p, (_, _, _, order) in enumerate(parts):
        for slot in range(1, 1 << bits):
            k = [i for i, b in enumerate(order) if slot & b][0]
            later = tuple(-int(bool(slot & b)) for b in order[k + 1 :])
            events.append((k, later, p, slot))
    return tuple((k, p, slot) for k, _, p, slot in sorted(events))


def scatter_kernel(parts, bits, events, count, *refs):
    x_refs, o_refs = refs[:count], refs[count : 2 * count]
    recvs, sends, owns = (refs[(2 + i) * count : (3 + i) * count] for i in range(3))
    send_sem, recv_sem, own_sem = refs[5 * count :]
    me = lax.axis_index("ctx")
    later = [sorted({s for k, p, s in events if k and parts[p][0] == a}) for a in range(count)]

    def load(a, slot):
        place = later[a].index(slot) + 1 if slot else 0
        return pltpu.make_async_copy(
            x_refs[a].at[flip(me, slot)], owns[a].at[place], own_sem.at[a, place]
        )

    greet(bits)

    def copy(p, slot, k, src):
        a, start, size, order = parts[p]
        return pltpu.make_async_remote_copy(
            src_ref=src,
            dst_ref=recvs[a].at[slot - 1, pl.ds(start, size)],
            send_sem=send_sem.at[p, slot - 1],
            recv_sem=recv_sem.at[p, slot - 1],
            device_id={"ctx": flip(me, order[k])},
            device_id_type=MESH,
        )

    loaded = set()

    def add_up(p, slot, k):
        a, start, size, order = parts[p]
        place = later[a].index(slot) + 1 if slot else 0
        if (a, slot) not in loaded:
            load(a, slot).wait()
            loaded.add((a, slot))
        for e in range(k):
            other = slot | order[e]
            copy(p, other, e, recvs[a].at[other - 1, pl.ds(start, size)]).wait_recv()
        target = sends[a].at[place - 1] if slot else o_refs[a]

        @pl.loop(0, size // 16)
        def _(t):
            part = pl.ds(pl.multiple_of(start + t * 16, 16), 16)
            total = owns[a][place, part].astype(f32)
            for e in range(k):
                total = total + recvs[a][(slot | order[e]) - 1, part].astype(f32)
            target[part] = total.astype(target.dtype)

    started = []
    first = [event for event in events if event[0] == 0]
    for index, (k, p, slot) in enumerate(events):
        a, start, size, order = parts[p]
        rows = pl.ds(start, size)
        if k == 0:
            src = x_refs[a].at[flip(me, slot), rows]
        else:
            add_up(p, slot, k)
            src = sends[a].at[later[a].index(slot), rows]
        sent = copy(p, slot, k, src)
        sent.start()
        started.append(sent)
        if index == len(first) // 2:
            for a in range(count):
                for own in [0] + later[a]:
                    load(a, own).start()
    for p in range(len(parts)):
        add_up(p, 0, bits)
    for sent in started:
        sent.wait_send()


def scatter_ctx(arrays, bits, collective):
    shapes = [item.shape[1:] for item in arrays]
    parts = all_parts(shapes, bits)
    parts = tuple((a, start, size, order[::-1]) for a, start, size, order in parts)
    events = scatter_events(parts, bits)
    count = len(arrays)
    others = (1 << bits) - 1
    held = [
        1 + len({s for k, p, s in events if k and parts[p][0] == a}) for a in range(count)
    ]
    return pl.pallas_call(
        functools.partial(scatter_kernel, parts, bits, events, count),
        name="scatter_ctx",
        out_shape=[jax.ShapeDtypeStruct(shape, f32) for shape in shapes],
        in_specs=[pl.BlockSpec(memory_space=pl.ANY)] * count,
        out_specs=[pl.BlockSpec(memory_space=pltpu.VMEM)] * count,
        scratch_shapes=[pltpu.VMEM((others,) + shape, bf16) for shape in shapes]
        + [pltpu.VMEM((n - 1,) + shape, bf16) for n, shape in zip(held, shapes)]
        + [pltpu.VMEM((n,) + shape, bf16) for n, shape in zip(held, shapes)]
        + [
            pltpu.SemaphoreType.DMA((len(parts), others)),
            pltpu.SemaphoreType.DMA((len(parts), others)),
            pltpu.SemaphoreType.DMA((count, max(held))),
        ],
        compiler_params=pltpu.CompilerParams(
            collective_id=collective, has_side_effects=True, vmem_limit_bytes=58 << 20
        ),
    )(*arrays)


def attend_kernel(block, count, q_ref, k_ref, v_ref, first_ref, wo_ref, o_ref, log_ref, part_ref):
    step = pl.program_id(0)
    for i in range(count):

        @pl.when(step == i)
        def _(i=i):
            extent = (i + 1) * block
            scores = dot_last(q_ref[...], k_ref[:extent, :])
            key_pos = lax.broadcasted_iota(jnp.int32, (block, extent), 1)
            query_pos = i * block + lax.broadcasted_iota(jnp.int32, (block, extent), 0)
            allowed = (key_pos >= first_ref[...]) & (key_pos <= query_pos)
            scores = jnp.where(allowed, scores, NEG)
            top = jnp.max(scores, axis=-1, keepdims=True)
            weights = jnp.exp(scores - top)
            total = jnp.sum(weights, axis=-1, keepdims=True)
            summed = dot(weights.astype(bf16), v_ref[:extent, :])
            o_ref[...] = summed / total
            column = jnp.broadcast_to(top + jnp.log(total), (block, 128))
            log_ref[...] = column.T[:1, :]
            part_ref[...] = dot((summed / total).astype(bf16), wo_ref[...]).astype(bf16)


def attend(queries, keys, values, first, w_output):
    length = queries.shape[0]
    block = min(256, length)
    count = length // block
    return pl.pallas_call(
        functools.partial(attend_kernel, block, count),
        name="attend",
        grid=(count,),
        out_shape=(
            jax.ShapeDtypeStruct((length, DV), f32),
            jax.ShapeDtypeStruct((1, length), f32),
            jax.ShapeDtypeStruct((length, D), bf16),
        ),
        in_specs=[
            pl.BlockSpec((block, WIDE), lambda i: (i, 0)),
            pl.BlockSpec((length, WIDE), lambda i: (0, 0)),
            pl.BlockSpec((length, DV), lambda i: (0, 0)),
            pl.BlockSpec((block, 1), lambda i: (i, 0)),
            pl.BlockSpec((DV, D), lambda i: (0, 0)),
        ],
        out_specs=(
            pl.BlockSpec((block, DV), lambda i: (i, 0)),
            pl.BlockSpec((1, block), lambda i: (0, i)),
            pl.BlockSpec((block, D), lambda i: (i, 0)),
        ),
        compiler_params=pltpu.CompilerParams(vmem_limit_bytes=60 << 20),
        cost_estimate=pl.CostEstimate(
            flops=length * length * (DN + DR + DV),
            bytes_accessed=length * 2000,
            transcendentals=length * length // 2,
        ),
    )(queries, keys, values, first, w_output)


def attend_back_kernel(
    block, count, q_ref, k_ref, v_ref, m_ref, att_ref, wo_ref, first_ref, log_ref,
    *refs,
):
    few = (len(refs) - 4) // 2
    lows, (dq_ref, dk_ref, dv_ref, gwo_ref) = refs[:few], refs[few : few + 4]
    wides = refs[few + 4 :]
    step = pl.program_id(0)
    for low_ref, wide_ref in zip(lows, wides):
        wide_ref[...] = low_ref[...].astype(f32)

    @pl.when(step == 0)
    def _():
        dk_ref[...] = jnp.zeros_like(dk_ref)
        dv_ref[...] = jnp.zeros_like(dv_ref)
        gwo_ref[...] = jnp.zeros_like(gwo_ref)

    grad = dot_last(m_ref[...], wo_ref[...]).astype(bf16)
    gwo_ref[...] += dot_first(att_ref[...].astype(bf16), m_ref[...])
    delta = jnp.sum((grad.astype(f32) * att_ref[...]).T, axis=0, keepdims=True)
    for i in range(count):

        @pl.when(step == i)
        def _(i=i):
            extent = (i + 1) * block
            keys = k_ref[:extent, :]
            scores = dot_last(keys, q_ref[...])
            key_pos = lax.broadcasted_iota(jnp.int32, (extent, block), 0)
            query_pos = i * block + lax.broadcasted_iota(jnp.int32, (extent, block), 1)
            allowed = (key_pos >= first_ref[...]) & (key_pos <= query_pos)
            weights = jnp.where(allowed, jnp.exp(scores - log_ref[...]), 0.0)
            grad_weights = dot_last(v_ref[:extent, :], grad)
            grad_scores = (weights * (grad_weights - delta)).astype(bf16)
            dv_ref[:extent, :] += dot(weights.astype(bf16), grad)
            dk_ref[:extent, :] += dot(grad_scores, q_ref[...])
            dq_ref[...] = dot_first(grad_scores, keys)


def attend_back(queries, keys, values, grad_mixed, attended, w_output, first, log_total, lows):
    length = queries.shape[0]
    block = min(256, length)
    count = length // block
    row = lambda: pl.BlockSpec((1, block), lambda i: (0, i))
    whole = lambda height, width: pl.BlockSpec((height, width), lambda i: (0, 0))
    part = lambda width: pl.BlockSpec((block, width), lambda i: (i, 0))
    tall, wide = lows[0].shape
    piece = 176 if tall % 176 == 0 else tall
    steps = tall // piece
    some = pl.BlockSpec((piece, wide), lambda i: (i * steps // count, 0))
    return pl.pallas_call(
        functools.partial(attend_back_kernel, block, count),
        name="attend_back",
        grid=(count,),
        out_shape=(
            jax.ShapeDtypeStruct((length, WIDE), f32),
            jax.ShapeDtypeStruct((length, WIDE), f32),
            jax.ShapeDtypeStruct((length, DV), f32),
            jax.ShapeDtypeStruct((DV, D), f32),
        )
        + tuple(jax.ShapeDtypeStruct((tall, wide), f32) for _ in lows),
        in_specs=[
            part(WIDE),
            whole(length, WIDE),
            whole(length, DV),
            part(D),
            part(DV),
            whole(DV, D),
            row(),
            row(),
        ]
        + [some] * len(lows),
        out_specs=(part(WIDE), whole(length, WIDE), whole(length, DV), whole(DV, D))
        + (some,) * len(lows),
        compiler_params=pltpu.CompilerParams(vmem_limit_bytes=60 << 20),
        cost_estimate=pl.CostEstimate(
            flops=length * length * (3 * (DN + DR) + 2 * DV),
            bytes_accessed=length * 4000,
            transcendentals=length * length // 2,
        ),
    )(queries, keys, values, grad_mixed, attended, w_output, first, log_total, *lows)


def lanes_of(value):
    return lax.broadcasted_iota(jnp.int32, value.shape, len(value.shape) - 1)


def swap_lanes(ropes):
    return jnp.where(
        lanes_of(ropes) % DR < DR // 2, -pltpu.roll(ropes, 96, 1), pltpu.roll(ropes, 32, 1)
    )


def assemble_kernel(
    cycle, slab, mine_ref, other_ref, mine_n_ref, other_n_ref,
    w_ref, we_ref, gains_ref, narrow_ref, expand_ref,
):
    me = lax.axis_index("fsdp")
    for f, (pack_ref, slim_ref) in enumerate(((mine_ref, mine_n_ref), (other_ref, other_n_ref))):
        owner = me if f == 0 else 1 - me

        @pl.loop(0, cycle)
        def _(c):
            rows = pl.ds(pl.multiple_of((c * 2 + owner) * slab, slab), slab)
            w_ref[rows, :DN] = pack_ref[c, :, :DN]
            w_ref[rows, 3 * DN :] = slim_ref[c, :, :KVR]
            tail = pack_ref[c, :, DN:256].astype(f32)
            slim = slim_ref[c, :, KVR:].astype(f32)
            ropes = jnp.where(lanes_of(tail) < DR, tail, pltpu.roll(slim, DR, 1))
            w_ref[rows, DN : 2 * DN] = ropes.astype(bf16)
            w_ref[rows, 2 * DN : 3 * DN] = swap_lanes(ropes).astype(bf16)
            narrow_ref[rows, :] = slim
            quarter = slab // 4
            for q in range(2):
                left = tail[2 * q * quarter : (2 * q + 1) * quarter]
                right = tail[(2 * q + 1) * quarter : (2 * q + 2) * quarter]
                both = jnp.where(lanes_of(left) < DR, pltpu.roll(left, DR, 1), right)
                spot = pl.ds(pl.multiple_of((c * 2 + owner) * quarter, quarter), quarter)
                expand_ref[spot, q * DN : (q + 1) * DN] = both

    we_ref[...] = expand_ref[...].astype(bf16)
    gains_ref[...] = narrow_ref[...].T[DR : DR + 8, :]


def assemble(mine, other, mine_n, other_n):
    cycle, slab, _ = mine.shape
    return pl.pallas_call(
        functools.partial(assemble_kernel, cycle, slab),
        name="assemble",
        out_shape=(
            jax.ShapeDtypeStruct((D, 3 * DN + KVR), bf16),
            jax.ShapeDtypeStruct((KVR, DN + DV), bf16),
            jax.ShapeDtypeStruct((8, D), f32),
        ),
        scratch_shapes=[pltpu.VMEM((D, DN), f32), pltpu.VMEM((KVR, DN + DV), f32)],
        compiler_params=pltpu.CompilerParams(vmem_limit_bytes=60 << 20),
    )(mine, other, mine_n, other_n)


def finish_kernel(
    cycle, slab, gw_ref, gwe_ref, w_ref, we_ref, extra_ref, first_ref, slim_ref,
    away_first, away_slim, got_first, got_slim, send_sem, recv_sem,
):
    me = lax.axis_index("fsdp")
    quarter = slab // 4
    barrier = pltpu.get_barrier_semaphore()
    pl.semaphore_signal(barrier, inc=1, device_id={"fsdp": 1 - me}, device_id_type=MESH)

    def by_slab(owner, first_out, slim_out):
        @pl.loop(0, cycle)
        def _(c):
            rows = pl.ds(pl.multiple_of((c * 2 + owner) * slab, slab), slab)
            some = pl.ds(pl.multiple_of((c * 2 + owner) * quarter, quarter), quarter)
            grad, expand = gw_ref[rows, :], gwe_ref[some, :]
            ropes = grad[:, DN : 2 * DN] - swap_lanes(grad[:, 2 * DN : 3 * DN])
            gain_one = jnp.sum(grad * w_ref[rows, :].astype(f32), axis=1, keepdims=True)
            gain_latent = jnp.sum(expand * we_ref[some, :].astype(f32), axis=1, keepdims=True)
            lanes = lanes_of(ropes)
            tail = jnp.where(lanes < DR, pltpu.roll(ropes, DR, 1), 0.0)
            tail = jnp.where(lanes == DR, gain_one, tail)
            tail = jnp.where(lanes == DR + 1, extra_ref[rows, :], tail)
            column = jnp.concatenate([gain_latent, jnp.zeros((slab - quarter, 1), f32)], axis=0)
            tail = jnp.where(lanes == DR + 2, column, tail)
            pieces = jnp.concatenate(
                [
                    pltpu.roll(expand[:, :DN], DR, 1),
                    expand[:, :DN],
                    pltpu.roll(expand[:, DN:], DR, 1),
                    expand[:, DN:],
                ],
                axis=0,
            )
            first_out[c, :, :DN] = grad[:, :DN].astype(bf16)
            first_out[c, :, DN:] = jnp.where(lanes < DR, ropes, pieces).astype(bf16)
            slim_out[c, :, :KVR] = grad[:, 3 * DN :].astype(bf16)
            slim_out[c, :, KVR:] = tail.astype(bf16)

    by_slab(1 - me, away_first, away_slim)
    pl.semaphore_wait(barrier, 1)
    copies = [
        pltpu.make_async_remote_copy(
            src_ref=src,
            dst_ref=dst,
            send_sem=send_sem.at[i],
            recv_sem=recv_sem.at[i],
            device_id={"fsdp": 1 - me},
            device_id_type=MESH,
        )
        for i, (src, dst) in enumerate(((away_first, got_first), (away_slim, got_slim)))
    ]
    for item in copies:
        item.start()
    by_slab(me, first_ref, slim_ref)
    for item in copies:
        item.wait()

    @pl.loop(0, cycle)
    def _(c):
        first_ref[c] = (first_ref[c].astype(f32) + got_first[c].astype(f32)).astype(bf16)
        slim_ref[c] = (slim_ref[c].astype(f32) + got_slim[c].astype(f32)).astype(bf16)


def finish(grad_w, grad_we, w_cat, w_expand, extra, cycle, slab, collective):
    shapes = [(cycle, slab, 256), (cycle, slab, KVR + DN)]
    return pl.pallas_call(
        functools.partial(finish_kernel, cycle, slab),
        name="finish",
        out_shape=tuple(jax.ShapeDtypeStruct(shape, bf16) for shape in shapes),
        in_specs=[pl.BlockSpec(memory_space=pltpu.VMEM)] * 5,
        out_specs=(pl.BlockSpec(memory_space=pltpu.VMEM),) * 2,
        scratch_shapes=[pltpu.VMEM(shape, bf16) for shape in shapes * 2]
        + [pltpu.SemaphoreType.DMA((2,)), pltpu.SemaphoreType.DMA((2,))],
        compiler_params=pltpu.CompilerParams(
            collective_id=collective, has_side_effects=True, vmem_limit_bytes=60 << 20
        ),
    )(grad_w, grad_we, w_cat, w_expand, extra)


def place_lanes(out_ref, pieces, width):
    total = width * len(pieces)
    for start in range(0, total, DN):
        tile = None
        for c in range(start // width, min(len(pieces), -(-(start + DN) // width))):
            moved = pieces[c]
            shift = (c * width - start) % 256
            if shift:
                moved = pltpu.roll(moved, shift, 1)
            moved = moved[:, :DN]
            lanes = lanes_of(moved) + start
            inside = (lanes >= c * width) & (lanes < (c + 1) * width)
            tile = jnp.where(inside, moved, 0.0 if tile is None else tile)
        out_ref[:, start : start + DN] = tile


def spread_kernel(cycle, slab, pack_ref, pack_s_ref, gq_ref, gwe_ref, gg_ref, gu_ref):
    quarter = slab // 4
    for ref, out_ref, start in (
        (pack_ref, gq_ref, 0),
        (pack_s_ref, gg_ref, 0),
        (pack_s_ref, gu_ref, 256),
    ):
        pieces = [ref[c, :, start : start + 256].astype(f32) for c in range(cycle)]
        place_lanes(out_ref, pieces, out_ref.shape[1] // cycle)
    for c in range(cycle):
        tail = pack_ref[c, :, DN:256].astype(f32)
        for q in range(2):
            left = tail[2 * q * quarter : (2 * q + 1) * quarter]
            right = tail[(2 * q + 1) * quarter : (2 * q + 2) * quarter]
            both = jnp.where(lanes_of(left) < DR, pltpu.roll(left, DR, 1), right)
            at = c * 2 * DN + q * DN
            gwe_ref[:, at : at + DN] = both


def spread(packed, packed_s, widths):
    cycle, slab, _ = packed.shape
    return pl.pallas_call(
        functools.partial(spread_kernel, cycle, slab),
        name="spread",
        out_shape=(
            jax.ShapeDtypeStruct((slab, widths[0]), f32),
            jax.ShapeDtypeStruct((slab // 4, widths[1]), f32),
            jax.ShapeDtypeStruct((slab, widths[2]), f32),
            jax.ShapeDtypeStruct((slab, widths[3]), f32),
        ),
        compiler_params=pltpu.CompilerParams(vmem_limit_bytes=60 << 20),
    )(packed, packed_s)


def fixed(shape):
    return pl.BlockSpec(shape, lambda i: (0,) * len(shape), pipeline_mode=pl.Buffered(1))


def second(shape):
    return pl.BlockSpec(shape, lambda i: (0, 1), pipeline_mode=pl.Buffered(1))


def by_rows(rows, cols):
    return pl.BlockSpec((rows, cols), lambda i: (i, 0))


def project_kernel(
    scale, x_ref, gain_ref, w_ref, gain_l_ref, we_ref, cos_ref, sin_ref,
    act_ref, q_ref, k_ref, v_ref, latent_ref, raw_ref,
):
    act = norm_forward(x_ref[...].astype(f32), gain_ref[...])[0].astype(bf16)
    act_ref[...] = act
    raw = dot(act, w_ref[...])
    turned = raw[:, DN : 2 * DN] * cos_ref[...] + raw[:, 2 * DN : 3 * DN] * sin_ref[...]
    low = lax.broadcasted_iota(jnp.int32, turned.shape, 1) < DR
    q_ref[:, :DN] = (raw[:, :DN] * scale).astype(bf16)
    q_ref[:, DN:] = jnp.where(low, turned * scale, 0.0).astype(bf16)
    raw_latent = raw[:, 3 * DN :]
    raw_ref[...] = raw_latent
    latent = norm_forward(raw_latent, gain_l_ref[...])[0].astype(bf16)
    latent_ref[...] = latent
    expanded = dot(latent, we_ref[...]).astype(bf16)
    k_ref[:, :DN] = expanded[:, :DN]
    k_ref[:, DN:] = jnp.where(low, pltpu.roll(turned, DR, 1), 0.0).astype(bf16)
    v_ref[...] = expanded[:, DN:]


def project(x, gain, w_cat, gain_latent, w_expand, cosine, sine, scale):
    length = x.shape[0]
    block = min(512, length)
    width = w_cat.shape[1]
    return pl.pallas_call(
        functools.partial(project_kernel, scale),
        name="project",
        grid=(length // block,),
        out_shape=(
            jax.ShapeDtypeStruct((length, D), bf16),
            jax.ShapeDtypeStruct((length, WIDE), bf16),
            jax.ShapeDtypeStruct((length, WIDE), bf16),
            jax.ShapeDtypeStruct((length, DV), bf16),
            jax.ShapeDtypeStruct((length, KVR), bf16),
            jax.ShapeDtypeStruct((length, KVR), f32),
        ),
        in_specs=[
            by_rows(block, D),
            fixed((1, D)),
            fixed((D, width)),
            fixed((1, KVR)),
            fixed((KVR, DN + DV)),
            by_rows(block, DN),
            by_rows(block, DN),
        ],
        out_specs=(
            by_rows(block, D),
            by_rows(block, WIDE),
            by_rows(block, WIDE),
            by_rows(block, DV),
            by_rows(block, KVR),
            by_rows(block, KVR),
        ),
        compiler_params=pltpu.CompilerParams(vmem_limit_bytes=60 << 20),
        cost_estimate=pl.CostEstimate(
            flops=2 * length * D * width, bytes_accessed=length * D * 6, transcendentals=0
        ),
    )(x, gain[None, :], w_cat, gain_latent[None, :], w_expand, cosine, sine)


def project_back_kernel(
    scale, copies, dq_ref, dk_ref, dv_ref, raw_ref, latent_ref, act_ref, cos_ref, sin_ref,
    we_ref, gain_l_ref, keep_q_ref, keep_e_ref, grads_ref, gw_ref, gwe_ref,
):
    @pl.when(pl.program_id(0) == 0)
    def _():
        gw_ref[...] = jnp.zeros_like(gw_ref)
        gwe_ref[...] = jnp.zeros_like(gwe_ref)

    grad_q = dq_ref[...] * scale
    grad_k = dk_ref[:, :DN]
    grad_v = dv_ref[...]
    if copies > 1:
        grad_q = grad_q * keep_q_ref[...]
        grad_k = grad_k * keep_e_ref[:, :DN]
        grad_v = grad_v * keep_e_ref[:, DN:]
    rope_q = grad_q[:, DN:]
    low = lax.broadcasted_iota(jnp.int32, rope_q.shape, 1) < DR
    rope_k = jnp.where(low, dk_ref[:, DN:] * (1.0 / copies), 0.0)
    ropes = jnp.where(low, rope_q, pltpu.roll(rope_k, DR, 1))
    expanded = jnp.concatenate([grad_k, grad_v], axis=-1).astype(bf16)
    grad_latent = dot_last(expanded, we_ref[...])
    raw = raw_ref[...]
    factor = lax.rsqrt(jnp.mean(raw * raw, axis=-1, keepdims=True) + EPS)
    grad_latent = norm_back_rows(raw, factor, gain_l_ref[...], grad_latent)
    grads = jnp.concatenate(
        [
            grad_q[:, :DN].astype(bf16),
            (ropes * cos_ref[...]).astype(bf16),
            (ropes * sin_ref[...]).astype(bf16),
            grad_latent.astype(bf16),
        ],
        axis=-1,
    )
    grads_ref[...] = grads
    gw_ref[...] += dot_first(act_ref[...], grads)
    gwe_ref[...] += dot_first(latent_ref[...], expanded)


def project_back(
    grad_q, grad_k, grad_v, raw, latent, act, cosine, sine, w_expand, gain_latent, keep_q,
    keep_e, scale, copies,
):
    length = act.shape[0]
    block = min(512, length)
    width = 3 * DN + KVR
    return pl.pallas_call(
        functools.partial(project_back_kernel, scale, copies),
        name="project_back",
        grid=(length // block,),
        out_shape=(
            jax.ShapeDtypeStruct((length, width), bf16),
            jax.ShapeDtypeStruct((D, width), f32),
            jax.ShapeDtypeStruct((KVR, DN + DV), f32),
        ),
        in_specs=[
            by_rows(block, WIDE),
            by_rows(block, WIDE),
            by_rows(block, DV),
            by_rows(block, KVR),
            by_rows(block, KVR),
            by_rows(block, D),
            by_rows(block, DN),
            by_rows(block, DN),
            fixed((KVR, DN + DV)),
            fixed((1, KVR)),
            fixed((1, WIDE)),
            fixed((1, DN + DV)),
        ],
        out_specs=(
            by_rows(block, width),
            pl.BlockSpec((D, width), lambda i: (0, 0)),
            pl.BlockSpec((KVR, DN + DV), lambda i: (0, 0)),
        ),
        compiler_params=pltpu.CompilerParams(vmem_limit_bytes=60 << 20),
        cost_estimate=pl.CostEstimate(
            flops=4 * length * D * width, bytes_accessed=length * D * 6, transcendentals=0
        ),
    )(
        grad_q, grad_k, grad_v, raw, latent, act, cosine, sine, w_expand, gain_latent[None, :],
        keep_q, keep_e,
    )


def rows_kernel(grads_ref, w_ref, low_ref, part_ref, wide_ref):
    wide_ref[...] = low_ref[...].astype(f32)
    part_ref[...] = dot_last(grads_ref[...], w_ref[...]).astype(bf16)


def project_back_rows(grads, w_cat, low):
    length, width = grads.shape
    block = min(512, length)
    count = length // block
    tall, wide = low.shape
    piece = 176 if tall % 176 == 0 else tall
    steps = tall // piece
    some = pl.BlockSpec((piece, wide), lambda i: (i * steps // count, 0))
    return pl.pallas_call(
        rows_kernel,
        name="project_back_rows",
        grid=(length // block,),
        out_shape=(
            jax.ShapeDtypeStruct((length, D), bf16),
            jax.ShapeDtypeStruct((tall, wide), f32),
        ),
        in_specs=[by_rows(block, width), fixed((D, width)), some],
        out_specs=(by_rows(block, D), some),
        compiler_params=pltpu.CompilerParams(vmem_limit_bytes=60 << 20),
        cost_estimate=pl.CostEstimate(
            flops=2 * length * D * width, bytes_accessed=length * D * 4, transcendentals=0
        ),
    )(grads, w_cat, low)


class Gather:
    def __init__(self, parts, bits, events, x_ref, o_ref, send_sem, recv_sem, own_sem):
        self.parts, self.bits, self.events = parts, bits, events
        self.x_ref, self.o_ref = x_ref, o_ref
        self.send_sem, self.recv_sem = send_sem, recv_sem
        self.me = lax.axis_index("ctx")
        self.own = pltpu.make_async_copy(x_ref, o_ref.at[self.me], own_sem)
        self.seen = set()
        self.started = []

    def send(self, index):
        _, _, p, slot, bit = self.events[index]
        if slot:
            self.arrived(p, slot)
        _, start, size, _ = self.parts[p]
        rows = pl.ds(start, size)
        block = flip(self.me, slot)
        item = pltpu.make_async_remote_copy(
            src_ref=self.x_ref.at[rows] if slot == 0 else self.o_ref.at[block, rows],
            dst_ref=self.o_ref.at[block, rows],
            send_sem=self.send_sem.at[index],
            recv_sem=self.recv_sem.at[p, slot ^ bit],
            device_id={"ctx": flip(self.me, bit)},
            device_id_type=MESH,
        )
        item.start()
        self.started.append(item)

    def arrived(self, p, slot):
        if (p, slot) in self.seen:
            return
        self.seen.add((p, slot))
        _, start, size, order = self.parts[p]
        rows = pl.ds(start, size)
        bit = [b for b in order if slot & b][-1]
        pltpu.make_async_remote_copy(
            src_ref=self.x_ref.at[rows],
            dst_ref=self.o_ref.at[flip(self.me, slot), rows],
            send_sem=self.send_sem.at[0],
            recv_sem=self.recv_sem.at[p, slot],
            device_id={"ctx": flip(self.me, bit)},
            device_id_type=MESH,
        ).wait_recv()

    def block(self, slot):
        if slot == 0:
            return self.x_ref
        for p in range(len(self.parts)):
            self.arrived(p, slot)
        return self.o_ref.at[flip(self.me, slot)]

    def finish(self):
        for slot in range(1, 1 << self.bits):
            self.block(slot)
        for item in self.started:
            item.wait_send()
        self.own.wait()


def gather_order(parts, bits, events, span):
    at = {}
    for index, (_, _, p, slot, bit) in enumerate(events):
        at[p, slot ^ bit] = span * (index + 1) / len(events)
    whole = {0: 0.0}
    for slot in range(1, 1 << bits):
        whole[slot] = max(at[p, slot] for p in range(len(parts)))
    return whole, at


def gather_plan(parts, bits, events, span, size, pieces, cost):
    whole, at = gather_order(parts, bits, events, span)
    slots = sorted(whole, key=lambda slot: (whole[slot], slot))
    groups = [slots[i : i + size] for i in range(0, len(slots), size)]
    ready = [max(whole[slot] for slot in group) for group in groups]
    work = [(g, k) for g in range(len(groups)) for k in range(pieces)]
    plan, now, e, w = [], 0.0, 0, 0
    while e < len(events) or w < len(work):
        _, _, p, slot, _ = events[e] if e < len(events) else (0, 0, 0, 0, 0)
        when = (at[p, slot] if slot else 0.0) if e < len(events) else math.inf
        then = ready[work[w][0]] if w < len(work) else math.inf
        if when <= now or when <= then:
            plan.append(("send", e))
            now = max(now, when) + 0.1
            e += 1
        else:
            plan.append(("work", work[w]))
            now = max(now, then) + cost / pieces
            w += 1
    return groups, plan


def expert_sizes(capacity, tokens, cycle):
    unit = 1
    while unit * capacity % 16:
        unit *= 2
    blocks = max(4, unit)
    return unit, blocks


def pick_rows(me, slots, unit, capacity, row_ref):
    tokens = row_ref.shape[2]
    places = []
    for q, slot in enumerate(slots):
        place = row_ref[flip(me, slot)]
        places.append(jnp.where(place >= 0, place + q * capacity, -1))
    place = jnp.concatenate(places, axis=1)
    shape = (unit * capacity, unit * tokens)
    return lax.broadcasted_iota(jnp.int32, shape, 0) == place


def as_bf16(mask):
    return mask.astype(f32).astype(bf16)


def experts_kernel(
    groups, plan, parts, bits, events, shares, unit, capacity, x_ref, row_ref, prob_ref, *refs
):
    weights, both_ref, down_ref = refs[: 3 * shares], refs[3 * shares], refs[3 * shares + 1]
    refs = refs[3 * shares + 2 :]
    o_ref, part_out, rows_out, gs_out, us_out, hs_out = refs[:6]
    kept_out, refs = refs[6 : 6 + 3 * shares], refs[6 + 3 * shares :]
    w, wb, wd, xg, rows, part, shared, kept = refs[:8]
    send_sem, recv_sem, own_sem, w_sem, x_sem, out_sem, part_sem = refs[8:]
    me = lax.axis_index("ctx")
    tokens = x_ref.shape[0]
    size = len(groups[0])
    tall, short = unit * tokens, unit * capacity
    width = wd.shape[0]
    gather = Gather(parts, bits, events, x_ref, o_ref, send_sem, recv_sem, own_sem)
    gather.own.start()
    loads = [pltpu.make_async_copy(weights[i], w.at[i], w_sem.at[i]) for i in range(3 * shares)]
    loads.append(pltpu.make_async_copy(both_ref, wb, w_sem.at[3 * shares]))
    loads.append(pltpu.make_async_copy(down_ref, wd, w_sem.at[3 * shares + 1]))
    greet(bits)
    ready = set()

    def need(i):
        if i not in ready:
            loads[i].wait()
            ready.add(i)
        return w[i] if i < 3 * shares else (wb if i == 3 * shares else wd)

    def outs(g):
        span = pl.ds(g * size * capacity, size * capacity)
        wide = pl.ds(g * size * tokens, size * tokens)
        items = [pltpu.make_async_copy(rows, rows_out.at[span], out_sem.at[0])]
        for i, ref in enumerate((gs_out, us_out, hs_out)):
            items.append(pltpu.make_async_copy(shared.at[i], ref.at[wide], out_sem.at[1 + i]))
        for i in range(3 * shares):
            items.append(
                pltpu.make_async_copy(kept.at[i], kept_out[i].at[span], out_sem.at[4 + i])
            )
        return items

    def part_outs(g, first=0, count=size):
        return [
            pltpu.make_async_copy(
                part.at[pl.ds(q * tokens, tokens)],
                part_out.at[flip(me, groups[g][q])],
                part_sem.at[q],
            )
            for q in range(first, first + count)
        ]

    state = {}

    def begin(g):
        copies = [
            pltpu.make_async_copy(
                gather.block(slot), xg.at[pl.ds(q * tokens, tokens)], x_sem.at[q]
            )
            for q, slot in enumerate(groups[g])
        ]
        for item in copies:
            item.start()
        if g:
            for item in outs(g - 1):
                item.wait()
        picks, scales = [], []
        for j in range(size // unit):
            slots = groups[g][j * unit : (j + 1) * unit]
            mask = pick_rows(me, slots, unit, capacity, row_ref)
            prob = jnp.concatenate([prob_ref[flip(me, slot)] for slot in slots], axis=1)
            scales.append(jnp.sum(jnp.where(mask, prob, 0.0), axis=1, keepdims=True))
            picks.append(as_bf16(mask))
        for item in copies:
            item.wait()
        for j, pick in enumerate(picks):
            chosen = dot(pick, xg[j * tall : (j + 1) * tall, :]).astype(bf16)
            rows[j * short : (j + 1) * short, :] = chosen
        state.update(picks=picks, scale=jnp.concatenate(scales, axis=0), total=0.0)

    def gate(s):
        state["gate"] = dot_last(rows[...], need(3 * s))

    def up(s):
        gated, upper = state["gate"], dot_last(rows[...], need(3 * s + 1))
        hidden = (gated * jax.nn.sigmoid(gated) * upper).astype(bf16)
        for i, value in enumerate((gated, upper, hidden)):
            kept[3 * s + i] = value.astype(bf16)

    def down(s):
        state["total"] = state["total"] + dot(kept[3 * s + 2], need(3 * s + 2))

    def shared_hidden(g):
        gated = dot(xg[...], need(3 * shares)[:, :width])
        upper = dot(xg[...], need(3 * shares)[:, width:])
        hidden = (gated * jax.nn.sigmoid(gated) * upper).astype(bf16)
        for i, value in enumerate((gated, upper, hidden)):
            shared[i] = value.astype(bf16)
        state["rows"] = (state["total"] * state["scale"]).astype(bf16)
        for item in outs(g):
            item.start()
        if g:
            for item in part_outs(g - 1):
                item.wait()

    def combine(g, j):
        inside = slice(j * tall, (j + 1) * tall)
        part[inside, :] = (
            dot_first(state["picks"][j], state["rows"][j * short : (j + 1) * short, :])
            + dot(shared[2, inside, :], need(3 * shares + 1)[...])
        ).astype(bf16)
        for item in part_outs(g, j * unit, unit):
            item.start()

    def piece(g, k):
        if k == 0:
            begin(g)
        elif k <= 3 * shares:
            (gate, up, down)[(k - 1) % 3]((k - 1) // 3)
        elif k == 3 * shares + 1:
            shared_hidden(g)
        else:
            combine(g, k - 3 * shares - 2)

    sent = 0
    for kind, item in plan:
        if kind == "send":
            gather.send(item)
            sent += 1
            if sent == bits * len(parts):
                for load in loads:
                    load.start()
        else:
            piece(*item)
    gather.finish()
    for item in outs(len(groups) - 1) + part_outs(len(groups) - 1):
        item.wait()


def experts(x, place, prob, weights, shared, capacity, bits, collective):
    tokens = x.shape[0]
    cycle = 1 << bits
    unit, size = expert_sizes(capacity, tokens, cycle)
    parts = all_parts([x.shape], bits)
    events = gather_events(parts, bits)
    shares = len(weights) // 3
    half = weights[0].shape[0]
    width = shared[1].shape[0]
    pieces = 3 * shares + 2 + size // unit
    groups, plan = gather_plan(parts, bits, events, 90.0, size, pieces, 10.5)
    anywhere = pl.BlockSpec(memory_space=pl.ANY)
    inside = pl.BlockSpec(memory_space=pltpu.VMEM)
    return pl.pallas_call(
        functools.partial(
            experts_kernel, groups, plan, parts, bits, events, shares, unit, capacity
        ),
        name="experts",
        out_shape=[
            jax.ShapeDtypeStruct((cycle, tokens, D), bf16),
            jax.ShapeDtypeStruct((cycle, tokens, D), bf16),
            jax.ShapeDtypeStruct((cycle * capacity, D), bf16),
        ]
        + [jax.ShapeDtypeStruct((cycle * tokens, width), bf16)] * 3
        + [jax.ShapeDtypeStruct((cycle * capacity, half), bf16)] * (3 * shares),
        in_specs=[anywhere, inside, inside] + [anywhere] * (3 * shares + 2),
        out_specs=[anywhere] * (6 + 3 * shares),
        scratch_shapes=[
            pltpu.VMEM((3 * shares, half, D), bf16),
            pltpu.VMEM((D, 2 * width), bf16),
            pltpu.VMEM((width, D), bf16),
            pltpu.VMEM((size * tokens, D), bf16),
            pltpu.VMEM((size * capacity, D), bf16),
            pltpu.VMEM((size * tokens, D), bf16),
            pltpu.VMEM((3, size * tokens, width), bf16),
            pltpu.VMEM((3 * shares, size * capacity, half), bf16),
            pltpu.SemaphoreType.DMA((len(events),)),
            pltpu.SemaphoreType.DMA((len(parts), cycle)),
            pltpu.SemaphoreType.DMA,
            pltpu.SemaphoreType.DMA((3 * shares + 2,)),
            pltpu.SemaphoreType.DMA((size,)),
            pltpu.SemaphoreType.DMA((4 + 3 * shares,)),
            pltpu.SemaphoreType.DMA((size,)),
        ],
        compiler_params=pltpu.CompilerParams(
            collective_id=collective, has_side_effects=True, vmem_limit_bytes=60 << 20
        ),
    )(x, place, prob, *weights, *shared)


def experts_back_kernel(
    groups, plan, parts, bits, events, shares, unit, capacity, x_ref, act_ref, row_ref, prob_ref,
    gs_in, us_in, hs_in, *refs,
):
    kept_in, refs = refs[: 2 * shares], refs[2 * shares :]
    weights, both_ref, down_ref = refs[: 3 * shares], refs[3 * shares], refs[3 * shares + 1]
    refs = refs[3 * shares + 2 :]
    o_ref, part_out, dy_out = refs[:3]
    grads_out, refs = refs[3 : 3 + 2 * shares], refs[3 + 2 * shares :]
    gws_ref, gwd_ref = refs[:2]
    w, wb, wd, dg, ag, dy, part, shared, kept, grads, gwg, gwu = refs[2:14]
    send_sem, recv_sem, own_sem, w_sem, x_sem, a_sem, k_sem, out_sem, part_sem = refs[14:]
    me = lax.axis_index("ctx")
    tokens = x_ref.shape[0]
    size = len(groups[0])
    tall, short = unit * tokens, unit * capacity
    width = wd.shape[0]
    gather = Gather(parts, bits, events, x_ref, o_ref, send_sem, recv_sem, own_sem)
    gather.own.start()
    loads = [pltpu.make_async_copy(weights[i], w.at[i], w_sem.at[i]) for i in range(3 * shares)]
    loads.append(pltpu.make_async_copy(both_ref, wb, w_sem.at[3 * shares]))
    loads.append(pltpu.make_async_copy(down_ref, wd, w_sem.at[3 * shares + 1]))
    greet(bits)
    for ref in (gwg, gwu, gwd_ref):
        ref[...] = jnp.zeros_like(ref)
    ready = set()

    def need(i):
        if i not in ready:
            loads[i].wait()
            ready.add(i)
        return w[i] if i < 3 * shares else (wb if i == 3 * shares else wd)

    def old(g):
        span = pl.ds(g * size * capacity, size * capacity)
        wide = pl.ds(g * size * tokens, size * tokens)
        items = [
            pltpu.make_async_copy(
                act_ref.at[flip(me, slot)], ag.at[pl.ds(q * tokens, tokens)], a_sem.at[q]
            )
            for q, slot in enumerate(groups[g])
        ]
        for i, ref in enumerate((gs_in, us_in, hs_in)):
            items.append(pltpu.make_async_copy(ref.at[wide], shared.at[i], k_sem.at[i]))
        for i in range(2 * shares):
            items.append(pltpu.make_async_copy(kept_in[i].at[span], kept.at[i], k_sem.at[3 + i]))
        return items

    def outs(g):
        span = pl.ds(g * size * capacity, size * capacity)
        items = [pltpu.make_async_copy(dy, dy_out.at[span], out_sem.at[0])]
        for i in range(2 * shares):
            items.append(
                pltpu.make_async_copy(grads.at[i], grads_out[i].at[span], out_sem.at[1 + i])
            )
        return items

    def part_outs(g, first=0, count=size):
        return [
            pltpu.make_async_copy(
                part.at[pl.ds(q * tokens, tokens)],
                part_out.at[flip(me, groups[g][q])],
                part_sem.at[q],
            )
            for q in range(first, first + count)
        ]

    state = {}

    def begin(g):
        copies = [
            pltpu.make_async_copy(
                gather.block(slot), dg.at[pl.ds(q * tokens, tokens)], x_sem.at[q]
            )
            for q, slot in enumerate(groups[g])
        ]
        for item in copies:
            item.start()
        if g:
            for item in outs(g - 1):
                item.wait()
        picks, scales = [], []
        for j in range(size // unit):
            slots = groups[g][j * unit : (j + 1) * unit]
            mask = pick_rows(me, slots, unit, capacity, row_ref)
            prob = jnp.concatenate([prob_ref[flip(me, slot)] for slot in slots], axis=1)
            scales.append(jnp.sum(jnp.where(mask, prob, 0.0), axis=1, keepdims=True))
            picks.append(as_bf16(mask))
        for item in copies:
            item.wait()
        for j, pick in enumerate(picks):
            chosen = dot(pick, dg[j * tall : (j + 1) * tall, :]) * scales[j]
            dy[j * short : (j + 1) * short, :] = chosen.astype(bf16)
        for item in old(g):
            item.wait()
        state.update(picks=picks, total=0.0)

    def hidden_back(s):
        grad_hidden = dot_last(dy[...], need(3 * s + 2))
        grad_gate, grad_up = silu_grads(
            kept[2 * s].astype(f32), kept[2 * s + 1].astype(f32), grad_hidden
        )
        grads[2 * s] = grad_gate
        grads[2 * s + 1] = grad_up

    def rows_back(s, i):
        state["total"] = state["total"] + dot(grads[2 * s + i], need(3 * s + i))

    def shared_back(g):
        for item in outs(g):
            item.start()
        grad_hidden = dot_last(dg[...], need(3 * shares + 1)[...])
        grad_gate, grad_up = silu_grads(
            shared[0].astype(f32), shared[1].astype(f32), grad_hidden
        )
        gwg[...] += dot_first(grad_gate, ag[...])
        state.update(gate=grad_gate, up=grad_up, rows=state["total"].astype(bf16))

    def shared_more(g):
        gwu[...] += dot_first(state["up"], ag[...])
        gwd_ref[...] += dot_first(shared[2], dg[...])
        if g + 1 < len(groups):
            for item in old(g + 1):
                item.start()
        if g:
            for item in part_outs(g - 1):
                item.wait()

    def combine(g, j):
        inside = slice(j * tall, (j + 1) * tall)
        both = need(3 * shares)
        part[inside, :] = (
            dot_first(state["picks"][j], state["rows"][j * short : (j + 1) * short, :])
            + dot_last(state["gate"][inside, :], both[:, :width])
            + dot_last(state["up"][inside, :], both[:, width:])
        ).astype(bf16)
        for item in part_outs(g, j * unit, unit):
            item.start()

    def piece(g, k):
        if k == 0:
            begin(g)
        elif k <= 3 * shares:
            s, i = (k - 1) // 3, (k - 1) % 3
            hidden_back(s) if i == 0 else rows_back(s, i - 1)
        elif k == 3 * shares + 1:
            shared_back(g)
        elif k == 3 * shares + 2:
            shared_more(g)
        else:
            combine(g, k - 3 * shares - 3)

    sent = 0
    for kind, item in plan:
        if kind == "send":
            gather.send(item)
            sent += 1
            if sent == bits * len(parts):
                for load in loads + old(0):
                    load.start()
        else:
            piece(*item)
    gws_ref[:, :width] = gwg[...].T.astype(bf16)
    gws_ref[:, width:] = gwu[...].T.astype(bf16)
    gather.finish()
    for item in outs(len(groups) - 1) + part_outs(len(groups) - 1):
        item.wait()


def experts_back(x, act, place, prob, saved, kept, weights, shared, capacity, bits, collective):
    tokens = x.shape[0]
    cycle = 1 << bits
    unit, size = expert_sizes(capacity, tokens, cycle)
    parts = all_parts([x.shape], bits)
    events = gather_events(parts, bits)
    shares = len(weights) // 3
    half = weights[0].shape[0]
    width = shared[1].shape[0]
    pieces = 3 * shares + 3 + size // unit
    groups, plan = gather_plan(parts, bits, events, 150.0, size, pieces, 15.0)
    anywhere = pl.BlockSpec(memory_space=pl.ANY)
    inside = pl.BlockSpec(memory_space=pltpu.VMEM)
    return pl.pallas_call(
        functools.partial(
            experts_back_kernel, groups, plan, parts, bits, events, shares, unit, capacity
        ),
        name="experts_back",
        out_shape=[
            jax.ShapeDtypeStruct((cycle, tokens, D), bf16),
            jax.ShapeDtypeStruct((cycle, tokens, D), bf16),
            jax.ShapeDtypeStruct((cycle * capacity, D), bf16),
        ]
        + [jax.ShapeDtypeStruct((cycle * capacity, half), bf16)] * (2 * shares)
        + [jax.ShapeDtypeStruct((D, 2 * width), bf16), jax.ShapeDtypeStruct((width, D), f32)],
        in_specs=[anywhere, anywhere, inside, inside] + [anywhere] * (5 + 5 * shares),
        out_specs=[anywhere] * (3 + 2 * shares) + [inside, inside],
        scratch_shapes=[
            pltpu.VMEM((3 * shares, half, D), bf16),
            pltpu.VMEM((D, 2 * width), bf16),
            pltpu.VMEM((width, D), bf16),
            pltpu.VMEM((size * tokens, D), bf16),
            pltpu.VMEM((size * tokens, D), bf16),
            pltpu.VMEM((size * capacity, D), bf16),
            pltpu.VMEM((size * tokens, D), bf16),
            pltpu.VMEM((3, size * tokens, width), bf16),
            pltpu.VMEM((2 * shares, size * capacity, half), bf16),
            pltpu.VMEM((2 * shares, size * capacity, half), bf16),
            pltpu.VMEM((width, D), f32),
            pltpu.VMEM((width, D), f32),
            pltpu.SemaphoreType.DMA((len(events),)),
            pltpu.SemaphoreType.DMA((len(parts), cycle)),
            pltpu.SemaphoreType.DMA,
            pltpu.SemaphoreType.DMA((3 * shares + 2,)),
            pltpu.SemaphoreType.DMA((size,)),
            pltpu.SemaphoreType.DMA((size,)),
            pltpu.SemaphoreType.DMA((3 + 2 * shares,)),
            pltpu.SemaphoreType.DMA((1 + 2 * shares,)),
            pltpu.SemaphoreType.DMA((size,)),
        ],
        compiler_params=pltpu.CompilerParams(
            collective_id=collective, has_side_effects=True, vmem_limit_bytes=61 << 20
        ),
    )(x, act, place, prob, *saved, *kept, *weights, *shared)


def shift_fsdp(x, groups, by):
    return lax.ppermute(x, "fsdp", [(i, (i + by) % groups) for i in range(groups)])


def gather_fsdp(x, groups):
    if groups != 2:
        return lax.all_gather(x, "fsdp", axis=0)
    other = shift_fsdp(x, groups, 1)
    mine_first = lax.axis_index("fsdp") == 0
    return jnp.stack([jnp.where(mine_first, x, other), jnp.where(mine_first, other, x)])


def scatter_fsdp(x, groups):
    if groups != 2:
        return lax.psum_scatter(x.astype(bf16), "fsdp", scatter_dimension=0).astype(f32)
    me = lax.axis_index("fsdp")
    away = lax.dynamic_index_in_dim(x, 1 - me, 0, keepdims=False).astype(bf16)
    mine = lax.dynamic_index_in_dim(x, me, 0, keepdims=False).astype(f32)
    return mine + shift_fsdp(away, groups, 1).astype(f32)


def shards(
    hidden_in,
    teacher,
    doc_starts,
    routes,
    gate_logits,
    input_gain,
    query_weight,
    latent_weight,
    latent_gain,
    expand_weight,
    output_weight,
    mixer_gain,
    shared_gate,
    shared_up,
    shared_down,
    expert_gate,
    expert_up,
    expert_down,
):
    cycle = lax.axis_size("ctx")
    groups = lax.axis_size("fsdp")
    bits = cycle.bit_length() - 1
    tokens = hidden_in.shape[1]
    length = tokens * cycle
    capacity = min(tokens, 3 * tokens * TOPK // (2 * cycle))
    scale = (DN + DR) ** (-0.5)
    copies = max(1, cycle // H)
    ctx_index = lax.axis_index("ctx")
    copy_index = ctx_index % copies
    slab = query_weight.shape[0]
    slab_latent = expand_weight.shape[0]

    def pieces(weight):
        rows, width = weight.shape
        return jnp.transpose(weight.reshape(rows, cycle, width // cycle), (1, 0, 2))

    def padded(item, width):
        return jnp.pad(item, ((0, 0), (0, 0), (0, width - item.shape[2])))

    def exchange(packed):
        return lax.all_to_all(packed, "ctx", split_axis=0, concat_axis=0, tiled=True)

    def same_head(part, axis):
        if copies == 1:
            return part
        teams = [[i * copies + j for j in range(copies)] for i in range(H)]
        return lax.all_gather(part, "ctx", axis=axis, tiled=True, axis_index_groups=teams)

    def own_part(full, axis=1):
        if copies == 1:
            return full
        width = full.shape[axis] // copies
        return lax.dynamic_slice_in_dim(full, copy_index * width, width, axis)

    def swap(pair):
        half = pair.shape[1] // 2
        return jnp.concatenate([-pair[:, half:], pair[:, :half]], axis=1)

    def all_rows(item):
        both = jnp.transpose(gather_fsdp(item, groups), (1, 0, 2, 3))
        return both.reshape(-1, item.shape[2])

    fast = copies == 1 and groups == 2 and cycle * groups * slab == D and slab == 64
    part_q, part_e = H * (DN + DR) // cycle, H * (DN + DV) // cycle
    part_s = shared_gate.shape[1] // cycle
    shared_width = -(-part_s // 128) * 128

    probs = jax.nn.softmax(gate_logits[0], axis=-1)
    chosen = routes[0][:, :, None] == jnp.arange(cycle, dtype=jnp.int32)[None, None, :]
    dense_probs = jnp.sum(jnp.where(chosen, probs[:, :, None], 0.0), axis=1).T
    high = lax.reduce_precision(dense_probs, 8, 7)
    dense_probs = jnp.concatenate([high, dense_probs - high], axis=1).astype(bf16)
    prob_width = 2 * tokens // slab
    dense_probs = dense_probs.reshape(cycle, slab, prob_width)
    expand_pieces = pieces(expand_weight)
    if fast:
        quarter = part_e // 4
        expand_pieces = jnp.concatenate(
            [expand_pieces[:, :, q * quarter : (q + 1) * quarter] for q in range(4)], axis=1
        )
    else:
        expand_pieces = expand_pieces.reshape(cycle, slab, -1)
    block_q = -(-(part_q + expand_pieces.shape[2]) // 128) * 128
    block_s = -(-(part_s + prob_width) // 128) * 128
    packed = padded(jnp.concatenate([pieces(query_weight), expand_pieces], axis=2), block_q)
    packed = exchange(packed)
    packed_s = jnp.concatenate(
        [
            padded(jnp.concatenate([pieces(shared_gate), dense_probs], axis=2), block_s),
            padded(pieces(shared_up), block_s),
        ],
        axis=2,
    )
    narrow = jnp.concatenate(
        [
            latent_weight,
            input_gain[:, None],
            mixer_gain[:, None],
            jnp.concatenate([latent_gain, jnp.zeros((slab - slab_latent,), bf16)])[:, None],
            jnp.zeros((slab, -(KVR + DR + 3) % 128), bf16),
        ],
        axis=1,
    )
    w_down_s = gather_fsdp(shared_down, groups).reshape(-1, D)
    w_down_s = jnp.pad(w_down_s, ((0, shared_width - w_down_s.shape[0]), (0, 0)))
    w_output = gather_fsdp(output_weight, groups).reshape(-1, D)
    if copies > 1:
        rows_o = w_output.shape[0]
        own_output = lax.dynamic_update_slice_in_dim(
            jnp.zeros((DV, D), bf16), w_output, copy_index * rows_o, 0
        )
        w_output = same_head(w_output, 0)
    else:
        own_output = w_output
    weights = [expert_gate[0].T, expert_up[0].T, expert_down[0]]
    for r in range(1, groups):
        weights += [shift_fsdp(item, groups, r) for item in weights[:3]]
    starts = doc_starts[0]
    positions = jnp.arange(length, dtype=jnp.int32)
    inside = starts[None, :] <= positions[:, None]
    first_pos = jnp.max(jnp.where(inside, starts[None, :], 0), axis=1)
    cosine, sine = rope_tables(positions - first_pos)
    first_col = first_pos[:, None]

    own_hidden, cosine, sine, first_col = lax.optimization_barrier(
        (hidden_in[0], cosine, sine, first_col)
    )
    all_hidden, narrow = gather_ctx([own_hidden, narrow], bits, 1)
    packed_s, _ = lax.optimization_barrier((packed_s, all_hidden))
    packed_s = exchange(packed_s)
    my_probs = packed_s[:, :, part_s : part_s + prob_width]
    my_probs = my_probs.reshape(cycle, 2, tokens).astype(f32)
    my_probs = my_probs[:, 0] + my_probs[:, 1]
    if fast:
        w_cat, w_expand, gains = assemble(
            packed, shift_fsdp(packed, groups, 1), narrow, shift_fsdp(narrow, groups, 1)
        )
        gain_one, gain_two = gains[0], gains[1]
        gain_latent = gains[2].reshape(-1, slab)[:, :slab_latent].reshape(-1)
    else:
        narrow, packed = all_rows(narrow), all_rows(packed)
        gain_one = narrow[:, KVR + DR].astype(f32)
        gain_two = narrow[:, KVR + DR + 1].astype(f32)
        gain_latent = narrow[:, KVR + DR + 2].reshape(-1, slab)[:, :slab_latent]
        gain_latent = gain_latent.reshape(-1).astype(f32)
        w_query = same_head(packed[:, :part_q], 1)
        w_expand = packed[:, part_q : part_q + expand_pieces.shape[2]].reshape(KVR, part_e)
        w_expand = same_head(w_expand, 1)
        rope_k = narrow[:, KVR : KVR + DR]
        w_cat = jnp.concatenate(
            [w_query, rope_k, swap(w_query[:, DN:]), swap(rope_k), narrow[:, :KVR]], axis=1
        )

    w_both_s = all_rows(packed_s)

    residual = hidden_in[0].astype(f32)
    act_one, queries, keys, values, latent, latent_raw = project(
        all_hidden.reshape(length, D), gain_one, w_cat, gain_latent, w_expand, cosine, sine, scale
    )
    attended, log_total, partial = attend(
        queries, keys, values, first_col, own_output
    )
    (mixing,) = scatter_ctx([partial.reshape(cycle, tokens, D)], bits, 3)
    mixed = residual + mixing

    normed_two, factor_two = norm_forward(mixed, gain_two)
    used = my_probs > 0.0
    place = jnp.cumsum(used.astype(jnp.int32), axis=1) - 1
    routing = (jnp.where(used, place, -1)[:, None, :], my_probs[:, None, :])
    shared = [w_both_s, w_down_s]
    all_act, partial, rows, gate_s, up_s, hidden_s, *kept = experts(
        normed_two.astype(bf16), *routing, weights, shared, capacity, bits, 2
    )
    (routed,) = scatter_ctx([partial], bits, 3)
    result = mixed + routed
    diff = result - teacher[0].astype(f32)
    share = jnp.sum(gather_fsdp(0.5 * jnp.sum(diff * diff, keepdims=True), groups))

    gates = [item for s in range(groups) for item in kept[3 * s : 3 * s + 2]]
    _, partial, grad_rows, *grads, grad_shared, grad_w_down = experts_back(
        diff.astype(bf16),
        all_act,
        *routing,
        [gate_s, up_s, hidden_s],
        gates,
        weights,
        shared,
        capacity,
        bits,
        6,
    )
    (grad_act_two,) = scatter_ctx([partial], bits, 3)
    grad_w_down = scatter_fsdp(grad_w_down[:part_s].reshape(groups, -1, D), groups)

    grad_gain_two = jnp.sum(grad_act_two * mixed * factor_two, axis=0)
    grad_mixed = diff + norm_back_rows(mixed, factor_two, gain_two, grad_act_two)
    def by_owner(grad):
        cut = jnp.transpose(grad.reshape(cycle, groups, slab, -1), (1, 0, 2, 3))
        return scatter_fsdp(cut, groups).astype(bf16)

    grad_shared = by_owner(grad_shared)
    high = lax.reduce_precision(share, 8, 7)
    mid = lax.reduce_precision(share - high, 8, 7)
    loss_parts = jnp.stack([high, mid, share - high - mid]).astype(bf16)
    spot = jnp.arange(grad_shared.shape[2], dtype=jnp.int32) - part_s
    loss_row = sum(jnp.where(spot == i, loss_parts[i], bf16(0)) for i in range(3))
    grad_shared = jnp.where(((spot >= 0) & (spot < 3))[None, None, :], loss_row, grad_shared)
    lefts = []
    for r in range(groups):
        lefts += [grads[2 * r], grads[2 * r + 1], kept[3 * r + 2]]
    all_mixed, *expert_grads = gather_multiply(
        grad_mixed.astype(bf16), rows, grad_rows, lefts, bits, 5
    )
    grad_shared, all_mixed = lax.optimization_barrier((grad_shared, all_mixed))
    packed_s = exchange(grad_shared)
    loss_parts = packed_s[:, 0, part_s : part_s + 3].astype(f32)
    loss_value = jnp.sum(loss_parts) / (length * groups * D)
    grad_query, grad_keys, grad_values, grad_w_output, *wide_grads = attend_back(
        queries,
        keys,
        values,
        all_mixed.reshape(length, D),
        attended,
        w_output,
        first_pos[None, :],
        log_total,
        expert_grads[:2],
    )
    grad_query, packed_s = lax.optimization_barrier((grad_query, packed_s))
    grad_w_output = own_part(grad_w_output, 0).reshape(groups, slab, D)
    grad_w_output = scatter_fsdp(grad_w_output, groups)
    lanes = jnp.arange(WIDE, dtype=jnp.int32)
    keep_q = (lanes // ((DN + DR) // copies) == copy_index).astype(f32)[None, :]
    keep_e = (lanes // ((DN + DV) // copies) == copy_index).astype(f32)[None, :]
    grads_cat, grad_w_cat, grad_w_expand = project_back(
        grad_query,
        grad_keys,
        grad_values,
        latent_raw,
        latent,
        act_one,
        cosine,
        sine,
        w_expand,
        gain_latent,
        keep_q,
        keep_e,
        scale,
        copies,
    )
    if fast:
        first, slim = finish(
            grad_w_cat, grad_w_expand, w_cat, w_expand, grad_gain_two[:, None], cycle, slab, 7
        )
    else:
        grad_gain_one = jnp.sum(grad_w_cat * w_cat.astype(f32), axis=1)
        grad_gain_latent = jnp.sum(grad_w_expand * w_expand.astype(f32), axis=1)
        turned = grad_w_cat[:, 2 * DN : 3 * DN]
        grad_ropes = grad_w_cat[:, DN : 2 * DN] - jnp.concatenate(
            [swap(turned[:, :DR]), swap(turned[:, DR:])], axis=1
        )
        grad_w_query = jnp.concatenate([grad_w_cat[:, :DN], grad_ropes[:, :DR]], axis=1)
        grad_we = own_part(grad_w_expand).reshape(cycle * groups, slab_latent, part_e)
        first = jnp.concatenate(
            [own_part(grad_w_query), grad_we.reshape(D, -1)], axis=1
        ).astype(bf16)
        spare = jnp.zeros((cycle * groups, slab - slab_latent), f32)
        grad_gain_latent = jnp.concatenate(
            [grad_gain_latent.reshape(cycle * groups, slab_latent), spare], axis=1
        ).reshape(-1)
        slim = jnp.concatenate(
            [
                grad_w_cat[:, 3 * DN :],
                grad_ropes[:, DR:],
                grad_gain_one[:, None],
                grad_gain_two[:, None],
                grad_gain_latent[:, None],
                jnp.zeros((D, -(KVR + DR + 3) % 128), f32),
            ],
            axis=1,
        ).astype(bf16)
        slim, first = by_owner(slim), padded(by_owner(first), block_q)
    packed = exchange(first)
    partial, last_grad = project_back_rows(grads_cat, w_cat, expert_grads[2])
    partial, packed = lax.optimization_barrier((partial, packed))
    grad_act_one, grad_narrow = scatter_ctx(
        [partial.reshape(cycle, tokens, D), slim], bits, 4
    )
    if fast:
        own_grads = spread(
            packed,
            packed_s,
            [w.shape[1] for w in (query_weight, expand_weight, shared_gate, shared_up)],
        )
    else:
        spots = (
            (packed, 0, part_q, query_weight),
            (packed, part_q, expand_pieces.shape[2], expand_weight),
            (packed_s, 0, part_s, shared_gate),
            (packed_s, shared_width, part_s, shared_up),
        )
        own_grads = []
        for item, start, width, like in spots:
            item = item[:, :, start : start + width].reshape(cycle, like.shape[0], -1)
            own_grads.append(jnp.transpose(item, (1, 0, 2)).reshape(like.shape).astype(f32))
    _, factor_one = norm_forward(residual, gain_one)
    grad_input = grad_mixed + norm_back_rows(residual, factor_one, gain_one, grad_act_one)
    return (
        result.astype(bf16)[None],
        loss_value,
        grad_input[None],
        grad_narrow[:, KVR + DR] / input_gain.astype(f32),
        own_grads[0],
        grad_narrow[:, : KVR + DR],
        grad_narrow[:slab_latent, KVR + DR + 2] / latent_gain.astype(f32),
        own_grads[1],
        grad_w_output,
        grad_narrow[:, KVR + DR + 1],
        own_grads[2],
        own_grads[3],
        grad_w_down,
        wide_grads[0].T[None],
        wide_grads[1].T[None],
        last_grad[None],
    )


def solution(mesh):
    tokens = P("fsdp", "ctx", None)
    rows = P(("ctx", "fsdp"), None)
    gain = P(("ctx", "fsdp"))
    wide = P("ctx", None, "fsdp")
    deep = P("ctx", "fsdp", None)
    in_specs = (
        tokens,
        tokens,
        P("fsdp", None),
        tokens,
        tokens,
        gain,
        rows,
        rows,
        gain,
        rows,
        rows,
        gain,
        rows,
        rows,
        rows,
        wide,
        wide,
        deep,
    )
    out_specs = (
        tokens,
        P(),
        tokens,
        gain,
        rows,
        rows,
        gain,
        rows,
        rows,
        gain,
        rows,
        rows,
        rows,
        wide,
        wide,
        deep,
    )
    return jax.shard_map(shards, mesh=mesh, in_specs=in_specs, out_specs=out_specs, check_vma=False)
```
